128 devices in a mesh: dp: 32 (over x, y, z_hi), mp: 4 (over z_lo, core).
Axes of the slice: x: 4, y: 4, z: 4 (z_hi: 2, z_lo: 2; z = z_hi * 2 + z_lo), core: 2. Of those that a mesh axis runs over, the one named last changes fastest.
Arguments:
- inputs: bfloat16 [16384, 1536], P(('dp', 'mp')), may hold values from -6 to 6
- cotangent: bfloat16 [16384, 1536], P(('dp', 'mp')), may hold values from -6 to 6
- seq_lengths: int32 [32], replicated, may hold values from 1 to 1024, 16384 in all
- gains: float32 [2, 1536], replicated, may hold values from 0.5 to 1.5
- gains_first: float32 [2, 1536], replicated, may hold values from -96 to 96
- gains_second: float32 [2, 1536], replicated, may hold values from 1228.8 to 4915.2
- conv_weight: float32 [3, 1536], P(None, 'mp'), may hold values from -3.5 to 3.5
- conv_first: float32 [3, 1536], P(None, 'mp'), may hold values from -80 to 80
- conv_second: float32 [3, 1536], P(None, 'mp'), may hold values from 819.2 to 3276.8
- in_weight: float32 [3, 1536, 1536], P(None, 'dp', 'mp'), may hold values from -0.15625 to 0.15625
- in_first: float32 [3, 1536, 1536], P(None, 'dp', 'mp'), may hold values from -80 to 80
- in_second: float32 [3, 1536, 1536], P(None, 'dp', 'mp'), may hold values from 819.2 to 3276.8
- out_weight: float32 [1536, 1536], P('mp', 'dp'), may hold values from -0.15625 to 0.15625
- out_first: float32 [1536, 1536], P('mp', 'dp'), may hold values from -80 to 80
- out_second: float32 [1536, 1536], P('mp', 'dp'), may hold values from 819.2 to 3276.8
- gate_up: float32 [2, 1536, 6912], P(None, 'dp', 'mp'), may hold values from -0.15625 to 0.15625
- gate_up_first: float32 [2, 1536, 6912], P(None, 'dp', 'mp'), may hold values from -28 to 28
- gate_up_second: float32 [2, 1536, 6912], P(None, 'dp', 'mp'), may hold values from 81.92 to 327.68
- down_weight: float32 [6912, 1536], P('mp', 'dp'), may hold values from -0.078125 to 0.078125
- down_first: float32 [6912, 1536], P('mp', 'dp'), may hold values from -40 to 40
- down_second: float32 [6912, 1536], P('mp', 'dp'), may hold values from 204.8 to 819.2
Outputs:
- block_out: bfloat16 [16384, 1536], P(('dp', 'mp'))
- input_grad: float32 [16384, 1536], P(('dp', 'mp'))
- gains_first_new: float32 [2, 1536], replicated
- gains_second_new: float32 [2, 1536], replicated
- gains_new: float32 [2, 1536], replicated
- conv_first_new: float32 [3, 1536], P(None, 'mp')
- conv_second_new: float32 [3, 1536], P(None, 'mp')
- conv_new: float32 [3, 1536], P(None, 'mp')
- in_first_new: float32 [3, 1536, 1536], P(None, 'dp', 'mp')
- in_second_new: float32 [3, 1536, 1536], P(None, 'dp', 'mp')
- in_new: float32 [3, 1536, 1536], P(None, 'dp', 'mp')
- out_first_new: float32 [1536, 1536], P('mp', 'dp')
- out_second_new: float32 [1536, 1536], P('mp', 'dp')
- out_new: float32 [1536, 1536], P('mp', 'dp')
- gate_up_first_new: float32 [2, 1536, 6912], P(None, 'dp', 'mp')
- gate_up_second_new: float32 [2, 1536, 6912], P(None, 'dp', 'mp')
- gate_up_new: float32 [2, 1536, 6912], P(None, 'dp', 'mp')
- down_first_new: float32 [6912, 1536], P('mp', 'dp')
- down_second_new: float32 [6912, 1536], P('mp', 'dp')
- down_new: float32 [6912, 1536], P('mp', 'dp')
The draws below stay inside these ranges and needn't reach their ends.
Inputs may be any that keep to these rules, and one draw needn't show every extreme that they name: `seq_lengths`: sequences lie end to end over all rows in order; the lengths sum to 16384 and the longest is exactly 1024.
All inputs are finite; a program needn't handle non-finite values.
Results may differ from the reference program's by a relative error of at most 0.04.
Values may be sent and summed in bfloat16 or wider, within the bound.
No kernel may reach another device: no remote copies, remote signals or barrier semaphores. Data moves between devices by JAX's collectives and lax.ppermute only.
A program may use at most 192 MiB of HBM per device.

```python
import math
import jax
import jax.numpy as jnp
import numpy as np
from jax import lax

D = 1536
FF = 6912
KW = 3
MAXLEN = 1024
STEP = 5
GROUP = 512
TOKENS = 16384
SEQS = 32
N_DP = 32


def block_scale(own_key, dims, shards, smallest, top_value):
    level, own = 1.0, jax.random.fold_in(own_key, 6)
    for position, blocks in shards:
        heights = jnp.exp(jax.random.uniform(jax.random.fold_in(own, position), (blocks,), jnp.float32, smallest / len(shards), top_value / len(shards)))
        level = level * jnp.repeat(heights, dims[position] // blocks).reshape([-1 if axis == position else 1 for axis in range(len(dims))])
    return level


def length_profile(number_of, total, bound, slope):
    weights = [(1 << 20) // math.isqrt(rank ** slope) + 1 for rank in range(2, number_of + 1)]
    surplus, counts = total - bound - (number_of - 1), [1] * (number_of - 1)
    while surplus > 0:
        free = [i for i in range(number_of - 1) if counts[i] < bound]
        mass, remaining = sum([weights[i] for i in free]), surplus
        for i in free:
            more = min(bound - counts[i], max(1, remaining * weights[i] // mass), surplus)
            counts[i] = counts[i] + more
            surplus = surplus - more
    return np.array([bound] + counts)


def ragged(stream_key, number_of, total, bound, slope):
    if number_of == 2:
        one = jax.random.randint(stream_key, (), max(1, total - bound), min(bound, total - 1) + 1)
        return jnp.stack([one, total - one])
    lengths = jnp.asarray(length_profile(number_of, total, bound, slope), jnp.int32)
    pairs = (number_of - 1) // 2
    donor, taker = lengths[1:1 + 2 * pairs:2], lengths[2:2 + 2 * pairs:2]
    room = jnp.minimum(donor - 1, bound - taker)
    passed = jax.random.randint(jax.random.fold_in(stream_key, 1), (pairs,), 0, 1 << 20) % (room + 1)
    lengths = lengths.at[1:1 + 2 * pairs:2].set(donor - passed).at[2:2 + 2 * pairs:2].set(taker + passed)
    return lengths[jax.random.permutation(jax.random.fold_in(stream_key, 2), number_of)]


def noise(stream_key, shape, scale, most, pieces=(), held_as=jnp.bfloat16):
    array = scale * jax.random.normal(stream_key, shape, jnp.float32)
    if pieces:
        array = array * block_scale(stream_key, shape, pieces, -0.22, 0.18)
    return jnp.clip(array, -most, most).astype(held_as)


def setup_inputs(seed: int = 0) -> dict:
    streams_of = jax.random.split(jax.random.key(seed), 22)
    inputs = noise(streams_of[0], (TOKENS, D), 1.0, 6.0, ((0, 128),))
    cotangent = noise(streams_of[1], (TOKENS, D), 1.0, 6.0, ((0, 128),))
    seq_lengths = ragged(streams_of[2], SEQS, TOKENS, MAXLEN, 1).astype(jnp.int32)
    gains = jnp.clip(1.0 + 0.1 * jax.random.normal(streams_of[3], (2, D), jnp.float32), 0.5, 1.5)
    gains_first = noise(streams_of[4], (2, D), (0.13 * TOKENS ** 0.5), 96.0, (), jnp.float32)
    gains_second = jnp.clip(jnp.exp(jax.random.uniform(streams_of[5], (2, D), jnp.float32, math.log(1228.8), math.log(4915.2))), 1228.8, 4915.2)
    conv_weight = noise(streams_of[6], (KW, D), 0.6, 3.5, ((1, 4),), jnp.float32)
    conv_first = noise(streams_of[7], (KW, D), (0.11 * TOKENS ** 0.5), 80.0, ((1, 4),), jnp.float32)
    conv_second = jnp.clip(jnp.exp(math.log(3276.8) - 1.3862944 * jax.random.uniform(streams_of[8], (KW, D), jnp.float32) ** block_scale(streams_of[8], (KW, D), ((1, 4),), -0.2, 0.2)), 819.2, 3276.8)
    in_weight = noise(streams_of[9], (3, D, D), D ** -0.5, 0.15625, ((1, 32), (2, 4)), jnp.float32)
    in_first = noise(streams_of[10], (3, D, D), (0.11 * TOKENS ** 0.5), 80.0, ((1, 32), (2, 4)), jnp.float32)
    in_second = jnp.clip(jnp.exp(math.log(3276.8) - 1.3862944 * jax.random.uniform(streams_of[11], (3, D, D), jnp.float32) ** block_scale(streams_of[11], (3, D, D), ((1, 32), (2, 4)), -0.2, 0.2)), 819.2, 3276.8)
    out_weight = noise(streams_of[12], (D, D), D ** -0.5, 0.15625, ((0, 4), (1, 32)), jnp.float32)
    out_first = noise(streams_of[13], (D, D), (0.11 * TOKENS ** 0.5), 80.0, ((0, 4), (1, 32)), jnp.float32)
    out_second = jnp.clip(jnp.exp(math.log(3276.8) - 1.3862944 * jax.random.uniform(streams_of[14], (D, D), jnp.float32) ** block_scale(streams_of[14], (D, D), ((0, 4), (1, 32)), -0.2, 0.2)), 819.2, 3276.8)
    gate_up = noise(streams_of[15], (2, D, FF), D ** -0.5, 0.15625, ((1, 32), (2, 4)), jnp.float32)
    gate_up_first = noise(streams_of[16], (2, D, FF), (0.035 * TOKENS ** 0.5), 28.0, ((1, 32), (2, 4)), jnp.float32)
    gate_up_second = jnp.clip(jnp.exp(math.log(327.68) - 1.3862944 * jax.random.uniform(streams_of[17], (2, D, FF), jnp.float32) ** block_scale(streams_of[17], (2, D, FF), ((1, 32), (2, 4)), -0.2, 0.2)), 81.92, 327.68)
    down_weight = noise(streams_of[18], (FF, D), FF ** -0.5, 0.078125, ((0, 4), (1, 32)), jnp.float32)
    down_first = noise(streams_of[19], (FF, D), (0.055 * TOKENS ** 0.5), 40.0, ((0, 4), (1, 32)), jnp.float32)
    down_second = jnp.clip(jnp.exp(math.log(819.2) - 1.3862944 * jax.random.uniform(streams_of[20], (FF, D), jnp.float32) ** block_scale(streams_of[20], (FF, D), ((0, 4), (1, 32)), -0.2, 0.2)), 204.8, 819.2)
    return {"inputs": inputs, "cotangent": cotangent, "seq_lengths": seq_lengths, "gains": gains, "gains_first": gains_first, "gains_second": gains_second, "conv_weight": conv_weight, "conv_first": conv_first, "conv_second": conv_second, "in_weight": in_weight, "in_first": in_first, "in_second": in_second, "out_weight": out_weight, "out_first": out_first, "out_second": out_second, "gate_up": gate_up, "gate_up_first": gate_up_first, "gate_up_second": gate_up_second, "down_weight": down_weight, "down_first": down_first, "down_second": down_second}


norm_eps = 1e-05
beta_one = 0.9
beta_two = 0.95
adam_eps = 1e-08
weight_decay = 0.1

@jax.custom_vjp
def low(v):
    return lax.optimization_barrier(v.astype(jnp.bfloat16)).astype(jnp.float32)

@jax.custom_vjp
def low_back(v):
    return v

def low_keep(v):
    return (low(v), None)

def low_pass(kept, grad):
    return (grad,)

def back_keep(v):
    return (v, None)

def back_low(kept, grad):
    return (low(grad),)
low.defvjp(low_keep, low_pass)
low_back.defvjp(back_keep, back_low)

def matmul(left, right):
    return jnp.dot(left, right, precision=lax.Precision.HIGHEST, preferred_element_type=jnp.float32)

def normalize(values):
    return values * lax.rsqrt(lax.optimization_barrier(jnp.mean(values * values, axis=-1, keepdims=True)) + norm_eps)

def positions(seq_lengths, first_row, count):
    ends = jnp.cumsum(seq_lengths).astype(jnp.int32)
    starts = (ends - seq_lengths).astype(jnp.int32)
    rows = first_row + jnp.arange(count, dtype=jnp.int32)
    covered = starts[None, :] <= rows[:, None]
    return (rows - lax.optimization_barrier(jnp.max(jnp.where(covered, starts[None, :], 0), axis=1))).astype(jnp.int32)

def forward(resid, gains, in_weight, conv_weight, out_weight, gate_up, down_weight, place):
    w_in = low(in_weight)
    w_out = low(out_weight)
    w_gate_up = low(gate_up)
    w_down = low(down_weight)
    blocks = resid.reshape(N_DP, GROUP, D)

    def mixer_in(rows_block):
        normed = low(normalize(rows_block) * gains[0])
        projected = low_back(jnp.einsum('td,kdc->ktc', normed, w_in, precision=lax.Precision.HIGHEST))
        return (projected[0] * projected[2], projected[1])
    gated, readout = lax.map(jax.checkpoint(mixer_in), blocks)
    gated = gated.reshape(TOKENS, D)
    readout = readout.reshape(TOKENS, D)
    zero_row = jnp.zeros((1, D), gated.dtype)
    one_mask = (place >= 1).astype(gated.dtype)[:, None]
    two_mask = (place >= 2).astype(gated.dtype)[:, None]
    one_back = jnp.concatenate([zero_row, gated[:-1]], 0) * one_mask
    two_back = jnp.concatenate([zero_row, zero_row, gated[:-2]], 0) * two_mask
    convolved = conv_weight[0] * gated + conv_weight[1] * one_back + conv_weight[2] * two_back
    mixed = readout * convolved

    def remainder(pair):
        rows_block, mixed_block = pair
        branch = low_back(matmul(low(mixed_block), w_out))
        middle = rows_block + branch
        normed = low(normalize(middle) * gains[1])
        gate_vals = low_back(jnp.einsum('td,kdf->ktf', normed, w_gate_up, precision=lax.Precision.HIGHEST))
        hidden = jax.nn.silu(gate_vals[0]) * gate_vals[1]
        return middle + low_back(matmul(low(hidden), w_down))
    result = lax.map(jax.checkpoint(remainder), (blocks, mixed.reshape(N_DP, GROUP, D)))
    return result.reshape(TOKENS, D)

def adam(weight, first, second, grad, rate, decay):
    first_new = beta_one * first + (1 - beta_one) * grad
    second_new = beta_two * second + (1 - beta_two) * grad * grad
    first_hat = first_new / (1 - beta_one ** STEP)
    second_hat = second_new / (1 - beta_two ** STEP)
    return (first_new, second_new, weight - rate * (first_hat / (jnp.sqrt(second_hat) + adam_eps) + decay * weight))

def reference(inputs, cotangent, seq_lengths, gains, gains_first, gains_second, conv_weight, conv_first, conv_second, in_weight, in_first, in_second, out_weight, out_first, out_second, gate_up, gate_up_first, gate_up_second, down_weight, down_first, down_second):
    place = positions(seq_lengths, 0, TOKENS)
    resid = inputs.astype(jnp.float32)

    def wrapped(resid_in, gains_in, in_in, conv_in, out_in, gate_in, down_in):
        return forward(resid_in, gains_in, in_in, conv_in, out_in, gate_in, down_in, place)
    output, pullback = jax.vjp(wrapped, resid, gains, in_weight, conv_weight, out_weight, gate_up, down_weight)
    grad_x, grad_gains, grad_in, grad_conv, grad_out, grad_gate_up, grad_down = pullback(cotangent.astype(jnp.float32))
    gains_set = adam(gains, gains_first, gains_second, grad_gains, 1.0, 0.0)
    conv_set = adam(conv_weight, conv_first, conv_second, grad_conv, 1.0, 0.0)
    in_set = adam(in_weight, in_first, in_second, grad_in, 2.0 * D ** (-0.5), weight_decay)
    out_set = adam(out_weight, out_first, out_second, grad_out, 2.0 * D ** (-0.5), weight_decay)
    gate_set = adam(gate_up, gate_up_first, gate_up_second, grad_gate_up, 2.0 * D ** (-0.5), weight_decay)
    down_set = adam(down_weight, down_first, down_second, grad_down, 2.0 * FF ** (-0.5), weight_decay)
    return (output.astype(jnp.bfloat16), grad_x, gains_set[0], gains_set[1], gains_set[2], conv_set[0], conv_set[1], conv_set[2], in_set[0], in_set[1], in_set[2], out_set[0], out_set[1], out_set[2], gate_set[0], gate_set[1], gate_set[2], down_set[0], down_set[1], down_set[2])
```

```python
import jax
import jax.numpy as jnp
from jax import lax
from jax.sharding import Mesh
from jax.sharding import PartitionSpec as P

D = 1536
FF = 6912
STEP = 5

norm_eps = 1e-05
beta_one = 0.9
beta_two = 0.95
adam_eps = 1e-08
weight_decay = 0.1

bf16 = jnp.bfloat16
f32 = jnp.float32

XY = ("x", "y")
DP = ("x", "y", "zh")
MP = ("zl", "core")
RING = ("zh", "zl")
COL = ("zh", "zl", "core")


def positions(seq_lengths, first_row, count):
    ends = jnp.cumsum(seq_lengths)
    starts = ends - seq_lengths
    rows = first_row + jnp.arange(count, dtype=jnp.int32)
    covered = starts[None, :] <= rows[:, None]
    return rows - jnp.max(jnp.where(covered, starts[None, :], 0), axis=1)


def adam(weight, first, second, grad, rate, decay):
    first_new = beta_one * first + (1 - beta_one) * grad
    second_new = beta_two * second + (1 - beta_two) * grad * grad
    first_hat = first_new / (1 - beta_one**STEP)
    second_hat = second_new / (1 - beta_two**STEP)
    return (
        first_new,
        second_new,
        weight - rate * (first_hat / (jnp.sqrt(second_hat) + adam_eps) + decay * weight),
    )


def shifted(block, axes, distance):
    size = 1
    for axis in axes:
        size *= lax.axis_size(axis)
    route = [(i - distance, i) for i in range(size) if 0 <= i - distance < size]
    return lax.ppermute(block, axes, route)


def swapped(block, axis):
    return lax.ppermute(block, axis, [(0, 1), (1, 0)])


def turned(block, distance):
    return lax.ppermute(block, RING, [(i, (i + distance) % 4) for i in range(4)])


def gathered(block, axes, parts):
    width = block.shape[1] // parts
    return jnp.concatenate(
        [
            lax.all_gather(block[:, i * width : (i + 1) * width], axes, axis=0, tiled=True)
            for i in range(parts)
        ],
        axis=1,
    )


def pick(blocks, index, axis=0):
    return lax.dynamic_index_in_dim(blocks, index, axis, keepdims=False)


def core_summed(partial, chips):
    core = lax.axis_index("core")
    blocks = partial.reshape(chips, 2, -1, partial.shape[1])
    other = swapped(pick(blocks, 1 - core, 1), "core")
    return pick(blocks, core, 1).astype(f32) + other.astype(f32)


def scattered_mp(partial):
    place = lax.axis_index("zl")
    summed = core_summed(partial, 2)
    other = swapped(pick(summed, 1 - place).astype(bf16), "zl")
    return pick(summed, place) + other.astype(f32)


def scattered_col(partial):
    place = lax.axis_index(RING)
    summed = core_summed(partial, 4)
    others = [
        turned(pick(summed, (place + i) % 4).astype(bf16), i).astype(f32) for i in (1, 3, 2)
    ]
    return pick(summed, place) + others[0] + others[1] + others[2]


def halves(block, width):
    low = lax.axis_index("zh") == 0
    first, last = block[..., :width], block[..., width:]
    return jnp.where(low, first, last), jnp.where(low, last, first)


def joined(own, other, axis):
    low = lax.axis_index("zh") == 0
    return jnp.where(
        low, jnp.concatenate([own, other], axis), jnp.concatenate([other, own], axis)
    )


def dot(left, right, dims):
    return lax.dot_general(left, right, ((dims[0], dims[1]), ((), ())), preferred_element_type=f32)


NN = ((1,), (0,))
NT = ((1,), (1,))
TN = ((0,), (0,))


def on_device(
    inputs,
    cotangent,
    seq_lengths,
    gains,
    gains_first,
    gains_second,
    conv_weight,
    conv_first,
    conv_second,
    in_weight,
    in_first,
    in_second,
    out_weight,
    out_first,
    out_second,
    gate_up,
    gate_up_first,
    gate_up_second,
    down_weight,
    down_first,
    down_second,
):
    tok_rows = inputs.shape[0]
    group_len = tok_rows * 4
    chan_len = conv_weight.shape[1]
    rows_len = in_weight.shape[1]
    half = gate_up.shape[2] // 2
    wide = -(-half // 128) * 128
    mp_index = lax.axis_index(MP)
    zh = lax.axis_index("zh")

    in_rows = in_weight.astype(bf16).transpose(1, 0, 2).reshape(rows_len, 3 * chan_len)
    out_rows = out_weight.astype(bf16).T
    w_in = lax.all_gather(in_rows, DP, axis=0, tiled=True)
    w_out = lax.all_gather(out_rows, DP, axis=0, tiled=True)

    def padded(block):
        return jnp.pad(block, ((0, 0), (0, wide - half)))

    own, away = halves(gate_up.astype(bf16), half)
    gate_rows = joined(
        jnp.concatenate([padded(own[0]), padded(own[1])], 1),
        swapped(jnp.concatenate([padded(away[0]), padded(away[1])], 1), "zh"),
        0,
    )
    own, away = halves(down_weight.astype(bf16).T, half)
    down_rows = joined(padded(own), swapped(padded(away), "zh"), 0)
    w_gate_up = lax.all_gather(gate_rows, XY, axis=0, tiled=True)
    w_down = lax.all_gather(down_rows, XY, axis=0, tiled=True)

    first_row = lax.axis_index(DP) * group_len
    place = positions(seq_lengths, first_row, group_len + 2)
    fwd_one = (place[:group_len] >= 1).astype(f32)[:, None]
    fwd_two = (place[:group_len] >= 2).astype(f32)[:, None]
    back_one = (place[1 : group_len + 1] >= 1).astype(f32)[:, None]
    back_two = (place[2:] >= 2).astype(f32)[:, None]

    resid = inputs.astype(f32)
    scale_one = lax.rsqrt(jnp.mean(resid * resid, axis=-1, keepdims=True) + norm_eps)
    unit_one = resid * scale_one
    normed_one = (unit_one * gains[0]).astype(bf16)
    group_in = gathered(normed_one, MP, 2)
    column_cot = gathered(cotangent, COL, 4)
    projected = dot(group_in, w_in, NN)
    proj_b = projected[:, :chan_len]
    proj_c = projected[:, chan_len : 2 * chan_len]
    proj_x = projected[:, 2 * chan_len :]
    gated = proj_b * proj_x
    carried = shifted(gated[group_len - 2 :], DP, 1)
    extended = jnp.concatenate([carried, gated], 0)
    one_back = extended[1 : group_len + 1] * fwd_one
    two_back = extended[:group_len] * fwd_two
    convolved = conv_weight[0] * gated + conv_weight[1] * one_back + conv_weight[2] * two_back
    mixed = (proj_c * convolved).astype(bf16)
    middle = resid + scattered_mp(dot(mixed, w_out, NT).astype(bf16))

    scale_two = lax.rsqrt(jnp.mean(middle * middle, axis=-1, keepdims=True) + norm_eps)
    unit_two = middle * scale_two
    normed_two = (unit_two * gains[1]).astype(bf16)
    column_mid = gathered(normed_two, COL, 4)
    gate_vals = dot(column_mid, w_gate_up, NN)
    gate, up = gate_vals[:, :wide], gate_vals[:, wide:]
    sigma = jax.nn.sigmoid(gate)
    swish = gate * sigma
    hidden = (swish * up).astype(bf16)
    grad_hidden = dot(column_cot, w_down, NN)
    grad_gate = grad_hidden * up * sigma * (1.0 + gate * (1.0 - sigma))
    grad_up = grad_hidden * swish
    grad_pair = jnp.concatenate([grad_gate.astype(bf16), grad_up.astype(bf16)], 1)
    grad_normed_two = scattered_col(dot(grad_pair, w_gate_up, NT).astype(bf16))
    block_out = (middle + scattered_col(dot(hidden, w_down, NT).astype(bf16))).astype(bf16)
    grad_down = dot(column_cot, hidden, TN).astype(bf16)
    grad_gate_up = dot(column_mid, grad_pair, TN).astype(bf16)
    grad_down = lax.psum_scatter(grad_down, XY, scatter_dimension=0, tiled=True)
    grad_gate_up = lax.psum_scatter(grad_gate_up, XY, scatter_dimension=0, tiled=True)

    gain_two_part = jnp.sum(grad_normed_two * unit_two, axis=0)
    grad_unit_two = grad_normed_two * gains[1]
    grad_middle = cotangent.astype(f32) + scale_two * (
        grad_unit_two - unit_two * jnp.mean(grad_unit_two * unit_two, axis=-1, keepdims=True)
    )

    group_back = gathered(grad_middle.astype(bf16), MP, 2)
    grad_mixed = dot(group_back, w_out, NN)
    grad_out = dot(group_back, mixed, TN).astype(bf16)
    grad_out = lax.psum_scatter(grad_out, XY, scatter_dimension=0, tiled=True)
    grad_readout = grad_mixed * convolved
    grad_conv_out = grad_mixed * proj_c
    conv_part = jnp.stack(
        [
            jnp.sum(grad_conv_out * gated, axis=0),
            jnp.sum(grad_conv_out * one_back, axis=0),
            jnp.sum(grad_conv_out * two_back, axis=0),
        ]
    )
    following = shifted(grad_conv_out[:2], DP, -1)
    ahead = jnp.concatenate([grad_conv_out, following], 0)
    grad_gated = (
        conv_weight[0] * grad_conv_out
        + conv_weight[1] * ahead[1 : group_len + 1] * back_one
        + conv_weight[2] * ahead[2:] * back_two
    )
    grad_proj = jnp.concatenate(
        [
            (grad_gated * proj_x).astype(bf16),
            grad_readout.astype(bf16),
            (grad_gated * proj_b).astype(bf16),
        ],
        1,
    )
    grad_in = dot(group_in, grad_proj, TN).astype(bf16)
    grad_in = lax.psum_scatter(grad_in, XY, scatter_dimension=0, tiled=True)
    grad_normed_one = scattered_mp(dot(grad_proj, w_in, NT).astype(bf16))
    gain_one_part = jnp.sum(grad_normed_one * unit_one, axis=0)
    grad_unit_one = grad_normed_one * gains[0]
    input_grad = grad_middle + scale_one * (
        grad_unit_one - unit_one * jnp.mean(grad_unit_one * unit_one, axis=-1, keepdims=True)
    )

    def both(block):
        pair = block.reshape(2, rows_len, -1)
        return pick(pair, zh), swapped(pick(pair, 1 - zh), "zh")

    own, other = both(grad_in)
    grad_in = (own.astype(f32) + other.astype(f32)).reshape(rows_len, 3, chan_len)
    grad_in = grad_in.transpose(1, 0, 2)
    own, other = both(grad_out)
    grad_out = (own.astype(f32) + other.astype(f32)).T
    own, other = both(grad_gate_up)
    grad_gate_up = jnp.stack(
        [
            joined(own[:, :half], other[:, :half], 1),
            joined(own[:, wide : wide + half], other[:, wide : wide + half], 1),
        ]
    ).astype(f32)
    own, other = both(grad_down)
    grad_down = joined(own[:, :half], other[:, :half], 1).astype(f32).T

    conv_full = lax.dynamic_update_slice(
        jnp.zeros((3, chan_len * 4), f32), conv_part, (jnp.int32(0), mp_index * chan_len)
    )
    gain_sum, conv_sum = lax.psum(
        (jnp.stack([gain_one_part, gain_two_part]), conv_full), DP + MP
    )
    grad_taps = lax.dynamic_slice_in_dim(conv_sum, mp_index * chan_len, chan_len, 1)
    gains_set = adam(gains, gains_first, gains_second, gain_sum, 1.0, 0.0)
    conv_set = adam(conv_weight, conv_first, conv_second, grad_taps, 1.0, 0.0)
    in_set = adam(in_weight, in_first, in_second, grad_in, 2.0 * D ** (-0.5), weight_decay)
    out_set = adam(out_weight, out_first, out_second, grad_out, 2.0 * D ** (-0.5), weight_decay)
    gate_set = adam(
        gate_up, gate_up_first, gate_up_second, grad_gate_up, 2.0 * D ** (-0.5), weight_decay
    )
    down_set = adam(
        down_weight, down_first, down_second, grad_down, 2.0 * FF ** (-0.5), weight_decay
    )
    return (block_out, input_grad, *gains_set, *conv_set, *in_set, *out_set, *gate_set, *down_set)


def solution(mesh):
    parts = Mesh(mesh.devices.reshape(4, 4, 2, 2, 2), ("x", "y", "zh", "zl", "core"))
    tokens = P(DP + MP, None)
    taps = P(None, MP)
    wide_in = P(None, DP, MP)
    wide_out = P(MP, DP)
    in_specs = (
        (tokens,) * 2 + (P(),) * 4 + (taps,) * 3 + (wide_in,) * 3 + (wide_out,) * 3
        + (wide_in,) * 3 + (wide_out,) * 3
    )
    out_specs = (
        (tokens,) * 2 + (P(),) * 3 + (taps,) * 3 + (wide_in,) * 3 + (wide_out,) * 3
        + (wide_in,) * 3 + (wide_out,) * 3
    )
    return jax.shard_map(
        on_device, mesh=parts, in_specs=in_specs, out_specs=out_specs, check_vma=False
    )
```

```python
import jax
import jax.numpy as jnp
from jax import lax
from jax.sharding import Mesh
from jax.sharding import PartitionSpec as P

D = 1536
FF = 6912
STEP = 5

norm_eps = 1e-05
beta_one = 0.9
beta_two = 0.95
adam_eps = 1e-08
weight_decay = 0.1

bf16 = jnp.bfloat16
f32 = jnp.float32

XY = ("x", "y")
DP = ("x", "y", "zh")
MP = ("zl", "core")
RING = ("zh", "zl")
COL = ("zh", "zl", "core")


def positions(seq_lengths, first_row, count):
    ends = jnp.cumsum(seq_lengths)
    starts = ends - seq_lengths
    rows = first_row + jnp.arange(count, dtype=jnp.int32)
    covered = starts[None, :] <= rows[:, None]
    return rows - jnp.max(jnp.where(covered, starts[None, :], 0), axis=1)


def adam(weight, first, second, grad, rate, decay):
    first_new = beta_one * first + (1 - beta_one) * grad
    second_new = beta_two * second + (1 - beta_two) * grad * grad
    first_hat = first_new / (1 - beta_one**STEP)
    second_hat = second_new / (1 - beta_two**STEP)
    return (
        first_new,
        second_new,
        weight - rate * (first_hat / (jnp.sqrt(second_hat) + adam_eps) + decay * weight),
    )


def shifted(block, axes, distance):
    size = 1
    for axis in axes:
        size *= lax.axis_size(axis)
    route = [(i - distance, i) for i in range(size) if 0 <= i - distance < size]
    return lax.ppermute(block, axes, route)


def swapped(block, axis):
    return lax.ppermute(block, axis, [(0, 1), (1, 0)])


def turned(block, distance):
    return lax.ppermute(block, RING, [(i, (i + distance) % 4) for i in range(4)])


def gathered(block, axes, parts):
    width = block.shape[1] // parts
    return jnp.concatenate(
        [
            lax.all_gather(block[:, i * width : (i + 1) * width], axes, axis=0, tiled=True)
            for i in range(parts)
        ],
        axis=1,
    )


def column_gathered(block):
    own = jnp.concatenate([block, turned(block, 1), turned(block, 3), turned(block, 2)], 0)
    return jnp.concatenate([own, swapped(own, "core")], 0)


def column_scattered(partial):
    own, away = jnp.split(partial, 2, 0)
    summed = own.astype(f32) + swapped(away, "core").astype(f32)
    blocks = jnp.split(summed, 4, 0)
    others = [turned(blocks[i].astype(bf16), d) for i, d in ((1, 3), (2, 1), (3, 2))]
    return blocks[0] + others[0].astype(f32) + others[1].astype(f32) + others[2].astype(f32)


def ring_scattered(blocks, axis):
    place = lax.axis_index(axis)
    others = [
        lax.ppermute(
            pick(blocks, (place + d) % 4), axis, [(i, (i + d) % 4) for i in range(4)]
        ).astype(f32)
        for d in (1, 3, 2)
    ]
    return pick(blocks, place).astype(f32) + others[0] + others[1] + others[2]


def small_sum(block):
    for axes in (COL, ("x",), ("y",)):
        block = jnp.sum(lax.all_gather(block, axes, axis=0), axis=0)
    return block


def pick(blocks, index, axis=0):
    return lax.dynamic_index_in_dim(blocks, index, axis, keepdims=False)


def core_summed(partial, chips):
    core = lax.axis_index("core")
    blocks = partial.reshape(chips, 2, -1, partial.shape[1])
    other = swapped(pick(blocks, 1 - core, 1), "core")
    return pick(blocks, core, 1).astype(f32) + other.astype(f32)


def scattered_mp(partial):
    place = lax.axis_index("zl")
    summed = core_summed(partial, 2)
    other = swapped(pick(summed, 1 - place).astype(bf16), "zl")
    return pick(summed, place) + other.astype(f32)


def halves(block, width):
    low = lax.axis_index("zh") == 0
    first, last = block[..., :width], block[..., width:]
    return jnp.where(low, first, last), jnp.where(low, last, first)


def joined(own, other, axis):
    low = lax.axis_index("zh") == 0
    return jnp.where(
        low, jnp.concatenate([own, other], axis), jnp.concatenate([other, own], axis)
    )


def dot(left, right, dims):
    return lax.dot_general(left, right, ((dims[0], dims[1]), ((), ())), preferred_element_type=f32)


NN = ((1,), (0,))
NT = ((1,), (1,))
TN = ((0,), (0,))


def on_device(
    inputs,
    cotangent,
    seq_lengths,
    gains,
    gains_first,
    gains_second,
    conv_weight,
    conv_first,
    conv_second,
    in_weight,
    in_first,
    in_second,
    out_weight,
    out_first,
    out_second,
    gate_up,
    gate_up_first,
    gate_up_second,
    down_weight,
    down_first,
    down_second,
):
    tok_rows = inputs.shape[0]
    group_len = tok_rows * 4
    chan_len = conv_weight.shape[1]
    rows_len = in_weight.shape[1]
    half = gate_up.shape[2] // 2
    wide = -(-half // 128) * 128
    mp_index = lax.axis_index(MP)
    zh = lax.axis_index("zh")

    mix_rows = jnp.concatenate(
        [
            in_weight.astype(bf16).transpose(1, 0, 2).reshape(rows_len, 3 * chan_len),
            out_weight.astype(bf16).T,
        ],
        1,
    )
    mix_rows = joined(mix_rows, swapped(mix_rows, "zh"), 0)
    w_mix = lax.all_gather(mix_rows, XY, axis=0, tiled=True)
    w_in, w_out = w_mix[:, : 3 * chan_len], w_mix[:, 3 * chan_len :]

    def padded(block):
        return jnp.pad(block, ((0, 0), (0, wide - half)))

    own_gate, away_gate = halves(gate_up.astype(bf16), half)
    own_down, away_down = halves(down_weight.astype(bf16).T, half)
    own, away = (
        jnp.concatenate([padded(g[0]), padded(g[1]), padded(d)], 1)
        for g, d in ((own_gate, own_down), (away_gate, away_down))
    )
    ff_rows = joined(own, swapped(away, "zh"), 0)
    w_ff = lax.all_gather(ff_rows, XY, axis=0, tiled=True)
    w_gate_up, w_down = w_ff[:, : 2 * wide], w_ff[:, 2 * wide :]

    first_row = lax.axis_index(DP) * group_len
    place = positions(seq_lengths, first_row, group_len + 2)
    fwd_one = (place[:group_len] >= 1).astype(f32)[:, None]
    fwd_two = (place[:group_len] >= 2).astype(f32)[:, None]
    back_one = (place[1 : group_len + 1] >= 1).astype(f32)[:, None]
    back_two = (place[2:] >= 2).astype(f32)[:, None]

    resid = inputs.astype(f32)
    scale_one = lax.rsqrt(jnp.mean(resid * resid, axis=-1, keepdims=True) + norm_eps)
    unit_one = resid * scale_one
    normed_one = (unit_one * gains[0]).astype(bf16)
    group_in = gathered(normed_one, MP, 2)
    lead = 16
    before = shifted(group_in[group_len - lead :], DP, 1)
    column_cot = column_gathered(cotangent)
    column_cot, w_in = lax.optimization_barrier((column_cot, w_in))
    projected = dot(jnp.concatenate([before, group_in], 0), w_in, NN)
    proj_b = projected[lead:, :chan_len]
    proj_c = projected[lead:, chan_len : 2 * chan_len]
    proj_x = projected[lead:, 2 * chan_len :]
    extended = projected[:, :chan_len] * projected[:, 2 * chan_len :]
    gated = extended[lead:]
    one_back = extended[lead - 1 : lead - 1 + group_len] * fwd_one
    two_back = extended[lead - 2 : lead - 2 + group_len] * fwd_two
    convolved = conv_weight[0] * gated + conv_weight[1] * one_back + conv_weight[2] * two_back
    mixed = (proj_c * convolved).astype(bf16)
    middle = resid + scattered_mp(dot(mixed, w_out, NT).astype(bf16))

    scale_two = lax.rsqrt(jnp.mean(middle * middle, axis=-1, keepdims=True) + norm_eps)
    unit_two = middle * scale_two
    normed_two = (unit_two * gains[1]).astype(bf16)
    column_mid = column_gathered(normed_two)
    gate_vals = dot(column_mid, w_gate_up, NN)
    gate, up = gate_vals[:, :wide], gate_vals[:, wide:]
    sigma = jax.nn.sigmoid(gate)
    swish = gate * sigma
    hidden = (swish * up).astype(bf16)
    grad_hidden = dot(column_cot, w_down, NN)
    grad_gate = grad_hidden * up * sigma * (1.0 + gate * (1.0 - sigma))
    grad_up = grad_hidden * swish
    grad_pair = jnp.concatenate([grad_gate.astype(bf16), grad_up.astype(bf16)], 1)
    grad_normed_two = dot(grad_pair, w_gate_up, NT).astype(bf16)
    grad_normed_two, grad_pair, hidden = lax.optimization_barrier(
        (grad_normed_two, grad_pair, hidden)
    )
    grad_normed_two = column_scattered(grad_normed_two)
    grad_ff = jnp.concatenate(
        [dot(column_mid, grad_pair, TN).astype(bf16), dot(column_cot, hidden, TN).astype(bf16)], 1
    )
    grad_normed_two, _ = lax.optimization_barrier((grad_normed_two, grad_ff))
    grad_ff = lax.psum_scatter(grad_ff, XY, scatter_dimension=0, tiled=True)
    block_out = (middle + column_scattered(dot(hidden, w_down, NT).astype(bf16))).astype(bf16)

    gain_two_part = jnp.sum(grad_normed_two * unit_two, axis=0)
    grad_unit_two = grad_normed_two * gains[1]
    grad_middle = cotangent.astype(f32) + scale_two * (
        grad_unit_two - unit_two * jnp.mean(grad_unit_two * unit_two, axis=-1, keepdims=True)
    )

    group_back = gathered(grad_middle.astype(bf16), MP, 2)
    grad_mixed = dot(group_back, w_out, NN)
    grad_conv_out = grad_mixed * proj_c
    following = shifted(grad_conv_out[:2], DP, -1)
    grad_readout = (grad_mixed * convolved).astype(bf16)
    early = jnp.concatenate(
        [dot(group_in, grad_readout, TN).astype(bf16), dot(group_back, mixed, TN).astype(bf16)], 1
    )
    conv_part = jnp.stack(
        [
            jnp.sum(grad_conv_out * gated, axis=0),
            jnp.sum(grad_conv_out * one_back, axis=0),
            jnp.sum(grad_conv_out * two_back, axis=0),
        ]
    )
    ahead = jnp.concatenate([grad_conv_out, following], 0)
    grad_gated = (
        conv_weight[0] * grad_conv_out
        + conv_weight[1] * ahead[1 : group_len + 1] * back_one
        + conv_weight[2] * ahead[2:] * back_two
    )
    grad_bx = jnp.concatenate(
        [(grad_gated * proj_x).astype(bf16), (grad_gated * proj_b).astype(bf16)], 1
    )
    late = dot(group_in, grad_bx, TN).astype(bf16)

    early = early.reshape(4, 4, 2 * rows_len, 2 * chan_len).transpose(1, 0, 2, 3)
    late = late.reshape(4, 4, 2 * rows_len, 2 * chan_len)
    early = ring_scattered(early, "y").astype(bf16)
    late = ring_scattered(late, "x").astype(bf16)
    early = ring_scattered(early, "x").astype(bf16)
    late = ring_scattered(late, "y").astype(bf16)
    grad_mix = jnp.concatenate([late, early], 1)

    grad_proj = jnp.concatenate([grad_bx[:, :chan_len], grad_readout, grad_bx[:, chan_len:]], 1)
    grad_normed_one = scattered_mp(dot(grad_proj, w_in, NT).astype(bf16))
    gain_one_part = jnp.sum(grad_normed_one * unit_one, axis=0)
    grad_unit_one = grad_normed_one * gains[0]
    input_grad = grad_middle + scale_one * (
        grad_unit_one - unit_one * jnp.mean(grad_unit_one * unit_one, axis=-1, keepdims=True)
    )

    def both(block):
        pair = block.reshape(2, rows_len, -1)
        return pick(pair, zh), swapped(pick(pair, 1 - zh), "zh")

    own, other = both(grad_mix)
    grad_mix = own.astype(f32) + other.astype(f32)
    order = (0, 2, 1, 3)
    grad_mix = [grad_mix[:, i * chan_len : (i + 1) * chan_len] for i in order]
    grad_in = jnp.stack(grad_mix[:3])
    grad_out = grad_mix[3].T
    own, other = both(grad_ff)
    grad_gate, grad_up, grad_down = (
        joined(own[:, i * wide : i * wide + half], other[:, i * wide : i * wide + half], 1)
        for i in range(3)
    )
    grad_gate_up = jnp.stack([grad_gate, grad_up]).astype(f32)
    grad_down = grad_down.astype(f32).T

    conv_full = lax.dynamic_update_slice(
        jnp.zeros((3, chan_len * 4), f32), conv_part, (jnp.int32(0), mp_index * chan_len)
    )
    small = small_sum(jnp.concatenate([gain_one_part[None], gain_two_part[None], conv_full], 0))
    gain_sum, conv_sum = small[:2], small[2:]
    grad_taps = lax.dynamic_slice_in_dim(conv_sum, mp_index * chan_len, chan_len, 1)
    gains_set = adam(gains, gains_first, gains_second, gain_sum, 1.0, 0.0)
    conv_set = adam(conv_weight, conv_first, conv_second, grad_taps, 1.0, 0.0)
    in_set = adam(in_weight, in_first, in_second, grad_in, 2.0 * D ** (-0.5), weight_decay)
    out_set = adam(out_weight, out_first, out_second, grad_out, 2.0 * D ** (-0.5), weight_decay)
    gate_set = adam(
        gate_up, gate_up_first, gate_up_second, grad_gate_up, 2.0 * D ** (-0.5), weight_decay
    )
    down_set = adam(
        down_weight, down_first, down_second, grad_down, 2.0 * FF ** (-0.5), weight_decay
    )
    return (block_out, input_grad, *gains_set, *conv_set, *in_set, *out_set, *gate_set, *down_set)


def solution(mesh):
    parts = Mesh(mesh.devices.reshape(4, 4, 2, 2, 2), ("x", "y", "zh", "zl", "core"))
    tokens = P(DP + MP, None)
    taps = P(None, MP)
    wide_in = P(None, DP, MP)
    wide_out = P(MP, DP)
    in_specs = (
        (tokens,) * 2 + (P(),) * 4 + (taps,) * 3 + (wide_in,) * 3 + (wide_out,) * 3
        + (wide_in,) * 3 + (wide_out,) * 3
    )
    out_specs = (
        (tokens,) * 2 + (P(),) * 3 + (taps,) * 3 + (wide_in,) * 3 + (wide_out,) * 3
        + (wide_in,) * 3 + (wide_out,) * 3
    )
    return jax.shard_map(
        on_device, mesh=parts, in_specs=in_specs, out_specs=out_specs, check_vma=False
    )
```

```python
import jax
import jax.numpy as jnp
from jax import lax
from jax.sharding import Mesh
from jax.sharding import PartitionSpec as P

D = 1536
FF = 6912
STEP = 5

norm_eps = 1e-05
beta_one = 0.9
beta_two = 0.95
adam_eps = 1e-08
weight_decay = 0.1

bf16 = jnp.bfloat16
f32 = jnp.float32

XY = ("x", "y")
DP = ("x", "y", "zh")
MP = ("zl", "core")
RING = ("zh", "zl")
COL = ("zh", "zl", "core")


def positions(seq_lengths, first_row, count):
    ends = jnp.cumsum(seq_lengths)
    starts = ends - seq_lengths
    rows = first_row + jnp.arange(count, dtype=jnp.int32)
    covered = starts[None, :] <= rows[:, None]
    return rows - jnp.max(jnp.where(covered, starts[None, :], 0), axis=1)


def adam(weight, first, second, grad, rate, decay):
    first_new = beta_one * first + (1 - beta_one) * grad
    second_new = beta_two * second + (1 - beta_two) * grad * grad
    first_hat = first_new / (1 - beta_one**STEP)
    second_hat = second_new / (1 - beta_two**STEP)
    return (
        first_new,
        second_new,
        weight - rate * (first_hat / (jnp.sqrt(second_hat) + adam_eps) + decay * weight),
    )


def shifted(block, axes, distance):
    size = 1
    for axis in axes:
        size *= lax.axis_size(axis)
    route = [(i - distance, i) for i in range(size) if 0 <= i - distance < size]
    return lax.ppermute(block, axes, route)


def swapped(block, axis):
    return lax.ppermute(block, axis, [(0, 1), (1, 0)])


def turned(block, distance):
    return lax.ppermute(block, RING, [(i, (i + distance) % 4) for i in range(4)])


def gathered(block, axes, parts):
    width = block.shape[1] // parts
    return jnp.concatenate(
        [
            lax.all_gather(block[:, i * width : (i + 1) * width], axes, axis=0, tiled=True)
            for i in range(parts)
        ],
        axis=1,
    )


def column_gathered(block):
    own = jnp.concatenate([block, turned(block, 1), turned(block, 3), turned(block, 2)], 0)
    return jnp.concatenate([own, swapped(own, "core")], 0)


def column_scattered(summed):
    blocks = jnp.split(summed, 4, 0)
    others = [turned(blocks[i].astype(bf16), d) for i, d in ((1, 3), (2, 1), (3, 2))]
    return blocks[0] + others[0].astype(f32) + others[1].astype(f32) + others[2].astype(f32)


def in_place_order(partial):
    z, core = lax.axis_index(RING), lax.axis_index("core")
    blocks = partial.reshape(8, -1, partial.shape[1])
    slots = []
    for i in range(8):
        offset = (i // 2 - z) % 4
        slot = jnp.where(offset == 0, 0, jnp.where(offset == 3, 1, offset + 1))
        slots.append(pick(blocks, slot + 4 * ((i % 2) ^ core)))
    return jnp.concatenate(slots, 0)


def ring_scattered(blocks, axis):
    place = lax.axis_index(axis)
    others = [
        lax.ppermute(
            pick(blocks, (place + d) % 4), axis, [(i, (i + d) % 4) for i in range(4)]
        ).astype(f32)
        for d in (1, 3, 2)
    ]
    return pick(blocks, place).astype(f32) + others[0] + others[1] + others[2]


def small_sum(block):
    for axes, count in ((COL, 8), (("x",), 4), (("y",), 4)):
        copies = jnp.broadcast_to(block, (count, *block.shape))
        block = jnp.sum(lax.all_to_all(copies, axes, 0, 0, tiled=True), axis=0)
    return block


def pick(blocks, index, axis=0):
    return lax.dynamic_index_in_dim(blocks, index, axis, keepdims=False)


def core_summed(partial, chips):
    core = lax.axis_index("core")
    blocks = partial.reshape(chips, 2, -1, partial.shape[1])
    other = swapped(pick(blocks, 1 - core, 1), "core")
    return pick(blocks, core, 1).astype(f32) + other.astype(f32)


def scattered_mp(partial):
    place = lax.axis_index("zl")
    summed = core_summed(partial, 2)
    other = swapped(pick(summed, 1 - place).astype(bf16), "zl")
    return pick(summed, place) + other.astype(f32)


def halves(block, width):
    low = lax.axis_index("zh") == 0
    first, last = block[..., :width], block[..., width:]
    return jnp.where(low, first, last), jnp.where(low, last, first)


def joined(own, other, axis):
    low = lax.axis_index("zh") == 0
    return jnp.where(
        low, jnp.concatenate([own, other], axis), jnp.concatenate([other, own], axis)
    )


def dot(left, right, dims):
    return lax.dot_general(left, right, ((dims[0], dims[1]), ((), ())), preferred_element_type=f32)


NN = ((1,), (0,))
NT = ((1,), (1,))
TN = ((0,), (0,))


def on_device(
    inputs,
    cotangent,
    seq_lengths,
    gains,
    gains_first,
    gains_second,
    conv_weight,
    conv_first,
    conv_second,
    in_weight,
    in_first,
    in_second,
    out_weight,
    out_first,
    out_second,
    gate_up,
    gate_up_first,
    gate_up_second,
    down_weight,
    down_first,
    down_second,
):
    tok_rows = inputs.shape[0]
    group_len = tok_rows * 4
    chan_len = conv_weight.shape[1]
    rows_len = in_weight.shape[1]
    half = gate_up.shape[2] // 2
    wide = -(-half // 128) * 128
    mp_index = lax.axis_index(MP)
    zh = lax.axis_index("zh")

    mix_rows = jnp.concatenate(
        [
            in_weight.astype(bf16).transpose(1, 0, 2).reshape(rows_len, 3 * chan_len),
            out_weight.astype(bf16).T,
        ],
        1,
    )

    def padded(block):
        return jnp.pad(block, ((0, 0), (0, wide - half)))

    own_down, away_down = halves(down_weight.astype(bf16).T, half)
    own = jnp.concatenate([mix_rows, padded(own_down)], 1)
    away = jnp.concatenate([mix_rows, padded(away_down)], 1)
    w_mix = lax.all_gather(joined(own, swapped(away, "zh"), 0), XY, axis=0, tiled=True)
    w_in, w_out = w_mix[:, : 3 * chan_len], w_mix[:, 3 * chan_len : 4 * chan_len]
    w_down = w_mix[:, 4 * chan_len :]
    own_gate, away_gate = halves(gate_up.astype(bf16), half)
    own, away = (jnp.concatenate([padded(g[0]), padded(g[1])], 1) for g in (own_gate, away_gate))
    w_gate_up = lax.all_gather(joined(own, swapped(away, "zh"), 0), XY, axis=0, tiled=True)

    first_row = lax.axis_index(DP) * group_len
    place = positions(seq_lengths, first_row, group_len + 2)
    fwd_one = (place[:group_len] >= 1).astype(f32)[:, None]
    fwd_two = (place[:group_len] >= 2).astype(f32)[:, None]
    back_one = (place[1 : group_len + 1] >= 1).astype(f32)[:, None]
    back_two = (place[2:] >= 2).astype(f32)[:, None]

    resid = inputs.astype(f32)
    scale_one = lax.rsqrt(jnp.mean(resid * resid, axis=-1, keepdims=True) + norm_eps)
    unit_one = resid * scale_one
    normed_one = (unit_one * gains[0]).astype(bf16)
    group_in = gathered(normed_one, MP, 2)
    lead = 16
    before = shifted(group_in[group_len - lead :], DP, 1)
    column_cot = column_gathered(cotangent)
    turned_in = group_in.reshape(group_len, 4, 4, D // 16).transpose(0, 2, 1, 3)
    turned_in = turned_in.reshape(group_len, D)
    column_cot, turned_in, w_in = lax.optimization_barrier((column_cot, turned_in, w_in))
    projected = dot(jnp.concatenate([before, group_in], 0), w_in, NN)
    proj_b = projected[lead:, :chan_len]
    proj_c = projected[lead:, chan_len : 2 * chan_len]
    proj_x = projected[lead:, 2 * chan_len :]
    extended = projected[:, :chan_len] * projected[:, 2 * chan_len :]
    gated = extended[lead:]
    one_back = extended[lead - 1 : lead - 1 + group_len] * fwd_one
    two_back = extended[lead - 2 : lead - 2 + group_len] * fwd_two
    convolved = conv_weight[0] * gated + conv_weight[1] * one_back + conv_weight[2] * two_back
    mixed = (proj_c * convolved).astype(bf16)
    middle = resid + scattered_mp(dot(mixed, w_out, NT).astype(bf16))
    grad_hidden = dot(column_cot, w_down, NN)
    middle, grad_hidden = lax.optimization_barrier((middle, grad_hidden))

    scale_two = lax.rsqrt(jnp.mean(middle * middle, axis=-1, keepdims=True) + norm_eps)
    unit_two = middle * scale_two
    normed_two = (unit_two * gains[1]).astype(bf16)
    column_mid = column_gathered(normed_two)
    gate_vals = dot(column_mid, w_gate_up, NN)
    gate, up = gate_vals[:, :wide], gate_vals[:, wide:]
    sigma = jax.nn.sigmoid(gate)
    swish = gate * sigma
    hidden = (swish * up).astype(bf16)
    grad_gate = grad_hidden * up * sigma * (1.0 + gate * (1.0 - sigma))
    grad_up = grad_hidden * swish
    grad_pair = jnp.concatenate([grad_gate.astype(bf16), grad_up.astype(bf16)], 1)
    own_pair, away_pair = jnp.split(grad_pair, 2, 0)
    away = dot(away_pair, w_gate_up, NT).astype(bf16)
    away, own_pair = lax.optimization_barrier((away, own_pair))
    summed, away = lax.optimization_barrier(
        (dot(own_pair, w_gate_up, NT), swapped(away, "core"))
    )
    summed = summed + away.astype(f32)
    summed, grad_pair, hidden = lax.optimization_barrier((summed, grad_pair, hidden))
    grad_normed_two = column_scattered(summed)
    grad_ff = jnp.concatenate(
        [dot(column_mid, grad_pair, TN).astype(bf16), dot(column_cot, hidden, TN).astype(bf16)], 1
    )
    ff_out = in_place_order(dot(hidden, w_down, NT).astype(bf16))
    grad_normed_two, grad_ff, ff_out = lax.optimization_barrier(
        (grad_normed_two, grad_ff, ff_out)
    )
    grad_ff = lax.psum_scatter(grad_ff, XY, scatter_dimension=0, tiled=True)
    ff_out = lax.psum_scatter(ff_out, COL, scatter_dimension=0, tiled=True)
    block_out = (middle + ff_out.astype(f32)).astype(bf16)

    gain_two_part = jnp.sum(grad_normed_two * unit_two, axis=0)
    grad_unit_two = grad_normed_two * gains[1]
    grad_middle = cotangent.astype(f32) + scale_two * (
        grad_unit_two - unit_two * jnp.mean(grad_unit_two * unit_two, axis=-1, keepdims=True)
    )

    group_back = gathered(grad_middle.astype(bf16), MP, 2)
    grad_mixed = dot(group_back, w_out, NN)
    grad_conv_out = grad_mixed * proj_c
    following = shifted(grad_conv_out[:2], DP, -1)
    grad_readout = (grad_mixed * convolved).astype(bf16)
    early = jnp.concatenate(
        [dot(group_in, grad_readout, TN).astype(bf16), dot(group_back, mixed, TN).astype(bf16)], 1
    )
    conv_part = jnp.stack(
        [
            jnp.sum(grad_conv_out * gated, axis=0),
            jnp.sum(grad_conv_out * one_back, axis=0),
            jnp.sum(grad_conv_out * two_back, axis=0),
        ]
    )
    following, early = lax.optimization_barrier((following, early))
    ahead = jnp.concatenate([grad_conv_out, following], 0)
    grad_gated = (
        conv_weight[0] * grad_conv_out
        + conv_weight[1] * ahead[1 : group_len + 1] * back_one
        + conv_weight[2] * ahead[2:] * back_two
    )
    grad_bx = jnp.concatenate(
        [(grad_gated * proj_x).astype(bf16), (grad_gated * proj_b).astype(bf16)], 1
    )
    late = dot(turned_in, grad_bx, TN).astype(bf16)

    grad_proj = jnp.concatenate([grad_bx[:, :chan_len], grad_readout, grad_bx[:, chan_len:]], 1)
    grad_normed_one = dot(grad_proj, w_in, NT)
    gain_one_part = jnp.sum(grad_normed_one * group_in.astype(f32), axis=0) / gains[0]
    grad_normed_one = scattered_mp(grad_normed_one.astype(bf16))
    early = early.reshape(4, 4, 2 * rows_len, 2 * chan_len)
    late = late.reshape(4, 4, 2 * rows_len, 2 * chan_len)
    early = ring_scattered(early, "x").astype(bf16)
    early, gain_one_part = lax.optimization_barrier((early, gain_one_part))
    late = ring_scattered(late, "y").astype(bf16)
    early = ring_scattered(early, "y").astype(bf16)
    late = ring_scattered(late, "x").astype(bf16)
    grad_mix = jnp.concatenate([late, early], 1)

    grad_unit_one = grad_normed_one * gains[0]
    input_grad = grad_middle + scale_one * (
        grad_unit_one - unit_one * jnp.mean(grad_unit_one * unit_one, axis=-1, keepdims=True)
    )

    def both(block):
        pair = block.reshape(2, rows_len, -1)
        return pick(pair, zh), swapped(pick(pair, 1 - zh), "zh")

    own_ff, other_ff = both(grad_ff)
    grad_mix, other_ff = lax.optimization_barrier((grad_mix, other_ff))
    own, other = both(grad_mix)
    grad_mix = own.astype(f32) + other.astype(f32)
    order = (0, 2, 1, 3)
    grad_mix = [grad_mix[:, i * chan_len : (i + 1) * chan_len] for i in order]
    grad_in = jnp.stack(grad_mix[:3])
    grad_out = grad_mix[3].T
    grad_gate, grad_up, grad_down = (
        joined(own_ff[:, i * wide : i * wide + half], other_ff[:, i * wide : i * wide + half], 1)
        for i in range(3)
    )
    grad_gate_up = jnp.stack([grad_gate, grad_up]).astype(f32)
    grad_down = grad_down.astype(f32).T

    conv_full = lax.dynamic_update_slice(
        jnp.zeros((3, chan_len * 4), f32), conv_part, (jnp.int32(0), mp_index * chan_len)
    )
    small = small_sum(jnp.concatenate([gain_one_part[None], gain_two_part[None], conv_full], 0))
    gain_sum, conv_sum = small[:2], small[2:]
    grad_taps = lax.dynamic_slice_in_dim(conv_sum, mp_index * chan_len, chan_len, 1)
    gains_set = adam(gains, gains_first, gains_second, gain_sum, 1.0, 0.0)
    conv_set = adam(conv_weight, conv_first, conv_second, grad_taps, 1.0, 0.0)
    in_set = adam(in_weight, in_first, in_second, grad_in, 2.0 * D ** (-0.5), weight_decay)
    out_set = adam(out_weight, out_first, out_second, grad_out, 2.0 * D ** (-0.5), weight_decay)
    gate_set = adam(
        gate_up, gate_up_first, gate_up_second, grad_gate_up, 2.0 * D ** (-0.5), weight_decay
    )
    down_set = adam(
        down_weight, down_first, down_second, grad_down, 2.0 * FF ** (-0.5), weight_decay
    )
    return (block_out, input_grad, *gains_set, *conv_set, *in_set, *out_set, *gate_set, *down_set)


def solution(mesh):
    parts = Mesh(mesh.devices.reshape(4, 4, 2, 2, 2), ("x", "y", "zh", "zl", "core"))
    tokens = P(DP + MP, None)
    taps = P(None, MP)
    wide_in = P(None, DP, MP)
    wide_out = P(MP, DP)
    in_specs = (
        (tokens,) * 2 + (P(),) * 4 + (taps,) * 3 + (wide_in,) * 3 + (wide_out,) * 3
        + (wide_in,) * 3 + (wide_out,) * 3
    )
    out_specs = (
        (tokens,) * 2 + (P(),) * 3 + (taps,) * 3 + (wide_in,) * 3 + (wide_out,) * 3
        + (wide_in,) * 3 + (wide_out,) * 3
    )
    return jax.shard_map(
        on_device, mesh=parts, in_specs=in_specs, out_specs=out_specs, check_vma=False
    )
```

```python
import jax
import jax.numpy as jnp
from jax import lax
from jax.sharding import Mesh
from jax.sharding import PartitionSpec as P

D = 1536
FF = 6912
STEP = 5

norm_eps = 1e-05
beta_one = 0.9
beta_two = 0.95
adam_eps = 1e-08
weight_decay = 0.1

bf16 = jnp.bfloat16
f32 = jnp.float32

XY = ("x", "y")
DP = ("x", "y", "zh")
MP = ("zl", "core")
RING = ("zh", "zl")
COL = ("zh", "zl", "core")


def positions(seq_lengths, first_row, count):
    ends = jnp.cumsum(seq_lengths)
    starts = ends - seq_lengths
    rows = first_row + jnp.arange(count, dtype=jnp.int32)
    covered = starts[None, :] <= rows[:, None]
    return rows - jnp.max(jnp.where(covered, starts[None, :], 0), axis=1)


def adam(weight, first, second, grad, rate, decay):
    first_new = beta_one * first + (1 - beta_one) * grad
    second_new = beta_two * second + (1 - beta_two) * grad * grad
    first_hat = first_new / (1 - beta_one**STEP)
    second_hat = second_new / (1 - beta_two**STEP)
    return (
        first_new,
        second_new,
        weight - rate * (first_hat / (jnp.sqrt(second_hat) + adam_eps) + decay * weight),
    )


def shifted(block, axes, distance):
    size = 1
    for axis in axes:
        size *= lax.axis_size(axis)
    route = [(i - distance, i) for i in range(size) if 0 <= i - distance < size]
    return lax.ppermute(block, axes, route)


def swapped(block, axis):
    return lax.ppermute(block, axis, [(0, 1), (1, 0)])


def exchanged(blocks, axes):
    return lax.all_to_all(blocks, axes, 0, 0, tiled=True)


def spread(block, axes, count):
    return exchanged(jnp.broadcast_to(block, (count, *block.shape)), axes)


def summed_over(block, axes, count):
    blocks = exchanged(block, axes).reshape(count, -1, *block.shape[1:])
    return jnp.sum(blocks.astype(f32), axis=0)


def from_others(blocks, axis):
    return [
        lax.ppermute(blocks[r], axis, [(i, (i + r) % 4) for i in range(4)]) for r in (1, 3, 2)
    ]


def ring_spread(block, axis):
    behind1, behind3, behind2 = from_others([block] * 4, axis)
    return jnp.stack([block, behind3, behind2, behind1])


def ring_summed(blocks, axis):
    total = blocks[0].astype(f32)
    for other in from_others(blocks, axis):
        total = total + other.astype(f32)
    return total


def rolled(blocks, shift):
    return jnp.stack([pick(blocks, (r - shift) % 4) for r in range(4)])


def gathered(block, axes, parts):
    width = block.shape[1] // parts
    return jnp.concatenate(
        [
            lax.all_gather(block[:, i * width : (i + 1) * width], axes, axis=0, tiled=True)
            for i in range(parts)
        ],
        axis=1,
    )


def column_own(block):
    return rolled(ring_spread(block, RING), lax.axis_index(RING)).reshape(-1, block.shape[1])


def pick(blocks, index, axis=0):
    return lax.dynamic_index_in_dim(blocks, index, axis, keepdims=False)


def scattered_mp(partial):
    core, place = lax.axis_index("core"), lax.axis_index("zl")
    blocks = partial.reshape(2, 2, -1, partial.shape[1])
    other = swapped(pick(blocks, 1 - core, 1), "core")
    summed = pick(blocks, core, 1).astype(f32) + other.astype(f32)
    other = swapped(pick(summed, 1 - place).astype(bf16), "zl")
    return pick(summed, place) + other.astype(f32)


def halves(block, width):
    low = lax.axis_index("zh") == 0
    first, last = block[..., :width], block[..., width:]
    return jnp.where(low, first, last), jnp.where(low, last, first)


def joined(own, other, axis):
    low = lax.axis_index("zh") == 0
    return jnp.where(
        low, jnp.concatenate([own, other], axis), jnp.concatenate([other, own], axis)
    )


def dot(left, right, dims):
    return lax.dot_general(left, right, ((dims[0], dims[1]), ((), ())), preferred_element_type=f32)


NN = ((1,), (0,))
NT = ((1,), (1,))
TN = ((0,), (0,))


def on_device(
    inputs,
    cotangent,
    seq_lengths,
    gains,
    gains_first,
    gains_second,
    conv_weight,
    conv_first,
    conv_second,
    in_weight,
    in_first,
    in_second,
    out_weight,
    out_first,
    out_second,
    gate_up,
    gate_up_first,
    gate_up_second,
    down_weight,
    down_first,
    down_second,
):
    tok_rows = inputs.shape[0]
    group_len = tok_rows * 4
    chan_len = conv_weight.shape[1]
    rows_len = in_weight.shape[1]
    half = gate_up.shape[2] // 2
    wide = -(-half // 128) * 128
    mp_index = lax.axis_index(MP)
    zh = lax.axis_index("zh")

    resid = inputs.astype(f32)
    scale_one = lax.rsqrt(jnp.mean(resid * resid, axis=-1, keepdims=True) + norm_eps)
    unit_one = resid * scale_one
    normed_one = (unit_one * gains[0]).astype(bf16)
    group_in = gathered(normed_one, MP, 2)

    def padded(block):
        return jnp.pad(block, ((0, 0), (0, wide - half)))

    in_rows = in_weight.astype(bf16)
    mix_rows = [in_rows[0], in_rows[2], in_rows[1], out_weight.astype(bf16).T]
    own_gate, away_gate = halves(gate_up.astype(bf16), half)
    own_down, away_down = halves(down_weight.astype(bf16).T, half)
    own, away = (
        jnp.concatenate([padded(g[0]), padded(g[1]), padded(d)] + mix_rows, 1)
        for g, d in ((own_gate, own_down), (away_gate, away_down))
    )
    rows = joined(own, swapped(away, "zh"), 0)
    rows, group_in = lax.optimization_barrier((rows, group_in))
    ff_rows, mix_rows = rows[:, : 3 * wide], rows[:, 3 * wide :]
    w_ff = lax.all_gather(ff_rows, XY, axis=0, tiled=True)
    w_gate_up, w_down = w_ff[:, : 2 * wide], w_ff[:, 2 * wide :]
    y = lax.axis_index("y")
    w_bx = spread(mix_rows[:, : 2 * chan_len], "x", 4)
    w_co = rolled(ring_spread(mix_rows[:, 2 * chan_len :], "y"), y)
    w_bx, w_co = lax.optimization_barrier((w_bx, w_co))
    w_bx, cotangent_sent = lax.optimization_barrier((ring_spread(w_bx, "y"), cotangent))
    w_co = spread(w_co, "x", 4).reshape(D, 2 * chan_len)
    w_c, w_out = w_co[:, :chan_len], w_co[:, chan_len:]
    turned_bx = w_bx.reshape(D, 2 * chan_len)

    first_row = lax.axis_index(DP) * group_len
    place = positions(seq_lengths, first_row, group_len + 2)
    fwd_one = (place[:group_len] >= 1).astype(f32)[:, None]
    fwd_two = (place[:group_len] >= 2).astype(f32)[:, None]
    back_one = (place[1 : group_len + 1] >= 1).astype(f32)[:, None]
    back_two = (place[2:] >= 2).astype(f32)[:, None]

    lead = 16
    before = shifted(group_in[group_len - lead :], DP, 1)
    turned_in = jnp.concatenate([before, group_in], 0).reshape(-1, 4, 4, D // 16)
    turned_in = rolled(turned_in.transpose(2, 0, 1, 3), -y).transpose(1, 0, 2, 3).reshape(-1, D)
    turned_in, turned_bx = lax.optimization_barrier((turned_in, turned_bx))
    proj_bx = dot(turned_in, turned_bx, NN)
    proj_c = dot(group_in, w_c, NN)
    proj_b, proj_x = proj_bx[lead:, :chan_len], proj_bx[lead:, chan_len:]
    extended = proj_bx[:, :chan_len] * proj_bx[:, chan_len:]
    gated = extended[lead:]
    one_back = extended[lead - 1 : lead - 1 + group_len] * fwd_one
    two_back = extended[lead - 2 : lead - 2 + group_len] * fwd_two
    convolved = conv_weight[0] * gated + conv_weight[1] * one_back + conv_weight[2] * two_back
    mixed = (proj_c * convolved).astype(bf16)
    own_cot = column_own(cotangent_sent)
    mixed, own_cot = lax.optimization_barrier((mixed, own_cot))
    column_cot = jnp.concatenate([own_cot, swapped(own_cot, "core")], 0)
    middle = resid + scattered_mp(dot(mixed, w_out, NT).astype(bf16))

    scale_two = lax.rsqrt(jnp.mean(middle * middle, axis=-1, keepdims=True) + norm_eps)
    unit_two = middle * scale_two
    normed_two = (unit_two * gains[1]).astype(bf16)
    own_mid = column_own(normed_two)
    grad_hidden = dot(column_cot, w_down, NN)
    own_mid, grad_hidden = lax.optimization_barrier((own_mid, grad_hidden))
    column_mid = jnp.concatenate([own_mid, swapped(own_mid, "core")], 0)
    gate_vals = dot(column_mid, w_gate_up, NN)
    gate, up = gate_vals[:, :wide], gate_vals[:, wide:]
    sigma = jax.nn.sigmoid(gate)
    swish = gate * sigma
    hidden = (swish * up).astype(bf16)
    grad_gate = grad_hidden * up * sigma * (1.0 + gate * (1.0 - sigma))
    grad_up = grad_hidden * swish
    grad_pair = jnp.concatenate([grad_gate.astype(bf16), grad_up.astype(bf16)], 1)
    own_pair, away_pair = jnp.split(grad_pair, 2, 0)
    away = dot(away_pair, w_gate_up, NT).astype(bf16)
    away, own_pair = lax.optimization_barrier((away, own_pair))
    summed, away = lax.optimization_barrier(
        (dot(own_pair, w_gate_up, NT), swapped(away, "core"))
    )
    summed = (summed + away.astype(f32)).astype(bf16)
    summed, grad_pair, hidden = lax.optimization_barrier((summed, grad_pair, hidden))
    grad_normed_two = summed_over(summed, RING, 4)
    grad_ff = jnp.concatenate(
        [dot(column_mid, grad_pair, TN).astype(bf16), dot(column_cot, hidden, TN).astype(bf16)], 1
    )
    grad_normed_two, grad_ff = lax.optimization_barrier((grad_normed_two, grad_ff))
    grad_ff = lax.psum_scatter(grad_ff, XY, scatter_dimension=0, tiled=True)

    gain_two_part = jnp.sum(grad_normed_two * unit_two, axis=0)
    grad_unit_two = grad_normed_two * gains[1]
    grad_middle = cotangent.astype(f32) + scale_two * (
        grad_unit_two - unit_two * jnp.mean(grad_unit_two * unit_two, axis=-1, keepdims=True)
    )

    group_back = gathered(grad_middle.astype(bf16), MP, 2)
    grad_mixed = dot(group_back, w_out, NN)
    grad_conv_out = grad_mixed * proj_c
    following = shifted(grad_conv_out[:2], DP, -1)
    grad_readout = (grad_mixed * convolved).astype(bf16)
    early = jnp.concatenate(
        [dot(group_in, grad_readout, TN).astype(bf16), dot(group_back, mixed, TN).astype(bf16)], 1
    )
    conv_part = jnp.stack(
        [
            jnp.sum(grad_conv_out * gated, axis=0),
            jnp.sum(grad_conv_out * one_back, axis=0),
            jnp.sum(grad_conv_out * two_back, axis=0),
        ]
    )
    following, early = lax.optimization_barrier((following, early))
    early = summed_over(early, "x", 4).astype(bf16)
    ahead = jnp.concatenate([grad_conv_out, following], 0)
    grad_gated = (
        conv_weight[0] * grad_conv_out
        + conv_weight[1] * ahead[1 : group_len + 1] * back_one
        + conv_weight[2] * ahead[2:] * back_two
    )
    grad_bx = jnp.concatenate(
        [(grad_gated * proj_x).astype(bf16), (grad_gated * proj_b).astype(bf16)], 1
    )
    late = dot(turned_in[lead:], grad_bx, TN).astype(bf16)
    late, grad_bx, hidden = lax.optimization_barrier((late, grad_bx, hidden))
    late = ring_summed(jnp.split(late, 4, 0), "y").astype(bf16)

    w_bx = rolled(w_bx, y).transpose(1, 0, 2, 3).reshape(D, 2 * chan_len)
    grad_normed_one = dot(grad_bx, w_bx, NT) + dot(grad_readout, w_c, NT)
    gain_one_part = jnp.sum(grad_normed_one * group_in.astype(f32), axis=0) / gains[0]
    early, late, gain_one_part = lax.optimization_barrier((early, late, gain_one_part))
    early = rolled(early.reshape(4, 2 * rows_len, 2 * chan_len), -y)
    early = ring_summed([early[r] for r in range(4)], "y")
    late = summed_over(late, "x", 4)
    grad_mix = jnp.concatenate([late, early], 1).astype(bf16)

    grad_normed_one = scattered_mp(grad_normed_one.astype(bf16))
    ff_out = dot(hidden, w_down, NT).astype(bf16)
    own, away = jnp.split(ff_out, 2, 0)
    ff_out = (own.astype(f32) + swapped(away, "core").astype(f32)).astype(bf16)
    ff_blocks = rolled(ff_out.reshape(4, tok_rows, D), -lax.axis_index(RING))
    block_out = (middle + ring_summed(ff_blocks, RING)).astype(bf16)
    grad_unit_one = grad_normed_one * gains[0]
    input_grad = grad_middle + scale_one * (
        grad_unit_one - unit_one * jnp.mean(grad_unit_one * unit_one, axis=-1, keepdims=True)
    )

    conv_full = lax.dynamic_update_slice(
        jnp.zeros((3, chan_len * 4), f32), conv_part, (jnp.int32(0), mp_index * chan_len)
    )
    small = jnp.concatenate([gain_one_part[None], gain_two_part[None], conv_full], 0)
    small = jnp.sum(lax.all_gather(small, COL, axis=0), axis=0)
    small, grad_mix = lax.optimization_barrier((small, grad_mix))
    small = jnp.sum(spread(small, XY, 16), axis=0)
    gain_sum, conv_sum = small[:2], small[2:]

    def both(block):
        pair = block.reshape(2, rows_len, -1)
        return pick(pair, zh), swapped(pick(pair, 1 - zh), "zh")

    own_ff, other_ff = both(grad_ff)
    grad_mix, other_ff = lax.optimization_barrier((grad_mix, other_ff))
    own, other = both(grad_mix)
    grad_mix = own.astype(f32) + other.astype(f32)
    order = (0, 2, 1, 3)
    grad_mix = [grad_mix[:, i * chan_len : (i + 1) * chan_len] for i in order]
    grad_in = jnp.stack(grad_mix[:3])
    grad_out = grad_mix[3].T
    grad_gate, grad_up, grad_down = (
        joined(own_ff[:, i * wide : i * wide + half], other_ff[:, i * wide : i * wide + half], 1)
        for i in range(3)
    )
    grad_gate_up = jnp.stack([grad_gate, grad_up]).astype(f32)
    grad_down = grad_down.astype(f32).T

    grad_taps = lax.dynamic_slice_in_dim(conv_sum, mp_index * chan_len, chan_len, 1)
    gains_set = adam(gains, gains_first, gains_second, gain_sum, 1.0, 0.0)
    conv_set = adam(conv_weight, conv_first, conv_second, grad_taps, 1.0, 0.0)
    in_set = adam(in_weight, in_first, in_second, grad_in, 2.0 * D ** (-0.5), weight_decay)
    out_set = adam(out_weight, out_first, out_second, grad_out, 2.0 * D ** (-0.5), weight_decay)
    gate_set = adam(
        gate_up, gate_up_first, gate_up_second, grad_gate_up, 2.0 * D ** (-0.5), weight_decay
    )
    down_set = adam(
        down_weight, down_first, down_second, grad_down, 2.0 * FF ** (-0.5), weight_decay
    )
    return (block_out, input_grad, *gains_set, *conv_set, *in_set, *out_set, *gate_set, *down_set)


def solution(mesh):
    parts = Mesh(mesh.devices.reshape(4, 4, 2, 2, 2), ("x", "y", "zh", "zl", "core"))
    tokens = P(DP + MP, None)
    taps = P(None, MP)
    wide_in = P(None, DP, MP)
    wide_out = P(MP, DP)
    in_specs = (
        (tokens,) * 2 + (P(),) * 4 + (taps,) * 3 + (wide_in,) * 3 + (wide_out,) * 3
        + (wide_in,) * 3 + (wide_out,) * 3
    )
    out_specs = (
        (tokens,) * 2 + (P(),) * 3 + (taps,) * 3 + (wide_in,) * 3 + (wide_out,) * 3
        + (wide_in,) * 3 + (wide_out,) * 3
    )
    return jax.shard_map(
        on_device, mesh=parts, in_specs=in_specs, out_specs=out_specs, check_vma=False
    )
```

```python
import jax
import jax.numpy as jnp
from jax import lax
from jax.sharding import Mesh
from jax.sharding import PartitionSpec as P

D = 1536
FF = 6912
STEP = 5

norm_eps = 1e-05
beta_one = 0.9
beta_two = 0.95
adam_eps = 1e-08
weight_decay = 0.1

bf16 = jnp.bfloat16
f32 = jnp.float32

XY = ("x", "y")
DP = ("x", "y", "zh")
MP = ("zl", "core")
RING = ("zh", "zl")
COL = ("zh", "zl", "core")


def positions(seq_lengths, first_row, count):
    ends = jnp.cumsum(seq_lengths)
    starts = ends - seq_lengths
    rows = first_row + jnp.arange(count, dtype=jnp.int32)
    covered = starts[None, :] <= rows[:, None]
    return rows - jnp.max(jnp.where(covered, starts[None, :], 0), axis=1)


def adam(weight, first, second, grad, rate, decay):
    first_new = beta_one * first + (1 - beta_one) * grad
    second_new = beta_two * second + (1 - beta_two) * grad * grad
    first_hat = first_new / (1 - beta_one**STEP)
    second_hat = second_new / (1 - beta_two**STEP)
    return (
        first_new,
        second_new,
        weight - rate * (first_hat / (jnp.sqrt(second_hat) + adam_eps) + decay * weight),
    )


def shifted(block, axes, distance):
    size = 1
    for axis in axes:
        size *= lax.axis_size(axis)
    route = [(i - distance, i) for i in range(size) if 0 <= i - distance < size]
    return lax.ppermute(block, axes, route)


def swapped(block, axis):
    return lax.ppermute(block, axis, [(0, 1), (1, 0)])


def exchanged(blocks, axes):
    return lax.all_to_all(blocks, axes, 0, 0, tiled=True)


def spread(block, axes, count):
    return exchanged(jnp.broadcast_to(block, (count, *block.shape)), axes)


def summed_over(block, axes, count):
    blocks = exchanged(block, axes).reshape(count, -1, *block.shape[1:])
    return jnp.sum(blocks.astype(f32), axis=0)


def from_others(blocks, axis):
    return [
        lax.ppermute(blocks[r], axis, [(i, (i + r) % 4) for i in range(4)]) for r in (1, 3, 2)
    ]


def ring_spread(block, axis):
    behind1, behind3, behind2 = from_others([block] * 4, axis)
    return jnp.stack([block, behind3, behind2, behind1])


def ring_summed(blocks, axis):
    total = blocks[0].astype(f32)
    for other in from_others(blocks, axis):
        total = total + other.astype(f32)
    return total


def rolled(blocks, shift):
    return jnp.stack([pick(blocks, (r - shift) % 4) for r in range(4)])


def gathered(block, axes, parts):
    width = block.shape[1] // parts
    return jnp.concatenate(
        [
            lax.all_gather(block[:, i * width : (i + 1) * width], axes, axis=0, tiled=True)
            for i in range(parts)
        ],
        axis=1,
    )


def column_own(block):
    return rolled(ring_spread(block, RING), lax.axis_index(RING)).reshape(-1, block.shape[1])


def pick(blocks, index, axis=0):
    return lax.dynamic_index_in_dim(blocks, index, axis, keepdims=False)


def scattered_mp(partial):
    core, place = lax.axis_index("core"), lax.axis_index("zl")
    blocks = partial.reshape(2, 2, -1, partial.shape[1])
    other = swapped(pick(blocks, 1 - core, 1), "core")
    summed = pick(blocks, core, 1).astype(f32) + other.astype(f32)
    other = swapped(pick(summed, 1 - place).astype(bf16), "zl")
    return pick(summed, place) + other.astype(f32)


def halves(block, width):
    low = lax.axis_index("zh") == 0
    first, last = block[..., :width], block[..., width:]
    return jnp.where(low, first, last), jnp.where(low, last, first)


def joined(own, other, axis):
    low = lax.axis_index("zh") == 0
    return jnp.where(
        low, jnp.concatenate([own, other], axis), jnp.concatenate([other, own], axis)
    )


def dot(left, right, dims):
    return lax.dot_general(left, right, ((dims[0], dims[1]), ((), ())), preferred_element_type=f32)


NN = ((1,), (0,))
NT = ((1,), (1,))
TN = ((0,), (0,))


def on_device(
    inputs,
    cotangent,
    seq_lengths,
    gains,
    gains_first,
    gains_second,
    conv_weight,
    conv_first,
    conv_second,
    in_weight,
    in_first,
    in_second,
    out_weight,
    out_first,
    out_second,
    gate_up,
    gate_up_first,
    gate_up_second,
    down_weight,
    down_first,
    down_second,
):
    tok_rows = inputs.shape[0]
    group_len = tok_rows * 4
    chan_len = conv_weight.shape[1]
    rows_len = in_weight.shape[1]
    half = gate_up.shape[2] // 2
    wide = -(-half // 128) * 128
    mp_index = lax.axis_index(MP)
    zh = lax.axis_index("zh")

    mix_rows = jnp.concatenate(
        [
            in_weight.astype(bf16).transpose(1, 0, 2).reshape(rows_len, 3 * chan_len),
            out_weight.astype(bf16).T,
        ],
        1,
    )

    def padded(block):
        return jnp.pad(block, ((0, 0), (0, wide - half)))

    own_down, away_down = halves(down_weight.astype(bf16).T, half)
    own = jnp.concatenate([mix_rows, padded(own_down)], 1)
    away = jnp.concatenate([mix_rows, padded(away_down)], 1)
    w_mix = lax.all_gather(joined(own, swapped(away, "zh"), 0), XY, axis=0, tiled=True)
    w_in, w_out = w_mix[:, : 3 * chan_len], w_mix[:, 3 * chan_len : 4 * chan_len]
    w_down = w_mix[:, 4 * chan_len :]
    own_gate, away_gate = halves(gate_up.astype(bf16), half)
    own, away = (jnp.concatenate([padded(g[0]), padded(g[1])], 1) for g in (own_gate, away_gate))
    w_gate_up = lax.all_gather(joined(own, swapped(away, "zh"), 0), XY, axis=0, tiled=True)

    first_row = lax.axis_index(DP) * group_len
    place = positions(seq_lengths, first_row, group_len + 2)
    fwd_one = (place[:group_len] >= 1).astype(f32)[:, None]
    fwd_two = (place[:group_len] >= 2).astype(f32)[:, None]
    back_one = (place[1 : group_len + 1] >= 1).astype(f32)[:, None]
    back_two = (place[2:] >= 2).astype(f32)[:, None]

    resid = inputs.astype(f32)
    scale_one = lax.rsqrt(jnp.mean(resid * resid, axis=-1, keepdims=True) + norm_eps)
    unit_one = resid * scale_one
    normed_one = (unit_one * gains[0]).astype(bf16)
    group_in = gathered(normed_one, MP, 2)
    lead = 16
    before = shifted(group_in[group_len - lead :], DP, 1)
    own_cot = column_own(cotangent)
    column_cot = jnp.concatenate([own_cot, swapped(own_cot, "core")], 0)
    column_cot, w_in = lax.optimization_barrier((column_cot, w_in))
    projected = dot(jnp.concatenate([before, group_in], 0), w_in, NN)
    proj_b = projected[lead:, :chan_len]
    proj_c = projected[lead:, chan_len : 2 * chan_len]
    proj_x = projected[lead:, 2 * chan_len :]
    extended = projected[:, :chan_len] * projected[:, 2 * chan_len :]
    gated = extended[lead:]
    one_back = extended[lead - 1 : lead - 1 + group_len] * fwd_one
    two_back = extended[lead - 2 : lead - 2 + group_len] * fwd_two
    convolved = conv_weight[0] * gated + conv_weight[1] * one_back + conv_weight[2] * two_back
    mixed = (proj_c * convolved).astype(bf16)
    middle = resid + scattered_mp(dot(mixed, w_out, NT).astype(bf16))
    grad_hidden = dot(column_cot, w_down, NN)
    middle, grad_hidden = lax.optimization_barrier((middle, grad_hidden))

    scale_two = lax.rsqrt(jnp.mean(middle * middle, axis=-1, keepdims=True) + norm_eps)
    unit_two = middle * scale_two
    normed_two = (unit_two * gains[1]).astype(bf16)
    own_mid = column_own(normed_two)
    column_mid = jnp.concatenate([own_mid, swapped(own_mid, "core")], 0)
    gate_vals = dot(column_mid, w_gate_up, NN)
    gate, up = gate_vals[:, :wide], gate_vals[:, wide:]
    sigma = jax.nn.sigmoid(gate)
    swish = gate * sigma
    hidden = (swish * up).astype(bf16)
    grad_gate = grad_hidden * up * sigma * (1.0 + gate * (1.0 - sigma))
    grad_up = grad_hidden * swish
    grad_pair = jnp.concatenate([grad_gate.astype(bf16), grad_up.astype(bf16)], 1)
    own_pair, away_pair = jnp.split(grad_pair, 2, 0)
    away = dot(away_pair, w_gate_up, NT).astype(bf16)
    away, own_pair = lax.optimization_barrier((away, own_pair))
    summed, away = lax.optimization_barrier(
        (dot(own_pair, w_gate_up, NT), swapped(away, "core"))
    )
    summed = (summed + away.astype(f32)).astype(bf16)
    summed, grad_pair, hidden = lax.optimization_barrier((summed, grad_pair, hidden))
    grad_normed_two = summed_over(summed, RING, 4)
    grad_ff = jnp.concatenate(
        [dot(column_mid, grad_pair, TN).astype(bf16), dot(column_cot, hidden, TN).astype(bf16)], 1
    )
    grad_normed_two, grad_ff = lax.optimization_barrier((grad_normed_two, grad_ff))
    grad_ff = lax.psum_scatter(grad_ff, XY, scatter_dimension=0, tiled=True)

    gain_two_part = jnp.sum(grad_normed_two * unit_two, axis=0)
    grad_unit_two = grad_normed_two * gains[1]
    grad_middle = cotangent.astype(f32) + scale_two * (
        grad_unit_two - unit_two * jnp.mean(grad_unit_two * unit_two, axis=-1, keepdims=True)
    )

    group_back = gathered(grad_middle.astype(bf16), MP, 2)
    grad_mixed = dot(group_back, w_out, NN)
    grad_conv_out = grad_mixed * proj_c
    following = shifted(grad_conv_out[:2], DP, -1)
    grad_readout = (grad_mixed * convolved).astype(bf16)
    grad_out = dot(group_back, mixed, TN).astype(bf16)
    conv_part = jnp.stack(
        [
            jnp.sum(grad_conv_out * gated, axis=0),
            jnp.sum(grad_conv_out * one_back, axis=0),
            jnp.sum(grad_conv_out * two_back, axis=0),
        ]
    )
    following, grad_out = lax.optimization_barrier((following, grad_out))
    ahead = jnp.concatenate([grad_conv_out, following], 0)
    grad_gated = (
        conv_weight[0] * grad_conv_out
        + conv_weight[1] * ahead[1 : group_len + 1] * back_one
        + conv_weight[2] * ahead[2:] * back_two
    )
    grad_proj = jnp.concatenate(
        [
            (grad_gated * proj_x).astype(bf16),
            grad_readout,
            (grad_gated * proj_b).astype(bf16),
        ],
        1,
    )
    grad_mix = jnp.concatenate([dot(group_in, grad_proj, TN).astype(bf16), grad_out], 1)
    grad_mix, grad_proj = lax.optimization_barrier((grad_mix, grad_proj))
    grad_mix = summed_over(grad_mix, DP, 32)
    grad_normed_one = dot(grad_proj, w_in, NT)
    gain_one_part = jnp.sum(grad_normed_one * group_in.astype(f32), axis=0) / gains[0]
    grad_normed_one = scattered_mp(grad_normed_one.astype(bf16))

    conv_full = lax.dynamic_update_slice(
        jnp.zeros((3, chan_len * 4), f32), conv_part, (jnp.int32(0), mp_index * chan_len)
    )
    small = jnp.concatenate([gain_one_part[None], gain_two_part[None], conv_full], 0)
    small = jnp.sum(lax.all_gather(small, COL, axis=0), axis=0)
    small, hidden = lax.optimization_barrier((small, hidden))
    small = jnp.sum(lax.all_gather(small, "x", axis=0), axis=0)
    small = jnp.sum(lax.all_gather(small, "y", axis=0), axis=0)
    gain_sum, conv_sum = small[:2], small[2:]

    ff_out = dot(hidden, w_down, NT).astype(bf16)
    own, away = jnp.split(ff_out, 2, 0)
    ff_out = (own.astype(f32) + swapped(away, "core").astype(f32)).astype(bf16)
    ff_blocks = rolled(ff_out.reshape(4, tok_rows, D), -lax.axis_index(RING))
    block_out = (middle + ring_summed(ff_blocks, RING)).astype(bf16)

    grad_unit_one = grad_normed_one * gains[0]
    input_grad = grad_middle + scale_one * (
        grad_unit_one - unit_one * jnp.mean(grad_unit_one * unit_one, axis=-1, keepdims=True)
    )

    def both(block):
        pair = block.reshape(2, rows_len, -1)
        return pick(pair, zh), swapped(pick(pair, 1 - zh), "zh")

    own_ff, other_ff = both(grad_ff)
    grad_in = jnp.stack([grad_mix[:, i * chan_len : (i + 1) * chan_len] for i in range(3)])
    grad_out = grad_mix[:, 3 * chan_len :].T
    grad_gate, grad_up, grad_down = (
        joined(own_ff[:, i * wide : i * wide + half], other_ff[:, i * wide : i * wide + half], 1)
        for i in range(3)
    )
    grad_gate_up = jnp.stack([grad_gate, grad_up]).astype(f32)
    grad_down = grad_down.astype(f32).T

    grad_taps = lax.dynamic_slice_in_dim(conv_sum, mp_index * chan_len, chan_len, 1)
    gains_set = adam(gains, gains_first, gains_second, gain_sum, 1.0, 0.0)
    conv_set = adam(conv_weight, conv_first, conv_second, grad_taps, 1.0, 0.0)
    in_set = adam(in_weight, in_first, in_second, grad_in, 2.0 * D ** (-0.5), weight_decay)
    out_set = adam(out_weight, out_first, out_second, grad_out, 2.0 * D ** (-0.5), weight_decay)
    gate_set = adam(
        gate_up, gate_up_first, gate_up_second, grad_gate_up, 2.0 * D ** (-0.5), weight_decay
    )
    down_set = adam(
        down_weight, down_first, down_second, grad_down, 2.0 * FF ** (-0.5), weight_decay
    )
    return (block_out, input_grad, *gains_set, *conv_set, *in_set, *out_set, *gate_set, *down_set)


def solution(mesh):
    parts = Mesh(mesh.devices.reshape(4, 4, 2, 2, 2), ("x", "y", "zh", "zl", "core"))
    tokens = P(DP + MP, None)
    taps = P(None, MP)
    wide_in = P(None, DP, MP)
    wide_out = P(MP, DP)
    in_specs = (
        (tokens,) * 2 + (P(),) * 4 + (taps,) * 3 + (wide_in,) * 3 + (wide_out,) * 3
        + (wide_in,) * 3 + (wide_out,) * 3
    )
    out_specs = (
        (tokens,) * 2 + (P(),) * 3 + (taps,) * 3 + (wide_in,) * 3 + (wide_out,) * 3
        + (wide_in,) * 3 + (wide_out,) * 3
    )
    return jax.shard_map(
        on_device, mesh=parts, in_specs=in_specs, out_specs=out_specs, check_vma=False
    )
```

```python
import jax
import jax.numpy as jnp
from jax import lax
from jax.experimental import pallas as pl
from jax.experimental.pallas import tpu as pltpu
from jax.sharding import Mesh
from jax.sharding import PartitionSpec as P

D = 1536
FF = 6912
STEP = 5

norm_eps = 1e-05
beta_one = 0.9
beta_two = 0.95
adam_eps = 1e-08
weight_decay = 0.1

bf16 = jnp.bfloat16
f32 = jnp.float32

XY = ("x", "y")
DP = ("x", "y", "zh")
MP = ("zl", "core")
RING = ("zh", "zl")
COL = ("zh", "zl", "core")


def positions(seq_lengths, first_row, count):
    ends = jnp.cumsum(seq_lengths)
    starts = ends - seq_lengths
    rows = first_row + jnp.arange(count, dtype=jnp.int32)
    covered = starts[None, :] <= rows[:, None]
    return rows - jnp.max(jnp.where(covered, starts[None, :], 0), axis=1)


def adam(weight, first, second, grad, rate, decay):
    first_new = beta_one * first + (1 - beta_one) * grad
    second_new = beta_two * second + (1 - beta_two) * grad * grad
    first_hat = first_new / (1 - beta_one**STEP)
    second_hat = second_new / (1 - beta_two**STEP)
    return (
        first_new,
        second_new,
        weight - rate * (first_hat / (jnp.sqrt(second_hat) + adam_eps) + decay * weight),
    )


def shifted(block, axes, distance):
    size = 1
    for axis in axes:
        size *= lax.axis_size(axis)
    route = [(i - distance, i) for i in range(size) if 0 <= i - distance < size]
    return lax.ppermute(block, axes, route)


def swapped(block, axis):
    return lax.ppermute(block, axis, [(0, 1), (1, 0)])


def exchanged(blocks, axes):
    return lax.all_to_all(blocks, axes, 0, 0, tiled=True)


def spread(block, axes, count):
    return exchanged(jnp.broadcast_to(block, (count, *block.shape)), axes)


def summed_over(block, axes, count):
    blocks = exchanged(block, axes).reshape(count, -1, *block.shape[1:])
    return jnp.sum(blocks.astype(f32), axis=0)


def from_others(blocks, axis):
    return [
        lax.ppermute(blocks[r], axis, [(i, (i + r) % 4) for i in range(4)]) for r in (1, 3, 2)
    ]


def ring_spread(block, axis):
    behind1, behind3, behind2 = from_others([block] * 4, axis)
    return jnp.stack([block, behind3, behind2, behind1])


def ring_summed(blocks, axis):
    total = blocks[0].astype(f32)
    for other in from_others(blocks, axis):
        total = total + other.astype(f32)
    return total


def rolled(blocks, shift):
    return jnp.stack([pick(blocks, (r - shift) % 4) for r in range(4)])


def gathered(block, axes, parts):
    width = block.shape[1] // parts
    return jnp.concatenate(
        [
            lax.all_gather(block[:, i * width : (i + 1) * width], axes, axis=0, tiled=True)
            for i in range(parts)
        ],
        axis=1,
    )


def column_own(block):
    return rolled(ring_spread(block, RING), lax.axis_index(RING)).reshape(-1, block.shape[1])


def small_sum(block):
    for axis, bit in (("core", 1), ("zl", 1), ("zh", 1), ("x", 1), ("x", 2), ("y", 1), ("y", 2)):
        route = [(i, i ^ bit) for i in range(lax.axis_size(axis))]
        block = block + lax.ppermute(block, axis, route)
    return block


def pick(blocks, index, axis=0):
    return lax.dynamic_index_in_dim(blocks, index, axis, keepdims=False)


def scattered_mp(partial):
    core, place = lax.axis_index("core"), lax.axis_index("zl")
    blocks = partial.reshape(2, 2, -1, partial.shape[1])
    other = swapped(pick(blocks, 1 - core, 1), "core")
    summed = pick(blocks, core, 1).astype(f32) + other.astype(f32)
    other = swapped(pick(summed, 1 - place).astype(bf16), "zl")
    return pick(summed, place) + other.astype(f32)


def halves(block, width):
    low = lax.axis_index("zh") == 0
    first, last = block[..., :width], block[..., width:]
    return jnp.where(low, first, last), jnp.where(low, last, first)


def joined(own, other, axis):
    low = lax.axis_index("zh") == 0
    return jnp.where(
        low, jnp.concatenate([own, other], axis), jnp.concatenate([other, own], axis)
    )


def dot(left, right, dims):
    return lax.dot_general(left, right, ((dims[0], dims[1]), ((), ())), preferred_element_type=f32)


NN = ((1,), (0,))
NT = ((1,), (1,))
TN = ((0,), (0,))


def weight_grads(pairs):
    rows, wide = pairs[0][0].shape
    step = 512
    ends = [0]
    for _, right in pairs:
        ends.append(ends[-1] + right.shape[1])
    count = len(pairs)

    def body(*refs):
        out = refs[2 * count]
        for i in range(count):
            left, right = refs[i][...], refs[count + i][...]
            out[:, ends[i] : ends[i + 1]] = dot(left, right, TN).astype(bf16)
        refs[2 * count + 1][...] = jnp.zeros((8, 128), f32)

    lefts = [pl.BlockSpec((rows, step), lambda i: (0, i)) for _ in pairs]
    rights = [pl.BlockSpec(right.shape, lambda i: (0, 0)) for _, right in pairs]
    return pl.pallas_call(
        body,
        grid=(wide // step,),
        in_specs=lefts + rights,
        out_specs=[
            pl.BlockSpec((step, ends[-1]), lambda i: (i, 0)),
            pl.BlockSpec((8, 128), lambda i: (0, 0)),
        ],
        out_shape=[
            jax.ShapeDtypeStruct((wide, ends[-1]), bf16),
            jax.ShapeDtypeStruct((8, 128), f32),
        ],
        compiler_params=pltpu.CompilerParams(vmem_limit_bytes=48 * 1024 * 1024),
        cost_estimate=pl.CostEstimate(
            flops=2 * rows * wide * ends[-1],
            bytes_accessed=2 * (count * rows * wide + (rows + wide) * ends[-1]),
            transcendentals=0,
        ),
    )(*[left for left, _ in pairs], *[right for _, right in pairs])


def on_device(
    inputs,
    cotangent,
    seq_lengths,
    gains,
    gains_first,
    gains_second,
    conv_weight,
    conv_first,
    conv_second,
    in_weight,
    in_first,
    in_second,
    out_weight,
    out_first,
    out_second,
    gate_up,
    gate_up_first,
    gate_up_second,
    down_weight,
    down_first,
    down_second,
):
    tok_rows = inputs.shape[0]
    group_len = tok_rows * 4
    chan_len = conv_weight.shape[1]
    rows_len = in_weight.shape[1]
    half = gate_up.shape[2] // 2
    wide = -(-half // 128) * 128
    mp_index = lax.axis_index(MP)
    zh = lax.axis_index("zh")

    mix_rows = jnp.concatenate(
        [
            in_weight.astype(bf16).transpose(1, 0, 2).reshape(rows_len, 3 * chan_len),
            out_weight.astype(bf16).T,
        ],
        1,
    )

    def padded(block):
        return jnp.pad(block, ((0, 0), (0, wide - half)))

    own_down, away_down = halves(down_weight.astype(bf16).T, half)
    own = jnp.concatenate([mix_rows, padded(own_down)], 1)
    away = jnp.concatenate([mix_rows, padded(away_down)], 1)
    w_mix = lax.all_gather(joined(own, swapped(away, "zh"), 0), XY, axis=0, tiled=True)
    w_in, w_out = w_mix[:, : 3 * chan_len], w_mix[:, 3 * chan_len : 4 * chan_len]
    w_down = w_mix[:, 4 * chan_len :]
    own_gate, away_gate = halves(gate_up.astype(bf16), half)
    own, away = (jnp.concatenate([padded(g[0]), padded(g[1])], 1) for g in (own_gate, away_gate))
    w_gate_up = lax.all_gather(joined(own, swapped(away, "zh"), 0), XY, axis=0, tiled=True)

    first_row = lax.axis_index(DP) * group_len
    place = positions(seq_lengths, first_row, group_len + 2)
    fwd_one = (place[:group_len] >= 1).astype(f32)[:, None]
    fwd_two = (place[:group_len] >= 2).astype(f32)[:, None]
    back_one = (place[1 : group_len + 1] >= 1).astype(f32)[:, None]
    back_two = (place[2:] >= 2).astype(f32)[:, None]

    resid = inputs.astype(f32)
    scale_one = lax.rsqrt(jnp.mean(resid * resid, axis=-1, keepdims=True) + norm_eps)
    unit_one = resid * scale_one
    normed_one = (unit_one * gains[0]).astype(bf16)
    group_in = gathered(normed_one, MP, 2)
    lead = 16
    before = shifted(group_in[group_len - lead :], DP, 1)
    own_cot = column_own(cotangent)
    column_cot = jnp.concatenate([own_cot, swapped(own_cot, "core")], 0)
    column_cot, w_in = lax.optimization_barrier((column_cot, w_in))
    projected = dot(jnp.concatenate([before, group_in], 0), w_in, NN)
    proj_b = projected[lead:, :chan_len]
    proj_c = projected[lead:, chan_len : 2 * chan_len]
    proj_x = projected[lead:, 2 * chan_len :]
    extended = projected[:, :chan_len] * projected[:, 2 * chan_len :]
    gated = extended[lead:]
    one_back = extended[lead - 1 : lead - 1 + group_len] * fwd_one
    two_back = extended[lead - 2 : lead - 2 + group_len] * fwd_two
    convolved = conv_weight[0] * gated + conv_weight[1] * one_back + conv_weight[2] * two_back
    mixed = (proj_c * convolved).astype(bf16)
    middle = resid + scattered_mp(dot(mixed, w_out, NT).astype(bf16))
    grad_hidden = dot(column_cot, w_down, NN)
    middle, grad_hidden = lax.optimization_barrier((middle, grad_hidden))

    scale_two = lax.rsqrt(jnp.mean(middle * middle, axis=-1, keepdims=True) + norm_eps)
    unit_two = middle * scale_two
    normed_two = (unit_two * gains[1]).astype(bf16)
    own_mid = column_own(normed_two)
    column_mid = jnp.concatenate([own_mid, swapped(own_mid, "core")], 0)
    gate_vals = dot(column_mid, w_gate_up, NN)
    gate, up = gate_vals[:, :wide], gate_vals[:, wide:]
    sigma = jax.nn.sigmoid(gate)
    swish = gate * sigma
    hidden = (swish * up).astype(bf16)
    grad_gate = grad_hidden * up * sigma * (1.0 + gate * (1.0 - sigma))
    grad_up = grad_hidden * swish
    grad_pair = jnp.concatenate([grad_gate.astype(bf16), grad_up.astype(bf16)], 1)
    own_pair, away_pair = jnp.split(grad_pair, 2, 0)
    away = dot(away_pair, w_gate_up, NT).astype(bf16)
    away, own_pair = lax.optimization_barrier((away, own_pair))
    summed, away = lax.optimization_barrier(
        (dot(own_pair, w_gate_up, NT), swapped(away, "core"))
    )
    summed = (summed + away.astype(f32)).astype(bf16)
    summed, grad_pair, hidden = lax.optimization_barrier((summed, grad_pair, hidden))
    grad_normed_two = summed_over(summed, RING, 4)
    grad_ff, _ = weight_grads([(column_mid, grad_pair), (column_cot, hidden)])
    grad_normed_two, grad_ff = lax.optimization_barrier((grad_normed_two, grad_ff))
    grad_ff = lax.psum_scatter(grad_ff, XY, scatter_dimension=0, tiled=True)

    gain_two_part = jnp.sum(grad_normed_two * unit_two, axis=0)
    grad_unit_two = grad_normed_two * gains[1]
    grad_middle = cotangent.astype(f32) + scale_two * (
        grad_unit_two - unit_two * jnp.mean(grad_unit_two * unit_two, axis=-1, keepdims=True)
    )

    group_back = gathered(grad_middle.astype(bf16), MP, 2)
    grad_mixed = dot(group_back, w_out, NN)
    grad_conv_out = grad_mixed * proj_c
    following = shifted(grad_conv_out[:2], DP, -1)
    grad_readout = (grad_mixed * convolved).astype(bf16)
    conv_part = jnp.stack(
        [
            jnp.sum(grad_conv_out * gated, axis=0),
            jnp.sum(grad_conv_out * one_back, axis=0),
            jnp.sum(grad_conv_out * two_back, axis=0),
        ]
    )
    ahead = jnp.concatenate([grad_conv_out, following], 0)
    grad_gated = (
        conv_weight[0] * grad_conv_out
        + conv_weight[1] * ahead[1 : group_len + 1] * back_one
        + conv_weight[2] * ahead[2:] * back_two
    )
    grad_proj = jnp.concatenate(
        [
            (grad_gated * proj_x).astype(bf16),
            grad_readout,
            (grad_gated * proj_b).astype(bf16),
        ],
        1,
    )
    grad_mix, zero = weight_grads([(group_in, grad_proj), (group_back, mixed)])
    grad_proj, zero = lax.optimization_barrier((grad_proj, zero))
    grad_mix = summed_over(grad_mix, XY, 16)
    grad_normed_one = dot(grad_proj, w_in, NT)
    gain_one_part = jnp.sum(grad_normed_one * group_in.astype(f32), axis=0) / gains[0]
    grad_normed_one = scattered_mp(grad_normed_one.astype(bf16))

    conv_full = lax.dynamic_update_slice(
        jnp.zeros((3, chan_len * 4), f32), conv_part, (jnp.int32(0), mp_index * chan_len)
    )
    small = jnp.concatenate([gain_one_part[None], gain_two_part[None], conv_full], 0)
    small = small + zero[:1, :1]
    small = small_sum(small)
    gain_sum, conv_sum = small[:2], small[2:]

    ff_out = dot(hidden, w_down, NT).astype(bf16)
    own, away = jnp.split(ff_out, 2, 0)
    ff_out = (own.astype(f32) + swapped(away, "core").astype(f32)).astype(bf16)
    ff_blocks = rolled(ff_out.reshape(4, tok_rows, D), -lax.axis_index(RING))
    block_out = (middle + ring_summed(ff_blocks, RING)).astype(bf16)

    grad_unit_one = grad_normed_one * gains[0]
    input_grad = grad_middle + scale_one * (
        grad_unit_one - unit_one * jnp.mean(grad_unit_one * unit_one, axis=-1, keepdims=True)
    )

    def both(block):
        pair = block.reshape(2, rows_len, -1)
        return pick(pair, zh), swapped(pick(pair, 1 - zh), "zh")

    own_ff, other_ff = both(grad_ff)
    other_ff, grad_mix = lax.optimization_barrier((other_ff, grad_mix))
    own, other = both(grad_mix.astype(bf16))
    grad_mix = own.astype(f32) + other.astype(f32)
    grad_in = jnp.stack([grad_mix[:, i * chan_len : (i + 1) * chan_len] for i in range(3)])
    grad_out = grad_mix[:, 3 * chan_len :].T
    grad_gate, grad_up, grad_down = (
        joined(own_ff[:, i * wide : i * wide + half], other_ff[:, i * wide : i * wide + half], 1)
        for i in range(3)
    )
    grad_gate_up = jnp.stack([grad_gate, grad_up]).astype(f32)
    grad_down = grad_down.astype(f32).T

    grad_taps = lax.dynamic_slice_in_dim(conv_sum, mp_index * chan_len, chan_len, 1)
    gains_set = adam(gains, gains_first, gains_second, gain_sum, 1.0, 0.0)
    conv_set = adam(conv_weight, conv_first, conv_second, grad_taps, 1.0, 0.0)
    in_set = adam(in_weight, in_first, in_second, grad_in, 2.0 * D ** (-0.5), weight_decay)
    out_set = adam(out_weight, out_first, out_second, grad_out, 2.0 * D ** (-0.5), weight_decay)
    gate_set = adam(
        gate_up, gate_up_first, gate_up_second, grad_gate_up, 2.0 * D ** (-0.5), weight_decay
    )
    down_set = adam(
        down_weight, down_first, down_second, grad_down, 2.0 * FF ** (-0.5), weight_decay
    )
    return (block_out, input_grad, *gains_set, *conv_set, *in_set, *out_set, *gate_set, *down_set)


def solution(mesh):
    parts = Mesh(mesh.devices.reshape(4, 4, 2, 2, 2), ("x", "y", "zh", "zl", "core"))
    tokens = P(DP + MP, None)
    taps = P(None, MP)
    wide_in = P(None, DP, MP)
    wide_out = P(MP, DP)
    in_specs = (
        (tokens,) * 2 + (P(),) * 4 + (taps,) * 3 + (wide_in,) * 3 + (wide_out,) * 3
        + (wide_in,) * 3 + (wide_out,) * 3
    )
    out_specs = (
        (tokens,) * 2 + (P(),) * 3 + (taps,) * 3 + (wide_in,) * 3 + (wide_out,) * 3
        + (wide_in,) * 3 + (wide_out,) * 3
    )
    return jax.shard_map(
        on_device, mesh=parts, in_specs=in_specs, out_specs=out_specs, check_vma=False
    )
```

```python
import jax
import jax.numpy as jnp
from jax import lax
from jax.experimental import pallas as pl
from jax.experimental.pallas import tpu as pltpu
from jax.sharding import Mesh
from jax.sharding import PartitionSpec as P

D = 1536
FF = 6912
STEP = 5

norm_eps = 1e-05
beta_one = 0.9
beta_two = 0.95
adam_eps = 1e-08
weight_decay = 0.1

bf16 = jnp.bfloat16
f32 = jnp.float32

XY = ("x", "y")
DP = ("x", "y", "zh")
MP = ("zl", "core")
RING = ("zh", "zl")
COL = ("zh", "zl", "core")


def positions(seq_lengths, first_row, count):
    ends = jnp.cumsum(seq_lengths)
    starts = ends - seq_lengths
    rows = first_row + jnp.arange(count, dtype=jnp.int32)
    covered = starts[None, :] <= rows[:, None]
    return rows - jnp.max(jnp.where(covered, starts[None, :], 0), axis=1)


def adam(weight, first, second, grad, rate, decay):
    first_new = beta_one * first + (1 - beta_one) * grad
    second_new = beta_two * second + (1 - beta_two) * grad * grad
    first_hat = first_new / (1 - beta_one**STEP)
    second_hat = second_new / (1 - beta_two**STEP)
    return (
        first_new,
        second_new,
        weight - rate * (first_hat / (jnp.sqrt(second_hat) + adam_eps) + decay * weight),
    )


def shifted(block, axes, distance):
    size = 1
    for axis in axes:
        size *= lax.axis_size(axis)
    route = [(i - distance, i) for i in range(size) if 0 <= i - distance < size]
    return lax.ppermute(block, axes, route)


def swapped(block, axis):
    return lax.ppermute(block, axis, [(0, 1), (1, 0)])


def exchanged(blocks, axes):
    return lax.all_to_all(blocks, axes, 0, 0, tiled=True)


def spread(block, axes, count):
    return exchanged(jnp.broadcast_to(block, (count, *block.shape)), axes)


def summed_over(block, axes, count):
    blocks = exchanged(block, axes).reshape(count, -1, *block.shape[1:])
    return jnp.sum(blocks.astype(f32), axis=0)


def from_others(blocks, axis):
    return [
        lax.ppermute(blocks[r], axis, [(i, (i + r) % 4) for i in range(4)]) for r in (1, 3, 2)
    ]


def ring_spread(block, axis):
    behind1, behind3, behind2 = from_others([block] * 4, axis)
    return jnp.stack([block, behind3, behind2, behind1])


def ring_summed(blocks, axis):
    total = blocks[0].astype(f32)
    for other in from_others(blocks, axis):
        total = total + other.astype(f32)
    return total


def rolled(blocks, shift):
    return jnp.stack([pick(blocks, (r - shift) % 4) for r in range(4)])


def gathered(block, axes, parts):
    width = block.shape[1] // parts
    return jnp.concatenate(
        [
            lax.all_gather(block[:, i * width : (i + 1) * width], axes, axis=0, tiled=True)
            for i in range(parts)
        ],
        axis=1,
    )


def column_own(block):
    return rolled(ring_spread(block, RING), lax.axis_index(RING)).reshape(-1, block.shape[1])


def small_sum(block):
    for axis, bit in (("core", 1), ("zl", 1), ("zh", 1), ("x", 1), ("x", 2), ("y", 1), ("y", 2)):
        route = [(i, i ^ bit) for i in range(lax.axis_size(axis))]
        block = block + lax.ppermute(block, axis, route)
    return block


def pick(blocks, index, axis=0):
    return lax.dynamic_index_in_dim(blocks, index, axis, keepdims=False)


def scattered_mp(partial):
    core, place = lax.axis_index("core"), lax.axis_index("zl")
    blocks = partial.reshape(2, 2, -1, partial.shape[1])
    other = swapped(pick(blocks, 1 - core, 1), "core")
    summed = pick(blocks, core, 1).astype(f32) + other.astype(f32)
    other = swapped(pick(summed, 1 - place).astype(bf16), "zl")
    return pick(summed, place) + other.astype(f32)


def halves(block, width):
    low = lax.axis_index("zh") == 0
    first, last = block[..., :width], block[..., width:]
    return jnp.where(low, first, last), jnp.where(low, last, first)


def joined(own, other, axis):
    low = lax.axis_index("zh") == 0
    return jnp.where(
        low, jnp.concatenate([own, other], axis), jnp.concatenate([other, own], axis)
    )


def dot(left, right, dims):
    return lax.dot_general(left, right, ((dims[0], dims[1]), ((), ())), preferred_element_type=f32)


NN = ((1,), (0,))
NT = ((1,), (1,))
TN = ((0,), (0,))


def kernel_costs(rows, wide, columns):
    return dict(
        compiler_params=pltpu.CompilerParams(vmem_limit_bytes=48 * 1024 * 1024),
        cost_estimate=pl.CostEstimate(
            flops=2 * rows * wide * columns,
            bytes_accessed=2 * (rows * wide + (rows + wide) * columns),
            transcendentals=0,
        ),
    )


def weight_grad(left, right, columns, start):
    rows, wide = left.shape
    step, width = (wide, 256) if start else (512, right.shape[1])

    def body(left_ref, right_ref, out_ref, turned):
        @pl.when(pl.program_id(1) == 0)
        def _():
            turned[...] = left_ref[...].T

        out_ref[...] = dot(turned[...], right_ref[...], NN).astype(bf16)

    return pl.pallas_call(
        body,
        grid=(wide // step, right.shape[1] // width),
        in_specs=[
            pl.BlockSpec((rows, step), lambda i, j: (0, i)),
            pl.BlockSpec((rows, width), lambda i, j: (0, j)),
        ],
        out_specs=pl.BlockSpec((step, width), lambda i, j: (i, start // width + j)),
        out_shape=jax.ShapeDtypeStruct((wide, columns), bf16),
        scratch_shapes=[pltpu.VMEM((step, rows), bf16)],
        **kernel_costs(rows, wide, right.shape[1]),
    )(left, right)


def mixer_grads(room, group_in, grad_proj, group_back, mixed):
    rows, wide = group_in.shape
    step, split = 512, grad_proj.shape[1]
    columns = split + mixed.shape[1]

    def body(_, in_ref, proj_ref, back_ref, mixed_ref, out_ref):
        out_ref[:, :split] = dot(in_ref[...], proj_ref[...], TN).astype(bf16)
        out_ref[:, split:] = dot(back_ref[...], mixed_ref[...], TN).astype(bf16)

    left = pl.BlockSpec((rows, step), lambda i: (0, i))
    return pl.pallas_call(
        body,
        grid=(wide // step,),
        in_specs=[
            pl.BlockSpec(memory_space=pl.ANY),
            left,
            pl.BlockSpec(grad_proj.shape, lambda i: (0, 0)),
            left,
            pl.BlockSpec(mixed.shape, lambda i: (0, 0)),
        ],
        out_specs=pl.BlockSpec((step, columns), lambda i: (i, 0)),
        out_shape=jax.ShapeDtypeStruct(room.shape, bf16),
        input_output_aliases={0: 0},
        **kernel_costs(rows, wide, columns),
    )(room, group_in, grad_proj, group_back, mixed)


def on_device(
    inputs,
    cotangent,
    seq_lengths,
    gains,
    gains_first,
    gains_second,
    conv_weight,
    conv_first,
    conv_second,
    in_weight,
    in_first,
    in_second,
    out_weight,
    out_first,
    out_second,
    gate_up,
    gate_up_first,
    gate_up_second,
    down_weight,
    down_first,
    down_second,
):
    tok_rows = inputs.shape[0]
    group_len = tok_rows * 4
    chan_len = conv_weight.shape[1]
    rows_len = in_weight.shape[1]
    half = gate_up.shape[2] // 2
    wide = -(-half // 128) * 128
    mp_index = lax.axis_index(MP)
    zh = lax.axis_index("zh")

    mix_rows = jnp.concatenate(
        [
            in_weight.astype(bf16).transpose(1, 0, 2).reshape(rows_len, 3 * chan_len),
            out_weight.astype(bf16).T,
        ],
        1,
    )

    def padded(block):
        return jnp.pad(block, ((0, 0), (0, wide - half)))

    own_down, away_down = halves(down_weight.astype(bf16).T, half)
    own = jnp.concatenate([mix_rows, padded(own_down)], 1)
    away = jnp.concatenate([mix_rows, padded(away_down)], 1)
    w_mix = lax.all_gather(joined(own, swapped(away, "zh"), 0), XY, axis=0, tiled=True)
    w_in, w_out = w_mix[:, : 3 * chan_len], w_mix[:, 3 * chan_len : 4 * chan_len]
    w_down = w_mix[:, 4 * chan_len :]
    own_gate, away_gate = halves(gate_up.astype(bf16), half)
    own, away = (jnp.concatenate([padded(g[0]), padded(g[1])], 1) for g in (own_gate, away_gate))
    w_gate_up = lax.all_gather(joined(own, swapped(away, "zh"), 0), XY, axis=0, tiled=True)

    first_row = lax.axis_index(DP) * group_len
    place = positions(seq_lengths, first_row, group_len + 2)
    fwd_one = (place[:group_len] >= 1).astype(f32)[:, None]
    fwd_two = (place[:group_len] >= 2).astype(f32)[:, None]
    back_one = (place[1 : group_len + 1] >= 1).astype(f32)[:, None]
    back_two = (place[2:] >= 2).astype(f32)[:, None]

    resid = inputs.astype(f32)
    scale_one = lax.rsqrt(jnp.mean(resid * resid, axis=-1, keepdims=True) + norm_eps)
    unit_one = resid * scale_one
    normed_one = (unit_one * gains[0]).astype(bf16)
    group_in = gathered(normed_one, MP, 2)
    lead = 16
    before = shifted(group_in[group_len - lead :], DP, 1)
    own_cot = column_own(cotangent)
    column_cot = jnp.concatenate([own_cot, swapped(own_cot, "core")], 0)
    column_cot, w_in = lax.optimization_barrier((column_cot, w_in))
    projected = dot(jnp.concatenate([before, group_in], 0), w_in, NN)
    proj_b = projected[lead:, :chan_len]
    proj_c = projected[lead:, chan_len : 2 * chan_len]
    proj_x = projected[lead:, 2 * chan_len :]
    extended = projected[:, :chan_len] * projected[:, 2 * chan_len :]
    gated = extended[lead:]
    one_back = extended[lead - 1 : lead - 1 + group_len] * fwd_one
    two_back = extended[lead - 2 : lead - 2 + group_len] * fwd_two
    convolved = conv_weight[0] * gated + conv_weight[1] * one_back + conv_weight[2] * two_back
    mixed = (proj_c * convolved).astype(bf16)
    middle = resid + scattered_mp(dot(mixed, w_out, NT).astype(bf16))
    grad_hidden = dot(column_cot, w_down, NN)
    middle, grad_hidden = lax.optimization_barrier((middle, grad_hidden))

    scale_two = lax.rsqrt(jnp.mean(middle * middle, axis=-1, keepdims=True) + norm_eps)
    unit_two = middle * scale_two
    normed_two = (unit_two * gains[1]).astype(bf16)
    own_mid = column_own(normed_two)
    column_mid = jnp.concatenate([own_mid, swapped(own_mid, "core")], 0)
    gate_vals = dot(column_mid, w_gate_up, NN)
    gate, up = gate_vals[:, :wide], gate_vals[:, wide:]
    sigma = jax.nn.sigmoid(gate)
    swish = gate * sigma
    hidden = (swish * up).astype(bf16)
    grad_gate = grad_hidden * up * sigma * (1.0 + gate * (1.0 - sigma))
    grad_up = grad_hidden * swish
    grad_pair = jnp.concatenate([grad_gate.astype(bf16), grad_up.astype(bf16)], 1)
    own_pair, away_pair = jnp.split(grad_pair, 2, 0)
    away = dot(away_pair, w_gate_up, NT).astype(bf16)
    away, own_pair = lax.optimization_barrier((away, own_pair))
    summed, away = lax.optimization_barrier(
        (dot(own_pair, w_gate_up, NT), swapped(away, "core"))
    )
    summed = (summed + away.astype(f32)).astype(bf16)
    summed, grad_pair, hidden = lax.optimization_barrier((summed, grad_pair, hidden))
    grad_normed_two = summed_over(summed, RING, 4)
    mix_cols = 4 * chan_len
    room = weight_grad(column_mid, grad_pair, mix_cols + 2 * wide, mix_cols)
    grad_down = weight_grad(column_cot, hidden, wide, 0)
    grad_normed_two, room, grad_down = lax.optimization_barrier(
        (grad_normed_two, room, grad_down)
    )
    grad_down = summed_over(grad_down, XY, 16)

    gain_two_part = jnp.sum(grad_normed_two * unit_two, axis=0)
    grad_unit_two = grad_normed_two * gains[1]
    grad_middle = cotangent.astype(f32) + scale_two * (
        grad_unit_two - unit_two * jnp.mean(grad_unit_two * unit_two, axis=-1, keepdims=True)
    )

    group_back = gathered(grad_middle.astype(bf16), MP, 2)
    grad_mixed = dot(group_back, w_out, NN)
    grad_conv_out = grad_mixed * proj_c
    following = shifted(grad_conv_out[:2], DP, -1)
    grad_readout = (grad_mixed * convolved).astype(bf16)
    conv_part = jnp.stack(
        [
            jnp.sum(grad_conv_out * gated, axis=0),
            jnp.sum(grad_conv_out * one_back, axis=0),
            jnp.sum(grad_conv_out * two_back, axis=0),
        ]
    )
    ahead = jnp.concatenate([grad_conv_out, following], 0)
    grad_gated = (
        conv_weight[0] * grad_conv_out
        + conv_weight[1] * ahead[1 : group_len + 1] * back_one
        + conv_weight[2] * ahead[2:] * back_two
    )
    grad_proj = jnp.concatenate(
        [
            (grad_gated * proj_x).astype(bf16),
            grad_readout,
            (grad_gated * proj_b).astype(bf16),
        ],
        1,
    )
    grad_down, mixed = lax.optimization_barrier((grad_down, mixed))
    grad_all = mixer_grads(room, group_in, grad_proj, group_back, mixed)
    grad_all = lax.psum_scatter(grad_all, XY, scatter_dimension=0, tiled=True)
    grad_normed_one = dot(grad_proj, w_in, NT)
    gain_one_part = jnp.sum(grad_normed_one * group_in.astype(f32), axis=0) / gains[0]
    grad_normed_one = scattered_mp(grad_normed_one.astype(bf16))

    conv_full = lax.dynamic_update_slice(
        jnp.zeros((3, chan_len * 4), f32), conv_part, (jnp.int32(0), mp_index * chan_len)
    )
    small = jnp.concatenate([gain_one_part[None], gain_two_part[None], conv_full], 0)
    small = small_sum(small)
    gain_sum, conv_sum = small[:2], small[2:]

    ff_out = dot(hidden, w_down, NT).astype(bf16)
    own, away = jnp.split(ff_out, 2, 0)
    ff_out = (own.astype(f32) + swapped(away, "core").astype(f32)).astype(bf16)
    ff_blocks = rolled(ff_out.reshape(4, tok_rows, D), -lax.axis_index(RING))
    block_out = (middle + ring_summed(ff_blocks, RING)).astype(bf16)

    grad_unit_one = grad_normed_one * gains[0]
    input_grad = grad_middle + scale_one * (
        grad_unit_one - unit_one * jnp.mean(grad_unit_one * unit_one, axis=-1, keepdims=True)
    )

    def both(block):
        pair = block.reshape(2, rows_len, -1)
        return pick(pair, zh), swapped(pick(pair, 1 - zh), "zh")

    def spliced(own, other, start):
        return joined(own[:, start : start + half], other[:, start : start + half], 1)

    own, other = both(grad_down.astype(bf16))
    grad_down = spliced(own, other, 0).astype(f32).T
    own, other = both(grad_all)
    grad_gate_up = jnp.stack(
        [spliced(own, other, mix_cols), spliced(own, other, mix_cols + wide)]
    ).astype(f32)
    grad_mix = own[:, :mix_cols].astype(f32) + other[:, :mix_cols].astype(f32)
    grad_in = jnp.stack([grad_mix[:, i * chan_len : (i + 1) * chan_len] for i in range(3)])
    grad_out = grad_mix[:, 3 * chan_len :].T

    grad_taps = lax.dynamic_slice_in_dim(conv_sum, mp_index * chan_len, chan_len, 1)
    gains_set = adam(gains, gains_first, gains_second, gain_sum, 1.0, 0.0)
    conv_set = adam(conv_weight, conv_first, conv_second, grad_taps, 1.0, 0.0)
    in_set = adam(in_weight, in_first, in_second, grad_in, 2.0 * D ** (-0.5), weight_decay)
    out_set = adam(out_weight, out_first, out_second, grad_out, 2.0 * D ** (-0.5), weight_decay)
    gate_set = adam(
        gate_up, gate_up_first, gate_up_second, grad_gate_up, 2.0 * D ** (-0.5), weight_decay
    )
    down_set = adam(
        down_weight, down_first, down_second, grad_down, 2.0 * FF ** (-0.5), weight_decay
    )
    return (block_out, input_grad, *gains_set, *conv_set, *in_set, *out_set, *gate_set, *down_set)


def solution(mesh):
    parts = Mesh(mesh.devices.reshape(4, 4, 2, 2, 2), ("x", "y", "zh", "zl", "core"))
    tokens = P(DP + MP, None)
    taps = P(None, MP)
    wide_in = P(None, DP, MP)
    wide_out = P(MP, DP)
    in_specs = (
        (tokens,) * 2 + (P(),) * 4 + (taps,) * 3 + (wide_in,) * 3 + (wide_out,) * 3
        + (wide_in,) * 3 + (wide_out,) * 3
    )
    out_specs = (
        (tokens,) * 2 + (P(),) * 3 + (taps,) * 3 + (wide_in,) * 3 + (wide_out,) * 3
        + (wide_in,) * 3 + (wide_out,) * 3
    )
    return jax.shard_map(
        on_device, mesh=parts, in_specs=in_specs, out_specs=out_specs, check_vma=False
    )
```

```python
import jax
import jax.numpy as jnp
from jax import lax
from jax.experimental import pallas as pl
from jax.experimental.pallas import tpu as pltpu
from jax.sharding import Mesh
from jax.sharding import PartitionSpec as P

D = 1536
FF = 6912
STEP = 5

norm_eps = 1e-05
beta_one = 0.9
beta_two = 0.95
adam_eps = 1e-08
weight_decay = 0.1

bf16 = jnp.bfloat16
f32 = jnp.float32

XY = ("x", "y")
DP = ("x", "y", "zh")
MP = ("zl", "core")
RING = ("zh", "zl")
COL = ("zh", "zl", "core")


def positions(seq_lengths, first_row, count):
    ends = jnp.cumsum(seq_lengths)
    starts = ends - seq_lengths
    rows = first_row + jnp.arange(count, dtype=jnp.int32)
    covered = starts[None, :] <= rows[:, None]
    return rows - jnp.max(jnp.where(covered, starts[None, :], 0), axis=1)


def adam(weight, first, second, grad, rate, decay):
    first_new = beta_one * first + (1 - beta_one) * grad
    second_new = beta_two * second + (1 - beta_two) * grad * grad
    first_hat = first_new / (1 - beta_one**STEP)
    second_hat = second_new / (1 - beta_two**STEP)
    return (
        first_new,
        second_new,
        weight - rate * (first_hat / (jnp.sqrt(second_hat) + adam_eps) + decay * weight),
    )


def shifted(block, axes, distance):
    size = 1
    for axis in axes:
        size *= lax.axis_size(axis)
    route = [(i - distance, i) for i in range(size) if 0 <= i - distance < size]
    return lax.ppermute(block, axes, route)


def swapped(block, axis):
    return lax.ppermute(block, axis, [(0, 1), (1, 0)])


def exchanged(blocks, axes):
    return lax.all_to_all(blocks, axes, 0, 0, tiled=True)


def spread(block, axes, count):
    return exchanged(jnp.broadcast_to(block, (count, *block.shape)), axes)


def summed_over(block, axes, count):
    blocks = exchanged(block, axes).reshape(count, -1, *block.shape[1:])
    return jnp.sum(blocks.astype(f32), axis=0)


def from_others(blocks, axis):
    return [
        lax.ppermute(blocks[r], axis, [(i, (i + r) % 4) for i in range(4)]) for r in (1, 3, 2)
    ]


def ring_spread(block, axis):
    behind1, behind3, behind2 = from_others([block] * 4, axis)
    return jnp.stack([block, behind3, behind2, behind1])


def ring_summed(blocks, axis):
    total = blocks[0].astype(f32)
    for other in from_others(blocks, axis):
        total = total + other.astype(f32)
    return total


def rolled(blocks, shift):
    return jnp.stack([pick(blocks, (r - shift) % 4) for r in range(4)])


def gathered(block, axes, parts):
    width = block.shape[1] // parts
    return jnp.concatenate(
        [
            lax.all_gather(block[:, i * width : (i + 1) * width], axes, axis=0, tiled=True)
            for i in range(parts)
        ],
        axis=1,
    )


def column_own(block):
    return rolled(ring_spread(block, RING), lax.axis_index(RING)).reshape(-1, block.shape[1])


def group_gathered(block):
    own = lax.all_gather(block, "zl", axis=0)
    other = swapped(own, "core")
    first = lax.axis_index("core") == 0
    rows = jnp.where(first, jnp.stack([own, other], 1), jnp.stack([other, own], 1))
    return rows.reshape(-1, block.shape[1])


def small_sum(block):
    for axis, bit in (("core", 1), ("zl", 1), ("zh", 1), ("x", 1), ("x", 2), ("y", 1), ("y", 2)):
        route = [(i, i ^ bit) for i in range(lax.axis_size(axis))]
        block = block + lax.ppermute(block, axis, route)
    return block


def pick(blocks, index, axis=0):
    return lax.dynamic_index_in_dim(blocks, index, axis, keepdims=False)


def scattered_mp(partial):
    core, place = lax.axis_index("core"), lax.axis_index("zl")
    blocks = partial.reshape(2, 2, -1, partial.shape[1])
    other = swapped(pick(blocks, 1 - core, 1), "core")
    summed = pick(blocks, core, 1).astype(f32) + other.astype(f32)
    other = swapped(pick(summed, 1 - place).astype(bf16), "zl")
    return pick(summed, place) + other.astype(f32)


def halves(block, width):
    low = lax.axis_index("zh") == 0
    first, last = block[..., :width], block[..., width:]
    return jnp.where(low, first, last), jnp.where(low, last, first)


def joined(own, other, axis):
    low = lax.axis_index("zh") == 0
    return jnp.where(
        low, jnp.concatenate([own, other], axis), jnp.concatenate([other, own], axis)
    )


def dot(left, right, dims):
    return lax.dot_general(left, right, ((dims[0], dims[1]), ((), ())), preferred_element_type=f32)


NN = ((1,), (0,))
NT = ((1,), (1,))
TN = ((0,), (0,))


def weight_grads(pairs, columns, start, room=None):
    rows, wide = pairs[0][0].shape
    step = 512
    ends = [0]
    for _, right in pairs:
        ends.append(ends[-1] + right.shape[1])
    count = len(pairs)
    kept = [] if room is None else [room]

    def body(*refs):
        refs = refs[len(kept) :]
        for i in range(count):
            product = dot(refs[i][...], refs[count + i][...], TN)
            refs[-1][:, ends[i] : ends[i + 1]] = product.astype(bf16)

    lefts = [pl.BlockSpec((rows, step), lambda i: (0, i)) for _ in pairs]
    rights = [pl.BlockSpec(right.shape, lambda i: (0, 0)) for _, right in pairs]
    return pl.pallas_call(
        body,
        grid=(wide // step,),
        in_specs=[pl.BlockSpec(memory_space=pl.ANY)] * len(kept) + lefts + rights,
        out_specs=pl.BlockSpec(
            (pl.Element(step), pl.Element(ends[-1])), lambda i: (i * step, start)
        ),
        out_shape=jax.ShapeDtypeStruct((wide, columns), bf16),
        input_output_aliases={0: 0} if kept else {},
        compiler_params=pltpu.CompilerParams(vmem_limit_bytes=48 * 1024 * 1024),
        cost_estimate=pl.CostEstimate(
            flops=2 * rows * wide * ends[-1],
            bytes_accessed=2 * (count * rows * wide + (rows + wide) * ends[-1]),
            transcendentals=0,
        ),
    )(*kept, *[left for left, _ in pairs], *[right for _, right in pairs])


def on_device(
    inputs,
    cotangent,
    seq_lengths,
    gains,
    gains_first,
    gains_second,
    conv_weight,
    conv_first,
    conv_second,
    in_weight,
    in_first,
    in_second,
    out_weight,
    out_first,
    out_second,
    gate_up,
    gate_up_first,
    gate_up_second,
    down_weight,
    down_first,
    down_second,
):
    tok_rows = inputs.shape[0]
    group_len = tok_rows * 4
    chan_len = conv_weight.shape[1]
    rows_len = in_weight.shape[1]
    half = gate_up.shape[2] // 2
    wide = -(-half // 128) * 128
    mp_index = lax.axis_index(MP)
    zh = lax.axis_index("zh")

    mix_rows = jnp.concatenate(
        [
            in_weight.astype(bf16).transpose(1, 0, 2).reshape(rows_len, 3 * chan_len),
            out_weight.astype(bf16).T,
        ],
        1,
    )

    def padded(block):
        return jnp.pad(block, ((0, 0), (0, wide - half)))

    own_down, away_down = halves(down_weight.astype(bf16).T, half)
    own = jnp.concatenate([mix_rows, padded(own_down)], 1)
    away = jnp.concatenate([mix_rows, padded(away_down)], 1)
    w_mix = lax.all_gather(joined(own, swapped(away, "zh"), 0), XY, axis=0, tiled=True)
    w_in, w_out = w_mix[:, : 3 * chan_len], w_mix[:, 3 * chan_len : 4 * chan_len]
    w_down = w_mix[:, 4 * chan_len :]
    own_gate, away_gate = halves(gate_up.astype(bf16), half)
    own, away = (jnp.concatenate([padded(g[0]), padded(g[1])], 1) for g in (own_gate, away_gate))
    w_gate_up = lax.all_gather(joined(own, swapped(away, "zh"), 0), XY, axis=0, tiled=True)

    first_row = lax.axis_index(DP) * group_len
    place = positions(seq_lengths, first_row, group_len + 2)
    fwd_one = (place[:group_len] >= 1).astype(f32)[:, None]
    fwd_two = (place[:group_len] >= 2).astype(f32)[:, None]
    back_one = (place[1 : group_len + 1] >= 1).astype(f32)[:, None]
    back_two = (place[2:] >= 2).astype(f32)[:, None]

    resid = inputs.astype(f32)
    scale_one = lax.rsqrt(jnp.mean(resid * resid, axis=-1, keepdims=True) + norm_eps)
    unit_one = resid * scale_one
    normed_one = (unit_one * gains[0]).astype(bf16)
    group_in = gathered(normed_one, MP, 2)
    lead = 16
    before = shifted(group_in[group_len - lead :], DP, 1)
    own_cot = column_own(cotangent)
    column_cot = jnp.concatenate([own_cot, swapped(own_cot, "core")], 0)
    column_cot, w_in = lax.optimization_barrier((column_cot, w_in))
    projected = dot(jnp.concatenate([before, group_in], 0), w_in, NN)
    proj_b = projected[lead:, :chan_len]
    proj_c = projected[lead:, chan_len : 2 * chan_len]
    proj_x = projected[lead:, 2 * chan_len :]
    extended = projected[:, :chan_len] * projected[:, 2 * chan_len :]
    gated = extended[lead:]
    one_back = extended[lead - 1 : lead - 1 + group_len] * fwd_one
    two_back = extended[lead - 2 : lead - 2 + group_len] * fwd_two
    convolved = conv_weight[0] * gated + conv_weight[1] * one_back + conv_weight[2] * two_back
    mixed = (proj_c * convolved).astype(bf16)
    middle = resid + scattered_mp(dot(mixed, w_out, NT).astype(bf16))
    grad_hidden = dot(column_cot, w_down, NN)
    middle, grad_hidden = lax.optimization_barrier((middle, grad_hidden))

    scale_two = lax.rsqrt(jnp.mean(middle * middle, axis=-1, keepdims=True) + norm_eps)
    unit_two = middle * scale_two
    normed_two = (unit_two * gains[1]).astype(bf16)
    own_mid = column_own(normed_two)
    column_mid = jnp.concatenate([own_mid, swapped(own_mid, "core")], 0)
    gate_vals = dot(column_mid, w_gate_up, NN)
    gate, up = gate_vals[:, :wide], gate_vals[:, wide:]
    sigma = jax.nn.sigmoid(gate)
    swish = gate * sigma
    hidden = (swish * up).astype(bf16)
    grad_gate = grad_hidden * up * sigma * (1.0 + gate * (1.0 - sigma))
    grad_up = grad_hidden * swish
    grad_pair = jnp.concatenate([grad_gate.astype(bf16), grad_up.astype(bf16)], 1)
    own_pair, away_pair = jnp.split(grad_pair, 2, 0)
    away = dot(away_pair, w_gate_up, NT).astype(bf16)
    away, own_pair = lax.optimization_barrier((away, own_pair))
    summed, away = lax.optimization_barrier(
        (dot(own_pair, w_gate_up, NT), swapped(away, "core"))
    )
    summed = (summed + away.astype(f32)).astype(bf16)
    summed, grad_pair, hidden = lax.optimization_barrier((summed, grad_pair, hidden))
    grad_normed_two = summed_over(summed, RING, 4)
    mix_cols = 4 * chan_len
    columns = mix_cols + 3 * wide
    grads = weight_grads([(column_mid, grad_pair), (column_cot, hidden)], columns, mix_cols)
    grad_normed_two, grads = lax.optimization_barrier((grad_normed_two, grads))

    gain_two_part = jnp.sum(grad_normed_two * unit_two, axis=0)
    grad_unit_two = grad_normed_two * gains[1]
    grad_middle = cotangent.astype(f32) + scale_two * (
        grad_unit_two - unit_two * jnp.mean(grad_unit_two * unit_two, axis=-1, keepdims=True)
    )

    group_back = group_gathered(grad_middle.astype(bf16))
    grad_mixed = dot(group_back, w_out, NN)
    grad_conv_out = grad_mixed * proj_c
    following = shifted(grad_conv_out[:2], DP, -1)
    grad_readout = (grad_mixed * convolved).astype(bf16)
    grads = weight_grads(
        [(group_in, grad_readout), (group_back, mixed)], columns, 0, grads
    )
    conv_part = jnp.stack(
        [
            jnp.sum(grad_conv_out * gated, axis=0),
            jnp.sum(grad_conv_out * one_back, axis=0),
            jnp.sum(grad_conv_out * two_back, axis=0),
        ]
    )
    ahead = jnp.concatenate([grad_conv_out, following], 0)
    grad_gated = (
        conv_weight[0] * grad_conv_out
        + conv_weight[1] * ahead[1 : group_len + 1] * back_one
        + conv_weight[2] * ahead[2:] * back_two
    )
    grad_proj = jnp.concatenate(
        [
            (grad_gated * proj_x).astype(bf16),
            grad_readout,
            (grad_gated * proj_b).astype(bf16),
        ],
        1,
    )
    split = jnp.concatenate([grad_proj[:, :chan_len], grad_proj[:, 2 * chan_len :]], 1)
    grads = weight_grads([(group_in, split)], columns, 2 * chan_len, grads)
    grads = lax.psum_scatter(grads, XY, scatter_dimension=0, tiled=True)
    grad_normed_one = dot(grad_proj, w_in, NT)
    gain_one_part = jnp.sum(grad_normed_one * group_in.astype(f32), axis=0) / gains[0]
    grad_normed_one = scattered_mp(grad_normed_one.astype(bf16))

    conv_full = lax.dynamic_update_slice(
        jnp.zeros((3, chan_len * 4), f32), conv_part, (jnp.int32(0), mp_index * chan_len)
    )
    small = jnp.concatenate([gain_one_part[None], gain_two_part[None], conv_full], 0)
    small = small_sum(small)
    gain_sum, conv_sum = small[:2], small[2:]

    ff_out = dot(hidden, w_down, NT).astype(bf16)
    own, away = jnp.split(ff_out, 2, 0)
    ff_out = (own.astype(f32) + swapped(away, "core").astype(f32)).astype(bf16)
    ff_blocks = rolled(ff_out.reshape(4, tok_rows, D), -lax.axis_index(RING))
    block_out = (middle + ring_summed(ff_blocks, RING)).astype(bf16)

    grad_unit_one = grad_normed_one * gains[0]
    input_grad = grad_middle + scale_one * (
        grad_unit_one - unit_one * jnp.mean(grad_unit_one * unit_one, axis=-1, keepdims=True)
    )

    def both(block):
        pair = block.reshape(2, rows_len, -1)
        return pick(pair, zh), swapped(pick(pair, 1 - zh), "zh")

    def spliced(own, other, start):
        return joined(own[:, start : start + half], other[:, start : start + half], 1)

    own, other = both(grads)
    grad_gate, grad_up, grad_down = (spliced(own, other, mix_cols + i * wide) for i in range(3))
    grad_gate_up = jnp.stack([grad_gate, grad_up]).astype(f32)
    grad_down = grad_down.astype(f32).T
    grad_mix = own[:, :mix_cols].astype(f32) + other[:, :mix_cols].astype(f32)
    grad_mix = [grad_mix[:, i * chan_len : (i + 1) * chan_len] for i in range(4)]
    grad_in = jnp.stack([grad_mix[2], grad_mix[0], grad_mix[3]])
    grad_out = grad_mix[1].T

    grad_taps = lax.dynamic_slice_in_dim(conv_sum, mp_index * chan_len, chan_len, 1)
    gains_set = adam(gains, gains_first, gains_second, gain_sum, 1.0, 0.0)
    conv_set = adam(conv_weight, conv_first, conv_second, grad_taps, 1.0, 0.0)
    in_set = adam(in_weight, in_first, in_second, grad_in, 2.0 * D ** (-0.5), weight_decay)
    out_set = adam(out_weight, out_first, out_second, grad_out, 2.0 * D ** (-0.5), weight_decay)
    gate_set = adam(
        gate_up, gate_up_first, gate_up_second, grad_gate_up, 2.0 * D ** (-0.5), weight_decay
    )
    down_set = adam(
        down_weight, down_first, down_second, grad_down, 2.0 * FF ** (-0.5), weight_decay
    )
    return (block_out, input_grad, *gains_set, *conv_set, *in_set, *out_set, *gate_set, *down_set)


def solution(mesh):
    parts = Mesh(mesh.devices.reshape(4, 4, 2, 2, 2), ("x", "y", "zh", "zl", "core"))
    tokens = P(DP + MP, None)
    taps = P(None, MP)
    wide_in = P(None, DP, MP)
    wide_out = P(MP, DP)
    in_specs = (
        (tokens,) * 2 + (P(),) * 4 + (taps,) * 3 + (wide_in,) * 3 + (wide_out,) * 3
        + (wide_in,) * 3 + (wide_out,) * 3
    )
    out_specs = (
        (tokens,) * 2 + (P(),) * 3 + (taps,) * 3 + (wide_in,) * 3 + (wide_out,) * 3
        + (wide_in,) * 3 + (wide_out,) * 3
    )
    return jax.shard_map(
        on_device, mesh=parts, in_specs=in_specs, out_specs=out_specs, check_vma=False
    )
```

```python
import jax
import jax.numpy as jnp
from jax import lax
from jax.experimental import pallas as pl
from jax.experimental.pallas import tpu as pltpu
from jax.sharding import Mesh
from jax.sharding import PartitionSpec as P

D = 1536
FF = 6912
STEP = 5

norm_eps = 1e-05
beta_one = 0.9
beta_two = 0.95
adam_eps = 1e-08
weight_decay = 0.1

bf16 = jnp.bfloat16
f32 = jnp.float32

XY = ("x", "y")
DP = ("x", "y", "zh")
MP = ("zl", "core")
RING = ("zh", "zl")
COL = ("zh", "zl", "core")


def positions(seq_lengths, first_row, count):
    ends = jnp.cumsum(seq_lengths)
    starts = ends - seq_lengths
    rows = first_row + jnp.arange(count, dtype=jnp.int32)
    covered = starts[None, :] <= rows[:, None]
    return rows - jnp.max(jnp.where(covered, starts[None, :], 0), axis=1)


def adam(weight, first, second, grad, rate, decay):
    first_new = beta_one * first + (1 - beta_one) * grad
    second_new = beta_two * second + (1 - beta_two) * grad * grad
    first_hat = first_new / (1 - beta_one**STEP)
    second_hat = second_new / (1 - beta_two**STEP)
    return (
        first_new,
        second_new,
        weight - rate * (first_hat / (jnp.sqrt(second_hat) + adam_eps) + decay * weight),
    )


def shifted(block, axes, distance):
    size = 1
    for axis in axes:
        size *= lax.axis_size(axis)
    route = [(i - distance, i) for i in range(size) if 0 <= i - distance < size]
    return lax.ppermute(block, axes, route)


def swapped(block, axis):
    return lax.ppermute(block, axis, [(0, 1), (1, 0)])


def exchanged(blocks, axes):
    return lax.all_to_all(blocks, axes, 0, 0, tiled=True)


def spread(block, axes, count):
    return exchanged(jnp.broadcast_to(block, (count, *block.shape)), axes)


def summed_over(block, axes, count):
    blocks = exchanged(block, axes).reshape(count, -1, *block.shape[1:])
    return jnp.sum(blocks.astype(f32), axis=0)


def from_others(blocks, axis):
    return [
        lax.ppermute(blocks[r], axis, [(i, (i + r) % 4) for i in range(4)]) for r in (1, 3, 2)
    ]


def ring_spread(block, axis):
    behind1, behind3, behind2 = from_others([block] * 4, axis)
    return jnp.stack([block, behind3, behind2, behind1])


def ring_summed(blocks, axis):
    total = blocks[0].astype(f32)
    for other in from_others(blocks, axis):
        total = total + other.astype(f32)
    return total


def rolled(blocks, shift):
    return jnp.stack([pick(blocks, (r - shift) % 4) for r in range(4)])


def column_own(block):
    return rolled(ring_spread(block, RING), lax.axis_index(RING)).reshape(-1, block.shape[1])


def column_summed(rows):
    return ring_summed(rolled(rows.reshape(4, -1, rows.shape[1]), -lax.axis_index(RING)), RING)


def by_place(own, other):
    own, other = (rows.reshape(4, -1, rows.shape[1]) for rows in (own, other))
    first = lax.axis_index("core") == 0
    rows = jnp.where(first, jnp.stack([own, other], 1), jnp.stack([other, own], 1))
    return rows.reshape(-1, own.shape[2])


def by_core(rows):
    core = lax.axis_index("core")
    blocks = rows.reshape(4, 2, -1, rows.shape[1])
    return tuple(pick(blocks, c, 1).reshape(-1, rows.shape[1]) for c in (core, 1 - core))


def core_summed(left, right, dims):
    away = dot(left[1], right, dims).astype(bf16)
    away, own = lax.optimization_barrier((away, left[0]))
    own, away = lax.optimization_barrier((dot(own, right, dims), swapped(away, "core")))
    return (own + away.astype(f32)).astype(bf16)


def paired_sum(block, steps):
    for axis, bit in steps:
        route = [(i, i ^ bit) for i in range(lax.axis_size(axis))]
        block = block + lax.ppermute(block, axis, route)
    return block


def pick(blocks, index, axis=0):
    return lax.dynamic_index_in_dim(blocks, index, axis, keepdims=False)


def halves(block, width):
    low = lax.axis_index("zh") == 0
    first, last = block[..., :width], block[..., width:]
    return jnp.where(low, first, last), jnp.where(low, last, first)


def joined(own, other, axis):
    low = lax.axis_index("zh") == 0
    return jnp.where(
        low, jnp.concatenate([own, other], axis), jnp.concatenate([other, own], axis)
    )


def dot(left, right, dims):
    return lax.dot_general(left, right, ((dims[0], dims[1]), ((), ())), preferred_element_type=f32)


NN = ((1,), (0,))
NT = ((1,), (1,))
TN = ((0,), (0,))


def weight_grads(groups):
    rows, wide = groups[0][0][0].shape
    step = 512
    terms = [term for group in groups for term in group]
    count = len(terms)
    columns = sum(group[0][1].shape[1] for group in groups)

    def body(*refs):
        at, products = 0, []
        for group in groups:
            total = None
            for _ in group:
                product = dot(refs[at][...], refs[count + at][...], TN)
                total = product if total is None else total + product
                at += 1
            products.append(total.astype(bf16))
        refs[-1][...] = jnp.concatenate(products, 1)

    lefts = [pl.BlockSpec((left.shape[0], step), lambda i: (0, i)) for left, _ in terms]
    rights = [pl.BlockSpec(right.shape, lambda i: (0, 0)) for _, right in terms]
    return pl.pallas_call(
        body,
        grid=(wide // step,),
        in_specs=lefts + rights,
        out_specs=pl.BlockSpec((step, columns), lambda i: (i, 0)),
        out_shape=jax.ShapeDtypeStruct((wide, columns), bf16),
        compiler_params=pltpu.CompilerParams(vmem_limit_bytes=48 * 1024 * 1024),
        cost_estimate=pl.CostEstimate(
            flops=2 * sum(left.shape[0] * right.shape[1] for left, right in terms) * wide,
            bytes_accessed=2 * (len(terms) * rows * wide + (rows + wide) * columns),
            transcendentals=0,
        ),
    )(*[left for left, _ in terms], *[right for _, right in terms])


def on_device(
    inputs,
    cotangent,
    seq_lengths,
    gains,
    gains_first,
    gains_second,
    conv_weight,
    conv_first,
    conv_second,
    in_weight,
    in_first,
    in_second,
    out_weight,
    out_first,
    out_second,
    gate_up,
    gate_up_first,
    gate_up_second,
    down_weight,
    down_first,
    down_second,
):
    tok_rows = inputs.shape[0]
    group_len = tok_rows * 8
    chan_len = conv_weight.shape[1] // 2
    rows_len = in_weight.shape[1]
    half = gate_up.shape[2] // 2
    wide = -(-half // 128) * 128
    mp_index = lax.axis_index(MP)
    zh = lax.axis_index("zh")

    resid = inputs.astype(f32)
    scale_one = lax.rsqrt(jnp.mean(resid * resid, axis=-1, keepdims=True) + norm_eps)
    unit_one = resid * scale_one
    normed_one = (unit_one * gains[0]).astype(bf16)

    def padded(block):
        return jnp.pad(block, ((0, 0), (0, wide - half)))

    own_in, away_in = halves(in_weight.astype(bf16), chan_len)
    own_out, away_out = halves(out_weight.astype(bf16).T, chan_len)
    own_down, away_down = halves(down_weight.astype(bf16).T, half)
    own, away = (
        jnp.concatenate([i[0], i[1], i[2], o, padded(d)], 1)
        for i, o, d in ((own_in, own_out, own_down), (away_in, away_out, away_down))
    )
    w_mix = lax.all_gather(joined(own, swapped(away, "zh"), 0), XY, axis=0, tiled=True)
    mix_cols = 4 * chan_len
    w_in, w_out = w_mix[:, : 3 * chan_len], w_mix[:, 3 * chan_len : mix_cols]
    w_down = w_mix[:, mix_cols:]
    own_gate, away_gate = halves(gate_up.astype(bf16), half)
    own, away = (jnp.concatenate([padded(g[0]), padded(g[1])], 1) for g in (own_gate, away_gate))
    w_gate_up = lax.all_gather(joined(own, swapped(away, "zh"), 0), XY, axis=0, tiled=True)

    first_row = lax.axis_index(XY) * group_len
    place = positions(seq_lengths, first_row, group_len + 2)
    fwd_one = (place[:group_len] >= 1).astype(f32)[:, None]
    fwd_two = (place[:group_len] >= 2).astype(f32)[:, None]
    back_one = (place[1 : group_len + 1] >= 1).astype(f32)[:, None]
    back_two = (place[2:] >= 2).astype(f32)[:, None]

    own_rows = column_own(normed_one)
    group_in = by_place(own_rows, swapped(own_rows, "core"))
    lead = 16
    before = shifted(group_in[group_len - lead :], XY, 1)
    own_cot = column_own(cotangent)
    column_cot = jnp.concatenate([own_cot, swapped(own_cot, "core")], 0)
    column_cot, w_in = lax.optimization_barrier((column_cot, w_in))
    taps = halves(conv_weight, chan_len)[0]
    projected = dot(jnp.concatenate([before, group_in], 0), w_in, NN)
    proj_b = projected[lead:, :chan_len]
    proj_c = projected[lead:, chan_len : 2 * chan_len]
    proj_x = projected[lead:, 2 * chan_len :]
    extended = projected[:, :chan_len] * projected[:, 2 * chan_len :]
    gated = extended[lead:]
    one_back = extended[lead - 1 : lead - 1 + group_len] * fwd_one
    two_back = extended[lead - 2 : lead - 2 + group_len] * fwd_two
    convolved = taps[0] * gated + taps[1] * one_back + taps[2] * two_back
    mixed = by_core((proj_c * convolved).astype(bf16))
    middle = resid + summed_over(core_summed(mixed, w_out, NT), RING, 4)
    grad_hidden = dot(column_cot, w_down, NN)
    middle, grad_hidden = lax.optimization_barrier((middle, grad_hidden))

    scale_two = lax.rsqrt(jnp.mean(middle * middle, axis=-1, keepdims=True) + norm_eps)
    unit_two = middle * scale_two
    normed_two = (unit_two * gains[1]).astype(bf16)
    own_mid = column_own(normed_two)
    column_mid = jnp.concatenate([own_mid, swapped(own_mid, "core")], 0)
    gate_vals = dot(column_mid, w_gate_up, NN)
    gate, up = gate_vals[:, :wide], gate_vals[:, wide:]
    sigma = jax.nn.sigmoid(gate)
    swish = gate * sigma
    hidden = (swish * up).astype(bf16)
    grad_gate = grad_hidden * up * sigma * (1.0 + gate * (1.0 - sigma))
    grad_up = grad_hidden * swish
    grad_pair = jnp.concatenate([grad_gate.astype(bf16), grad_up.astype(bf16)], 1)
    summed = core_summed(jnp.split(grad_pair, 2, 0), w_gate_up, NT)
    summed, grad_pair, hidden = lax.optimization_barrier((summed, grad_pair, hidden))
    grad_normed_two = summed_over(summed, RING, 4)
    grad_ff = weight_grads([[(column_mid, grad_pair)], [(column_cot, hidden)]])
    grad_normed_two, grad_ff = lax.optimization_barrier((grad_normed_two, grad_ff))
    grad_ff = lax.psum_scatter(grad_ff, XY, scatter_dimension=0, tiled=True)

    gain_two_part = jnp.sum(grad_normed_two * unit_two, axis=0)
    grad_unit_two = grad_normed_two * gains[1]
    grad_middle = cotangent.astype(f32) + scale_two * (
        grad_unit_two - unit_two * jnp.mean(grad_unit_two * unit_two, axis=-1, keepdims=True)
    )

    own_back = column_own(grad_middle.astype(bf16))
    ff_out = dot(hidden, w_down, NT).astype(bf16)
    own_back, ff_out = lax.optimization_barrier((own_back, ff_out))
    other_back = swapped(own_back, "core")
    grad_mixed = by_place(dot(own_back, w_out, NN), dot(other_back, w_out, NN))
    grad_conv_out = grad_mixed * proj_c
    following = shifted(grad_conv_out[:2], XY, -1)
    grad_readout = (grad_mixed * convolved).astype(bf16)
    conv_part = jnp.stack(
        [
            jnp.sum(grad_conv_out * gated, axis=0),
            jnp.sum(grad_conv_out * one_back, axis=0),
            jnp.sum(grad_conv_out * two_back, axis=0),
        ]
    )
    ahead = jnp.concatenate([grad_conv_out, following], 0)
    grad_gated = (
        taps[0] * grad_conv_out
        + taps[1] * ahead[1 : group_len + 1] * back_one
        + taps[2] * ahead[2:] * back_two
    )
    grad_proj = jnp.concatenate(
        [
            (grad_gated * proj_x).astype(bf16),
            grad_readout,
            (grad_gated * proj_b).astype(bf16),
        ],
        1,
    )
    grad_mix = weight_grads(
        [[(group_in, grad_proj)], [(own_back, mixed[0]), (other_back, mixed[1])]]
    )
    grad_mix, grad_proj = lax.optimization_barrier((grad_mix, grad_proj))
    grad_mix = summed_over(grad_mix, XY, 16).astype(bf16)
    grad_normed_one = dot(grad_proj, w_in, NT)
    gain_one_part = jnp.sum(grad_normed_one * group_in.astype(f32), axis=0) / gains[0]
    own, away = by_core(grad_normed_one.astype(bf16))
    own = (own.astype(f32) + swapped(away, "core").astype(f32)).astype(bf16)
    grad_normed_one = column_summed(own)

    conv_full = lax.dynamic_update_slice(
        jnp.zeros((3, D), f32), conv_part, (jnp.int32(0), (2 * mp_index + zh) * chan_len)
    )
    small = jnp.concatenate([gain_one_part[None], gain_two_part[None], conv_full], 0)
    small = paired_sum(small, (("core", 1), ("zl", 1), ("zh", 1)))
    small, grad_mix = lax.optimization_barrier((small, grad_mix))
    small = jnp.sum(spread(small, XY, 16), axis=0)
    gain_sum, conv_sum = small[:2], small[2:]

    own, away = jnp.split(ff_out, 2, 0)
    ff_out = (own.astype(f32) + swapped(away, "core").astype(f32)).astype(bf16)
    block_out = (middle + column_summed(ff_out)).astype(bf16)

    grad_unit_one = grad_normed_one * gains[0]
    input_grad = grad_middle + scale_one * (
        grad_unit_one - unit_one * jnp.mean(grad_unit_one * unit_one, axis=-1, keepdims=True)
    )

    def both(block):
        pair = block.reshape(2, rows_len, -1)
        return pick(pair, zh), swapped(pick(pair, 1 - zh), "zh")

    def spliced(pair, start, width):
        own, other = (block[:, start : start + width] for block in pair)
        return joined(own, other, 1).astype(f32)

    pair = both(grad_mix)
    grad_in = jnp.stack([spliced(pair, i * chan_len, chan_len) for i in range(3)])
    grad_out = spliced(pair, 3 * chan_len, chan_len).T
    pair = both(grad_ff)
    grad_gate_up = jnp.stack([spliced(pair, i * wide, half) for i in range(2)])
    grad_down = spliced(pair, 2 * wide, half).T

    grad_taps = lax.dynamic_slice_in_dim(conv_sum, mp_index * 2 * chan_len, 2 * chan_len, 1)
    gains_set = adam(gains, gains_first, gains_second, gain_sum, 1.0, 0.0)
    conv_set = adam(conv_weight, conv_first, conv_second, grad_taps, 1.0, 0.0)
    in_set = adam(in_weight, in_first, in_second, grad_in, 2.0 * D ** (-0.5), weight_decay)
    out_set = adam(out_weight, out_first, out_second, grad_out, 2.0 * D ** (-0.5), weight_decay)
    gate_set = adam(
        gate_up, gate_up_first, gate_up_second, grad_gate_up, 2.0 * D ** (-0.5), weight_decay
    )
    down_set = adam(
        down_weight, down_first, down_second, grad_down, 2.0 * FF ** (-0.5), weight_decay
    )
    return (block_out, input_grad, *gains_set, *conv_set, *in_set, *out_set, *gate_set, *down_set)


def solution(mesh):
    parts = Mesh(mesh.devices.reshape(4, 4, 2, 2, 2), ("x", "y", "zh", "zl", "core"))
    tokens = P(DP + MP, None)
    taps = P(None, MP)
    wide_in = P(None, DP, MP)
    wide_out = P(MP, DP)
    in_specs = (
        (tokens,) * 2 + (P(),) * 4 + (taps,) * 3 + (wide_in,) * 3 + (wide_out,) * 3
        + (wide_in,) * 3 + (wide_out,) * 3
    )
    out_specs = (
        (tokens,) * 2 + (P(),) * 3 + (taps,) * 3 + (wide_in,) * 3 + (wide_out,) * 3
        + (wide_in,) * 3 + (wide_out,) * 3
    )
    return jax.shard_map(
        on_device, mesh=parts, in_specs=in_specs, out_specs=out_specs, check_vma=False
    )
```

```python
import jax
import jax.numpy as jnp
from jax import lax
from jax.experimental import pallas as pl
from jax.experimental.pallas import tpu as pltpu
from jax.sharding import Mesh
from jax.sharding import PartitionSpec as P

D = 1536
FF = 6912
STEP = 5

norm_eps = 1e-05
beta_one = 0.9
beta_two = 0.95
adam_eps = 1e-08
weight_decay = 0.1

bf16 = jnp.bfloat16
f32 = jnp.float32

XY = ("x", "y")
DP = ("x", "y", "zh")
MP = ("zl", "core")
RING = ("zh", "zl")
COL = ("zh", "zl", "core")


def positions(seq_lengths, first_row, count):
    ends = jnp.cumsum(seq_lengths)
    starts = ends - seq_lengths
    rows = first_row + jnp.arange(count, dtype=jnp.int32)
    covered = starts[None, :] <= rows[:, None]
    return rows - jnp.max(jnp.where(covered, starts[None, :], 0), axis=1)


def adam(weight, first, second, grad, rate, decay):
    first_new = beta_one * first + (1 - beta_one) * grad
    second_new = beta_two * second + (1 - beta_two) * grad * grad
    first_hat = first_new / (1 - beta_one**STEP)
    second_hat = second_new / (1 - beta_two**STEP)
    return (
        first_new,
        second_new,
        weight - rate * (first_hat / (jnp.sqrt(second_hat) + adam_eps) + decay * weight),
    )


def shifted(block, axes, distance):
    size = 1
    for axis in axes:
        size *= lax.axis_size(axis)
    route = [(i - distance, i) for i in range(size) if 0 <= i - distance < size]
    return lax.ppermute(block, axes, route)


def swapped(block, axis):
    return lax.ppermute(block, axis, [(0, 1), (1, 0)])


def exchanged(blocks, axes):
    return lax.all_to_all(blocks, axes, 0, 0, tiled=True)


def spread(block, axes, count):
    return exchanged(jnp.broadcast_to(block, (count, *block.shape)), axes)


def summed_over(block, axes, count):
    blocks = exchanged(block, axes).reshape(count, -1, *block.shape[1:])
    return jnp.sum(blocks.astype(f32), axis=0)


def from_others(blocks, axis):
    return [
        lax.ppermute(blocks[r], axis, [(i, (i + r) % 4) for i in range(4)]) for r in (1, 3, 2)
    ]


def ring_spread(block, axis):
    behind1, behind3, behind2 = from_others([block] * 4, axis)
    return jnp.stack([block, behind3, behind2, behind1])


def ring_summed(blocks, axis):
    total = blocks[0].astype(f32)
    for other in from_others(blocks, axis):
        total = total + other.astype(f32)
    return total


def rolled(blocks, shift):
    return jnp.stack([pick(blocks, (r - shift) % 4) for r in range(4)])


def column_own(block):
    return rolled(ring_spread(block, RING), lax.axis_index(RING)).reshape(-1, block.shape[1])


def column_summed(rows):
    return ring_summed(rolled(rows.reshape(4, -1, rows.shape[1]), -lax.axis_index(RING)), RING)


def by_place(own, other):
    own, other = (rows.reshape(4, -1, rows.shape[1]) for rows in (own, other))
    first = lax.axis_index("core") == 0
    rows = jnp.stack([jnp.where(first, own, other), jnp.where(first, other, own)], 1)
    return rows.reshape(-1, own.shape[2])


def by_core(rows):
    core = lax.axis_index("core")
    blocks = rows.reshape(4, 2, -1, rows.shape[1])
    return tuple(pick(blocks, c, 1).reshape(-1, rows.shape[1]) for c in (core, 1 - core))


def core_summed(left, right, dims):
    away = dot(left[1], right, dims).astype(bf16)
    away, own = lax.optimization_barrier((away, left[0]))
    own, away = lax.optimization_barrier((dot(own, right, dims), swapped(away, "core")))
    return (own + away.astype(f32)).astype(bf16)


def paired_sum(block, steps):
    for axis, bit in steps:
        route = [(i, i ^ bit) for i in range(lax.axis_size(axis))]
        block = block + lax.ppermute(block, axis, route)
    return block


def pick(blocks, index, axis=0):
    return lax.dynamic_index_in_dim(blocks, index, axis, keepdims=False)


def halves(block, width):
    low = lax.axis_index("zh") == 0
    first, last = block[..., :width], block[..., width:]
    return jnp.where(low, first, last), jnp.where(low, last, first)


def joined(own, other, axis):
    low = lax.axis_index("zh") == 0
    return jnp.where(
        low, jnp.concatenate([own, other], axis), jnp.concatenate([other, own], axis)
    )


def dot(left, right, dims):
    return lax.dot_general(left, right, ((dims[0], dims[1]), ((), ())), preferred_element_type=f32)


NN = ((1,), (0,))
NT = ((1,), (1,))
TN = ((0,), (0,))


def weight_grads(groups):
    rows, wide = groups[0][0][0].shape
    step = 512
    terms = [term for group in groups for term in group]
    count = len(terms)
    columns = sum(group[0][1].shape[1] for group in groups)

    def body(*refs):
        at, products = 0, []
        for group in groups:
            total = None
            for _ in group:
                product = dot(refs[at][...], refs[count + at][...], TN)
                total = product if total is None else total + product
                at += 1
            products.append(total.astype(bf16))
        refs[-1][...] = jnp.concatenate(products, 1)

    lefts = [pl.BlockSpec((left.shape[0], step), lambda i: (0, i)) for left, _ in terms]
    rights = [pl.BlockSpec(right.shape, lambda i: (0, 0)) for _, right in terms]
    return pl.pallas_call(
        body,
        grid=(wide // step,),
        in_specs=lefts + rights,
        out_specs=pl.BlockSpec((step, columns), lambda i: (i, 0)),
        out_shape=jax.ShapeDtypeStruct((wide, columns), bf16),
        compiler_params=pltpu.CompilerParams(vmem_limit_bytes=48 * 1024 * 1024),
        cost_estimate=pl.CostEstimate(
            flops=2 * sum(left.shape[0] * right.shape[1] for left, right in terms) * wide,
            bytes_accessed=2 * (len(terms) * rows * wide + (rows + wide) * columns),
            transcendentals=0,
        ),
    )(*[left for left, _ in terms], *[right for _, right in terms])


def on_device(
    inputs,
    cotangent,
    seq_lengths,
    gains,
    gains_first,
    gains_second,
    conv_weight,
    conv_first,
    conv_second,
    in_weight,
    in_first,
    in_second,
    out_weight,
    out_first,
    out_second,
    gate_up,
    gate_up_first,
    gate_up_second,
    down_weight,
    down_first,
    down_second,
):
    tok_rows = inputs.shape[0]
    group_len = tok_rows * 8
    chan_len = conv_weight.shape[1] // 2
    rows_len = in_weight.shape[1]
    half = gate_up.shape[2] // 2
    wide = -(-half // 128) * 128
    mp_index = lax.axis_index(MP)
    zh = lax.axis_index("zh")

    resid = inputs.astype(f32)
    scale_one = lax.rsqrt(jnp.mean(resid * resid, axis=-1, keepdims=True) + norm_eps)
    unit_one = resid * scale_one
    normed_one = (unit_one * gains[0]).astype(bf16)

    def padded(block):
        return jnp.pad(block, ((0, 0), (0, wide - half)))

    own_in, away_in = halves(in_weight.astype(bf16), chan_len)
    own_out, away_out = halves(out_weight.astype(bf16).T, chan_len)
    own_down, away_down = halves(down_weight.astype(bf16).T, half)
    own, away = (
        jnp.concatenate([i[0], i[1], i[2], o, padded(d)], 1)
        for i, o, d in ((own_in, own_out, own_down), (away_in, away_out, away_down))
    )
    w_mix = lax.all_gather(joined(own, swapped(away, "zh"), 0), XY, axis=0, tiled=True)
    mix_cols = 4 * chan_len
    w_in, w_out = w_mix[:, : 3 * chan_len], w_mix[:, 3 * chan_len : mix_cols]
    w_down = w_mix[:, mix_cols:]
    own_gate, away_gate = halves(gate_up.astype(bf16), half)
    own, away = (jnp.concatenate([padded(g[0]), padded(g[1])], 1) for g in (own_gate, away_gate))
    w_gate_up = lax.all_gather(joined(own, swapped(away, "zh"), 0), XY, axis=0, tiled=True)

    first_row = lax.axis_index(XY) * group_len
    place = positions(seq_lengths, first_row, group_len + 2)
    fwd_one = (place[:group_len] >= 1).astype(f32)[:, None]
    fwd_two = (place[:group_len] >= 2).astype(f32)[:, None]
    back_one = (place[1 : group_len + 1] >= 1).astype(f32)[:, None]
    back_two = (place[2:] >= 2).astype(f32)[:, None]

    own_rows = column_own(normed_one)
    group_in = by_place(own_rows, swapped(own_rows, "core"))
    lead = 16
    before = shifted(group_in[group_len - lead :], XY, 1)
    group_in, cotangent_sent = lax.optimization_barrier((group_in, cotangent))
    own_cot = column_own(cotangent_sent)
    column_cot = jnp.concatenate([own_cot, swapped(own_cot, "core")], 0)
    column_cot, w_in = lax.optimization_barrier((column_cot, w_in))
    taps = halves(conv_weight, chan_len)[0]
    projected = dot(jnp.concatenate([before, group_in], 0), w_in, NN)
    proj_b = projected[lead:, :chan_len]
    proj_c = projected[lead:, chan_len : 2 * chan_len]
    proj_x = projected[lead:, 2 * chan_len :]
    extended = projected[:, :chan_len] * projected[:, 2 * chan_len :]
    gated = extended[lead:]
    one_back = extended[lead - 1 : lead - 1 + group_len] * fwd_one
    two_back = extended[lead - 2 : lead - 2 + group_len] * fwd_two
    convolved = taps[0] * gated + taps[1] * one_back + taps[2] * two_back
    mixed = by_core((proj_c * convolved).astype(bf16))
    middle = resid + summed_over(core_summed(mixed, w_out, NT), RING, 4)
    grad_hidden = dot(column_cot, w_down, NN)
    middle, grad_hidden = lax.optimization_barrier((middle, grad_hidden))

    scale_two = lax.rsqrt(jnp.mean(middle * middle, axis=-1, keepdims=True) + norm_eps)
    unit_two = middle * scale_two
    normed_two = (unit_two * gains[1]).astype(bf16)
    own_mid = column_own(normed_two)
    column_mid = jnp.concatenate([own_mid, swapped(own_mid, "core")], 0)
    gate_vals = dot(column_mid, w_gate_up, NN)
    gate, up = gate_vals[:, :wide], gate_vals[:, wide:]
    sigma = jax.nn.sigmoid(gate)
    swish = gate * sigma
    hidden = (swish * up).astype(bf16)
    grad_gate = grad_hidden * up * sigma * (1.0 + gate * (1.0 - sigma))
    grad_up = grad_hidden * swish
    grad_pair = jnp.concatenate([grad_gate.astype(bf16), grad_up.astype(bf16)], 1)
    summed = core_summed(jnp.split(grad_pair, 2, 0), w_gate_up, NT)
    summed, grad_pair, hidden = lax.optimization_barrier((summed, grad_pair, hidden))
    grad_normed_two = summed_over(summed, RING, 4)
    grad_ff = weight_grads([[(column_mid, grad_pair)], [(column_cot, hidden)]])
    grad_normed_two, grad_ff = lax.optimization_barrier((grad_normed_two, grad_ff))
    grad_ff = lax.psum_scatter(grad_ff, XY, scatter_dimension=0, tiled=True)

    gain_two_part = jnp.sum(grad_normed_two * unit_two, axis=0)
    grad_unit_two = grad_normed_two * gains[1]
    grad_middle = cotangent.astype(f32) + scale_two * (
        grad_unit_two - unit_two * jnp.mean(grad_unit_two * unit_two, axis=-1, keepdims=True)
    )

    own_back = column_own(grad_middle.astype(bf16))
    ff_out = dot(hidden, w_down, NT).astype(bf16)
    own_back, ff_out = lax.optimization_barrier((own_back, ff_out))
    other_back = swapped(own_back, "core")
    grad_mixed = by_place(dot(own_back, w_out, NN), dot(other_back, w_out, NN))
    grad_conv_out = grad_mixed * proj_c
    following = shifted(grad_conv_out[:2], XY, -1)
    grad_readout = (grad_mixed * convolved).astype(bf16)
    conv_part = jnp.stack(
        [
            jnp.sum(grad_conv_out * gated, axis=0),
            jnp.sum(grad_conv_out * one_back, axis=0),
            jnp.sum(grad_conv_out * two_back, axis=0),
        ]
    )
    ahead = jnp.concatenate([grad_conv_out, following], 0)
    grad_gated = (
        taps[0] * grad_conv_out
        + taps[1] * ahead[1 : group_len + 1] * back_one
        + taps[2] * ahead[2:] * back_two
    )
    grad_proj = jnp.concatenate(
        [
            (grad_gated * proj_x).astype(bf16),
            grad_readout,
            (grad_gated * proj_b).astype(bf16),
        ],
        1,
    )
    grad_mix = weight_grads(
        [[(group_in, grad_proj)], [(own_back, mixed[0]), (other_back, mixed[1])]]
    )
    grad_mix, ff_out = lax.optimization_barrier((grad_mix, ff_out))
    grad_mix = summed_over(grad_mix, XY, 16).astype(bf16)
    own, away = jnp.split(ff_out, 2, 0)
    away, grad_proj = lax.optimization_barrier((swapped(away, "core"), grad_proj))
    ff_out = (own.astype(f32) + away.astype(f32)).astype(bf16)
    grad_normed_one = dot(grad_proj, w_in, NT)
    gain_one_part = jnp.sum(grad_normed_one * group_in.astype(f32), axis=0) / gains[0]
    own, away = by_core(grad_normed_one.astype(bf16))
    own = (own.astype(f32) + swapped(away, "core").astype(f32)).astype(bf16)
    grad_mix, own, ff_out = lax.optimization_barrier((grad_mix, own, ff_out))
    grad_normed_one = column_summed(own)
    block_out = (middle + column_summed(ff_out)).astype(bf16)

    def both(block):
        pair = block.reshape(2, rows_len, -1)
        return pick(pair, zh), swapped(pick(pair, 1 - zh), "zh")

    conv_full = lax.dynamic_update_slice(
        jnp.zeros((3, D), f32), conv_part, (jnp.int32(0), (2 * mp_index + zh) * chan_len)
    )
    small = jnp.concatenate([gain_one_part[None], gain_two_part[None], conv_full], 0)
    small = paired_sum(small, (("core", 1), ("zl", 1), ("zh", 1)))
    own_ff, other_ff = both(grad_ff)
    small, grad_mix = lax.optimization_barrier((small, grad_mix))
    small = jnp.sum(spread(small, XY, 16), axis=0)
    gain_sum, conv_sum = small[:2], small[2:]

    grad_unit_one = grad_normed_one * gains[0]
    input_grad = grad_middle + scale_one * (
        grad_unit_one - unit_one * jnp.mean(grad_unit_one * unit_one, axis=-1, keepdims=True)
    )

    def spliced(pair, start, width):
        own, other = (block[:, start : start + width] for block in pair)
        return joined(own, other, 1).astype(f32)

    pair = both(grad_mix)
    grad_in = jnp.stack([spliced(pair, i * chan_len, chan_len) for i in range(3)])
    grad_out = spliced(pair, 3 * chan_len, chan_len).T
    pair = (own_ff, other_ff)
    grad_gate_up = jnp.stack([spliced(pair, i * wide, half) for i in range(2)])
    grad_down = spliced(pair, 2 * wide, half).T

    grad_taps = lax.dynamic_slice_in_dim(conv_sum, mp_index * 2 * chan_len, 2 * chan_len, 1)
    gains_set = adam(gains, gains_first, gains_second, gain_sum, 1.0, 0.0)
    conv_set = adam(conv_weight, conv_first, conv_second, grad_taps, 1.0, 0.0)
    in_set = adam(in_weight, in_first, in_second, grad_in, 2.0 * D ** (-0.5), weight_decay)
    out_set = adam(out_weight, out_first, out_second, grad_out, 2.0 * D ** (-0.5), weight_decay)
    gate_set = adam(
        gate_up, gate_up_first, gate_up_second, grad_gate_up, 2.0 * D ** (-0.5), weight_decay
    )
    down_set = adam(
        down_weight, down_first, down_second, grad_down, 2.0 * FF ** (-0.5), weight_decay
    )
    return (block_out, input_grad, *gains_set, *conv_set, *in_set, *out_set, *gate_set, *down_set)


def solution(mesh):
    parts = Mesh(mesh.devices.reshape(4, 4, 2, 2, 2), ("x", "y", "zh", "zl", "core"))
    tokens = P(DP + MP, None)
    taps = P(None, MP)
    wide_in = P(None, DP, MP)
    wide_out = P(MP, DP)
    in_specs = (
        (tokens,) * 2 + (P(),) * 4 + (taps,) * 3 + (wide_in,) * 3 + (wide_out,) * 3
        + (wide_in,) * 3 + (wide_out,) * 3
    )
    out_specs = (
        (tokens,) * 2 + (P(),) * 3 + (taps,) * 3 + (wide_in,) * 3 + (wide_out,) * 3
        + (wide_in,) * 3 + (wide_out,) * 3
    )
    return jax.shard_map(
        on_device, mesh=parts, in_specs=in_specs, out_specs=out_specs, check_vma=False
    )
```

```python
import jax
import jax.numpy as jnp
from jax import lax
from jax.experimental import pallas as pl
from jax.experimental.pallas import tpu as pltpu
from jax.sharding import Mesh
from jax.sharding import PartitionSpec as P

D = 1536
FF = 6912
STEP = 5

norm_eps = 1e-05
beta_one = 0.9
beta_two = 0.95
adam_eps = 1e-08
weight_decay = 0.1

bf16 = jnp.bfloat16
f32 = jnp.float32

XY = ("x", "y")
DP = ("x", "y", "zh")
MP = ("zl", "core")
RING = ("zh", "zl")
COL = ("zh", "zl", "core")


def positions(seq_lengths, first_row, count):
    ends = jnp.cumsum(seq_lengths)
    starts = ends - seq_lengths
    rows = first_row + jnp.arange(count, dtype=jnp.int32)
    covered = starts[None, :] <= rows[:, None]
    return rows - jnp.max(jnp.where(covered, starts[None, :], 0), axis=1)


def adam(weight, first, second, grad, rate, decay):
    first_new = beta_one * first + (1 - beta_one) * grad
    second_new = beta_two * second + (1 - beta_two) * grad * grad
    first_hat = first_new / (1 - beta_one**STEP)
    second_hat = second_new / (1 - beta_two**STEP)
    return (
        first_new,
        second_new,
        weight - rate * (first_hat / (jnp.sqrt(second_hat) + adam_eps) + decay * weight),
    )


def shifted(block, axes, distance):
    size = 1
    for axis in axes:
        size *= lax.axis_size(axis)
    route = [(i - distance, i) for i in range(size) if 0 <= i - distance < size]
    return lax.ppermute(block, axes, route)


def swapped(block, axis):
    return lax.ppermute(block, axis, [(0, 1), (1, 0)])


def exchanged(blocks, axes):
    return lax.all_to_all(blocks, axes, 0, 0, tiled=True)


def spread(block, axes, count):
    return exchanged(jnp.broadcast_to(block, (count, *block.shape)), axes)


def summed_over(block, axes, count):
    blocks = exchanged(block, axes).reshape(count, -1, *block.shape[1:])
    return jnp.sum(blocks.astype(f32), axis=0)


def from_others(blocks, axis):
    return [
        lax.ppermute(blocks[r], axis, [(i, (i + r) % 4) for i in range(4)]) for r in (1, 3, 2)
    ]


def ring_spread(block, axis):
    behind1, behind3, behind2 = from_others([block] * 4, axis)
    return jnp.stack([block, behind3, behind2, behind1])


def ring_summed(blocks, axis):
    total = blocks[0].astype(f32)
    for other in from_others(blocks, axis):
        total = total + other.astype(f32)
    return total


def rolled(blocks, shift):
    return jnp.stack([pick(blocks, (r - shift) % 4) for r in range(4)])


def column_own(block):
    return rolled(ring_spread(block, RING), lax.axis_index(RING)).reshape(-1, block.shape[1])


def column_summed(rows):
    return ring_summed(rolled(rows.reshape(4, -1, rows.shape[1]), -lax.axis_index(RING)), RING)


def by_place(own, other):
    own, other = (rows.reshape(4, -1, rows.shape[1]) for rows in (own, other))
    first = lax.axis_index("core") == 0
    rows = jnp.stack([jnp.where(first, own, other), jnp.where(first, other, own)], 1)
    return rows.reshape(-1, own.shape[2])


def by_core(rows):
    core = lax.axis_index("core")
    blocks = rows.reshape(4, 2, -1, rows.shape[1])
    return tuple(pick(blocks, c, 1).reshape(-1, rows.shape[1]) for c in (core, 1 - core))


def core_summed(left, right, dims):
    away = dot(left[1], right, dims).astype(bf16)
    away, own = lax.optimization_barrier((away, left[0]))
    own, away = lax.optimization_barrier((dot(own, right, dims), swapped(away, "core")))
    return (own + away.astype(f32)).astype(bf16)


def paired_sum(block, steps):
    for axis, bit in steps:
        route = [(i, i ^ bit) for i in range(lax.axis_size(axis))]
        block = block + lax.ppermute(block, axis, route)
    return block


def pick(blocks, index, axis=0):
    return lax.dynamic_index_in_dim(blocks, index, axis, keepdims=False)


def halves(block, width):
    low = lax.axis_index("zh") == 0
    first, last = block[..., :width], block[..., width:]
    return jnp.where(low, first, last), jnp.where(low, last, first)


def joined(own, other, axis):
    low = lax.axis_index("zh") == 0
    return jnp.where(
        low, jnp.concatenate([own, other], axis), jnp.concatenate([other, own], axis)
    )


def dot(left, right, dims):
    return lax.dot_general(left, right, ((dims[0], dims[1]), ((), ())), preferred_element_type=f32)


NN = ((1,), (0,))
NT = ((1,), (1,))
TN = ((0,), (0,))


def weight_grads(groups):
    rows, wide = groups[0][0][0].shape
    step = 512
    terms = [term for group in groups for term in group]
    count = len(terms)
    columns = sum(group[0][1].shape[1] for group in groups)

    def body(*refs):
        at, products = 0, []
        for group in groups:
            total = None
            for _ in group:
                product = dot(refs[at][...], refs[count + at][...], TN)
                total = product if total is None else total + product
                at += 1
            products.append(total.astype(bf16))
        refs[-1][...] = jnp.concatenate(products, 1)

    lefts = [pl.BlockSpec((left.shape[0], step), lambda i: (0, i)) for left, _ in terms]
    rights = [pl.BlockSpec(right.shape, lambda i: (0, 0)) for _, right in terms]
    return pl.pallas_call(
        body,
        grid=(wide // step,),
        in_specs=lefts + rights,
        out_specs=pl.BlockSpec((step, columns), lambda i: (i, 0)),
        out_shape=jax.ShapeDtypeStruct((wide, columns), bf16),
        compiler_params=pltpu.CompilerParams(vmem_limit_bytes=48 * 1024 * 1024),
        cost_estimate=pl.CostEstimate(
            flops=2 * sum(left.shape[0] * right.shape[1] for left, right in terms) * wide,
            bytes_accessed=2 * (len(terms) * rows * wide + (rows + wide) * columns),
            transcendentals=0,
        ),
    )(*[left for left, _ in terms], *[right for _, right in terms])


def on_device(
    inputs,
    cotangent,
    seq_lengths,
    gains,
    gains_first,
    gains_second,
    conv_weight,
    conv_first,
    conv_second,
    in_weight,
    in_first,
    in_second,
    out_weight,
    out_first,
    out_second,
    gate_up,
    gate_up_first,
    gate_up_second,
    down_weight,
    down_first,
    down_second,
):
    tok_rows = inputs.shape[0]
    group_len = tok_rows * 8
    chan_len = conv_weight.shape[1] // 2
    rows_len = in_weight.shape[1]
    half = gate_up.shape[2] // 2
    wide = -(-half // 128) * 128
    mp_index = lax.axis_index(MP)
    zh = lax.axis_index("zh")

    resid = inputs.astype(f32)
    scale_one = lax.rsqrt(jnp.mean(resid * resid, axis=-1, keepdims=True) + norm_eps)
    unit_one = resid * scale_one
    normed_one = (unit_one * gains[0]).astype(bf16)

    def padded(block):
        return jnp.pad(block, ((0, 0), (0, wide - half)))

    own_in, away_in = halves(in_weight.astype(bf16), chan_len)
    own_out, away_out = halves(out_weight.astype(bf16).T, chan_len)
    own_down, away_down = halves(down_weight.astype(bf16).T, half)
    own, away = (
        jnp.concatenate([i[0], i[1], i[2], o, padded(d)], 1)
        for i, o, d in ((own_in, own_out, own_down), (away_in, away_out, away_down))
    )
    w_mix = lax.all_gather(joined(own, swapped(away, "zh"), 0), XY, axis=0, tiled=True)
    mix_cols = 4 * chan_len
    w_in, w_out = w_mix[:, : 3 * chan_len], w_mix[:, 3 * chan_len : mix_cols]
    w_down = w_mix[:, mix_cols:]
    own_gate, away_gate = halves(gate_up.astype(bf16), half)
    own, away = (jnp.concatenate([padded(g[0]), padded(g[1])], 1) for g in (own_gate, away_gate))
    w_gate_up = lax.all_gather(joined(own, swapped(away, "zh"), 0), XY, axis=0, tiled=True)

    first_row = lax.axis_index(XY) * group_len
    place = positions(seq_lengths, first_row, group_len + 2)
    fwd_one = (place[:group_len] >= 1).astype(f32)[:, None]
    fwd_two = (place[:group_len] >= 2).astype(f32)[:, None]
    back_one = (place[1 : group_len + 1] >= 1).astype(f32)[:, None]
    back_two = (place[2:] >= 2).astype(f32)[:, None]

    own_rows = column_own(normed_one)
    group_in = by_place(own_rows, swapped(own_rows, "core"))
    lead = 16
    before = shifted(group_in[group_len - lead :], XY, 1)
    group_in, cotangent_sent = lax.optimization_barrier((group_in, cotangent))
    own_cot = column_own(cotangent_sent)
    column_cot = jnp.concatenate([own_cot, swapped(own_cot, "core")], 0)
    column_cot, w_in = lax.optimization_barrier((column_cot, w_in))
    taps = halves(conv_weight, chan_len)[0]
    projected = dot(jnp.concatenate([before, group_in], 0), w_in, NN)
    proj_b = projected[lead:, :chan_len]
    proj_c = projected[lead:, chan_len : 2 * chan_len]
    proj_x = projected[lead:, 2 * chan_len :]
    extended = projected[:, :chan_len] * projected[:, 2 * chan_len :]
    gated = extended[lead:]
    one_back = extended[lead - 1 : lead - 1 + group_len] * fwd_one
    two_back = extended[lead - 2 : lead - 2 + group_len] * fwd_two
    convolved = taps[0] * gated + taps[1] * one_back + taps[2] * two_back
    mixed = (proj_c * convolved).astype(bf16)
    middle = resid + summed_over(core_summed(by_core(mixed), w_out, NT), RING, 4)
    grad_hidden = dot(column_cot, w_down, NN)
    middle, grad_hidden = lax.optimization_barrier((middle, grad_hidden))

    scale_two = lax.rsqrt(jnp.mean(middle * middle, axis=-1, keepdims=True) + norm_eps)
    unit_two = middle * scale_two
    normed_two = (unit_two * gains[1]).astype(bf16)
    own_mid = column_own(normed_two)
    column_mid = jnp.concatenate([own_mid, swapped(own_mid, "core")], 0)
    gate_vals = dot(column_mid, w_gate_up, NN)
    gate, up = gate_vals[:, :wide], gate_vals[:, wide:]
    sigma = jax.nn.sigmoid(gate)
    swish = gate * sigma
    hidden = (swish * up).astype(bf16)
    grad_gate = grad_hidden * up * sigma * (1.0 + gate * (1.0 - sigma))
    grad_up = grad_hidden * swish
    grad_pair = jnp.concatenate([grad_gate.astype(bf16), grad_up.astype(bf16)], 1)
    summed = core_summed(jnp.split(grad_pair, 2, 0), w_gate_up, NT)
    summed, grad_pair, hidden = lax.optimization_barrier((summed, grad_pair, hidden))
    grad_normed_two = summed_over(summed, RING, 4)
    grad_ff = weight_grads([[(column_mid, grad_pair)], [(column_cot, hidden)]])
    grad_normed_two, grad_ff = lax.optimization_barrier((grad_normed_two, grad_ff))
    grad_ff = lax.psum_scatter(grad_ff, XY, scatter_dimension=0, tiled=True)

    gain_two_part = jnp.sum(grad_normed_two * unit_two, axis=0)
    grad_unit_two = grad_normed_two * gains[1]
    grad_middle = cotangent.astype(f32) + scale_two * (
        grad_unit_two - unit_two * jnp.mean(grad_unit_two * unit_two, axis=-1, keepdims=True)
    )

    own_back = column_own(grad_middle.astype(bf16))
    ff_out = dot(hidden, w_down, NT).astype(bf16)
    own_back, ff_out = lax.optimization_barrier((own_back, ff_out))
    group_back = by_place(own_back, swapped(own_back, "core"))
    grad_mixed = dot(group_back, w_out, NN)
    grad_conv_out = grad_mixed * proj_c
    following = shifted(grad_conv_out[:2], XY, -1)
    grad_readout = (grad_mixed * convolved).astype(bf16)
    conv_part = jnp.stack(
        [
            jnp.sum(grad_conv_out * gated, axis=0),
            jnp.sum(grad_conv_out * one_back, axis=0),
            jnp.sum(grad_conv_out * two_back, axis=0),
        ]
    )
    ahead = jnp.concatenate([grad_conv_out, following], 0)
    grad_gated = (
        taps[0] * grad_conv_out
        + taps[1] * ahead[1 : group_len + 1] * back_one
        + taps[2] * ahead[2:] * back_two
    )
    grad_proj = jnp.concatenate(
        [
            (grad_gated * proj_x).astype(bf16),
            grad_readout,
            (grad_gated * proj_b).astype(bf16),
        ],
        1,
    )
    grad_mix = weight_grads([[(group_in, grad_proj)], [(group_back, mixed)]])
    grad_mix, grad_proj = lax.optimization_barrier((grad_mix, grad_proj))
    grad_mix = summed_over(grad_mix, XY, 16).astype(bf16)
    own, away = jnp.split(ff_out, 2, 0)
    ff_out = (own.astype(f32) + swapped(away, "core").astype(f32)).astype(bf16)
    grad_normed_one = dot(grad_proj, w_in, NT)
    gain_one_part = jnp.sum(grad_normed_one * group_in.astype(f32), axis=0) / gains[0]
    own, away = by_core(grad_normed_one.astype(bf16))
    own = (own.astype(f32) + swapped(away, "core").astype(f32)).astype(bf16)
    grad_normed_one = column_summed(own)
    block_out = (middle + column_summed(ff_out)).astype(bf16)

    def both(block):
        pair = block.reshape(2, rows_len, -1)
        return pick(pair, zh), swapped(pick(pair, 1 - zh), "zh")

    conv_full = lax.dynamic_update_slice(
        jnp.zeros((3, D), f32), conv_part, (jnp.int32(0), (2 * mp_index + zh) * chan_len)
    )
    small = jnp.concatenate([gain_one_part[None], gain_two_part[None], conv_full], 0)
    small = paired_sum(small, (("core", 1), ("zl", 1), ("zh", 1)))
    own_ff, other_ff = both(grad_ff)
    small, grad_mix = lax.optimization_barrier((small, grad_mix))
    small = jnp.sum(spread(small, XY, 16), axis=0)
    small, other_ff = lax.optimization_barrier((small, other_ff))
    gain_sum, conv_sum = small[:2], small[2:]

    grad_unit_one = grad_normed_one * gains[0]
    input_grad = grad_middle + scale_one * (
        grad_unit_one - unit_one * jnp.mean(grad_unit_one * unit_one, axis=-1, keepdims=True)
    )

    def spliced(pair, start, width):
        own, other = (block[:, start : start + width] for block in pair)
        return joined(own, other, 1).astype(f32)

    pair = both(grad_mix)
    grad_in = jnp.stack([spliced(pair, i * chan_len, chan_len) for i in range(3)])
    grad_out = spliced(pair, 3 * chan_len, chan_len).T
    pair = (own_ff, other_ff)
    grad_gate_up = jnp.stack([spliced(pair, i * wide, half) for i in range(2)])
    grad_down = spliced(pair, 2 * wide, half).T

    grad_taps = lax.dynamic_slice_in_dim(conv_sum, mp_index * 2 * chan_len, 2 * chan_len, 1)
    gains_set = adam(gains, gains_first, gains_second, gain_sum, 1.0, 0.0)
    conv_set = adam(conv_weight, conv_first, conv_second, grad_taps, 1.0, 0.0)
    in_set = adam(in_weight, in_first, in_second, grad_in, 2.0 * D ** (-0.5), weight_decay)
    out_set = adam(out_weight, out_first, out_second, grad_out, 2.0 * D ** (-0.5), weight_decay)
    gate_set = adam(
        gate_up, gate_up_first, gate_up_second, grad_gate_up, 2.0 * D ** (-0.5), weight_decay
    )
    down_set = adam(
        down_weight, down_first, down_second, grad_down, 2.0 * FF ** (-0.5), weight_decay
    )
    return (block_out, input_grad, *gains_set, *conv_set, *in_set, *out_set, *gate_set, *down_set)


def solution(mesh):
    parts = Mesh(mesh.devices.reshape(4, 4, 2, 2, 2), ("x", "y", "zh", "zl", "core"))
    tokens = P(DP + MP, None)
    taps = P(None, MP)
    wide_in = P(None, DP, MP)
    wide_out = P(MP, DP)
    in_specs = (
        (tokens,) * 2 + (P(),) * 4 + (taps,) * 3 + (wide_in,) * 3 + (wide_out,) * 3
        + (wide_in,) * 3 + (wide_out,) * 3
    )
    out_specs = (
        (tokens,) * 2 + (P(),) * 3 + (taps,) * 3 + (wide_in,) * 3 + (wide_out,) * 3
        + (wide_in,) * 3 + (wide_out,) * 3
    )
    return jax.shard_map(
        on_device, mesh=parts, in_specs=in_specs, out_specs=out_specs, check_vma=False
    )
```

```python
import jax
import jax.numpy as jnp
from jax import lax
from jax.experimental import pallas as pl
from jax.experimental.pallas import tpu as pltpu
from jax.sharding import Mesh
from jax.sharding import PartitionSpec as P

D = 1536
FF = 6912
STEP = 5

norm_eps = 1e-05
beta_one = 0.9
beta_two = 0.95
adam_eps = 1e-08
weight_decay = 0.1

bf16 = jnp.bfloat16
f32 = jnp.float32

XY = ("x", "y")
DP = ("x", "y", "zh")
MP = ("zl", "core")
RING = ("zh", "zl")
COL = ("zh", "zl", "core")


def positions(seq_lengths, first_row, count):
    ends = jnp.cumsum(seq_lengths)
    starts = ends - seq_lengths
    rows = first_row + jnp.arange(count, dtype=jnp.int32)
    covered = starts[None, :] <= rows[:, None]
    return rows - jnp.max(jnp.where(covered, starts[None, :], 0), axis=1)


def adam(weight, first, second, grad, rate, decay):
    first_new = beta_one * first + (1 - beta_one) * grad
    second_new = beta_two * second + (1 - beta_two) * grad * grad
    first_hat = first_new / (1 - beta_one**STEP)
    second_hat = second_new / (1 - beta_two**STEP)
    return (
        first_new,
        second_new,
        weight - rate * (first_hat / (jnp.sqrt(second_hat) + adam_eps) + decay * weight),
    )


def shifted(block, axes, distance):
    size = 1
    for axis in axes:
        size *= lax.axis_size(axis)
    route = [(i - distance, i) for i in range(size) if 0 <= i - distance < size]
    return lax.ppermute(block, axes, route)


def swapped(block, axis):
    return lax.ppermute(block, axis, [(0, 1), (1, 0)])


def exchanged(blocks, axes):
    return lax.all_to_all(blocks, axes, 0, 0, tiled=True)


def spread(block, axes, count):
    return exchanged(jnp.broadcast_to(block, (count, *block.shape)), axes)


def summed_over(block, axes, count):
    blocks = exchanged(block, axes).reshape(count, -1, *block.shape[1:])
    return jnp.sum(blocks.astype(f32), axis=0)


def from_others(blocks, axis):
    return [
        lax.ppermute(blocks[r], axis, [(i, (i + r) % 4) for i in range(4)]) for r in (1, 3, 2)
    ]


def ring_spread(block, axis):
    behind1, behind3, behind2 = from_others([block] * 4, axis)
    return jnp.stack([block, behind3, behind2, behind1])


def ring_summed(blocks, axis):
    total = blocks[0].astype(f32)
    for other in from_others(blocks, axis):
        total = total + other.astype(f32)
    return total


def rolled(blocks, shift):
    return jnp.stack([pick(blocks, (r - shift) % 4) for r in range(4)])


def column_own(block):
    return rolled(ring_spread(block, RING), lax.axis_index(RING)).reshape(-1, block.shape[1])


def column_summed(rows):
    return ring_summed(rolled(rows.reshape(4, -1, rows.shape[1]), -lax.axis_index(RING)), RING)


def by_place(own, other):
    own, other = (rows.reshape(4, -1, rows.shape[1]) for rows in (own, other))
    first = lax.axis_index("core") == 0
    rows = jnp.stack([jnp.where(first, own, other), jnp.where(first, other, own)], 1)
    return rows.reshape(-1, own.shape[2])


def by_core(rows):
    core = lax.axis_index("core")
    blocks = rows.reshape(4, 2, -1, rows.shape[1])
    return tuple(pick(blocks, c, 1).reshape(-1, rows.shape[1]) for c in (core, 1 - core))


def core_summed(left, right, dims):
    away = dot(left[1], right, dims).astype(bf16)
    away, own = lax.optimization_barrier((away, left[0]))
    own, away = lax.optimization_barrier((dot(own, right, dims), swapped(away, "core")))
    return (own + away.astype(f32)).astype(bf16)


def paired_sum(block, steps):
    for axis, bit in steps:
        route = [(i, i ^ bit) for i in range(lax.axis_size(axis))]
        block = block + lax.ppermute(block, axis, route)
    return block


def pick(blocks, index, axis=0):
    return lax.dynamic_index_in_dim(blocks, index, axis, keepdims=False)


def halves(block, width):
    low = lax.axis_index("zh") == 0
    first, last = block[..., :width], block[..., width:]
    return jnp.where(low, first, last), jnp.where(low, last, first)


def joined(own, other, axis):
    low = lax.axis_index("zh") == 0
    return jnp.where(
        low, jnp.concatenate([own, other], axis), jnp.concatenate([other, own], axis)
    )


def dot(left, right, dims):
    return lax.dot_general(left, right, ((dims[0], dims[1]), ((), ())), preferred_element_type=f32)


NN = ((1,), (0,))
NT = ((1,), (1,))
TN = ((0,), (0,))


def weight_grads(groups):
    rows, wide = groups[0][0][0].shape
    step = 512
    terms = [term for group in groups for term in group]
    count = len(terms)
    columns = sum(group[0][1].shape[1] for group in groups)

    def body(*refs):
        at, products = 0, []
        for group in groups:
            total = None
            for _ in group:
                product = dot(refs[at][...], refs[count + at][...], TN)
                total = product if total is None else total + product
                at += 1
            products.append(total.astype(bf16))
        refs[-1][...] = jnp.concatenate(products, 1)

    lefts = [pl.BlockSpec((left.shape[0], step), lambda i: (0, i)) for left, _ in terms]
    rights = [pl.BlockSpec(right.shape, lambda i: (0, 0)) for _, right in terms]
    return pl.pallas_call(
        body,
        grid=(wide // step,),
        in_specs=lefts + rights,
        out_specs=pl.BlockSpec((step, columns), lambda i: (i, 0)),
        out_shape=jax.ShapeDtypeStruct((wide, columns), bf16),
        compiler_params=pltpu.CompilerParams(vmem_limit_bytes=48 * 1024 * 1024),
        cost_estimate=pl.CostEstimate(
            flops=2 * sum(left.shape[0] * right.shape[1] for left, right in terms) * wide,
            bytes_accessed=2 * (len(terms) * rows * wide + (rows + wide) * columns),
            transcendentals=0,
        ),
    )(*[left for left, _ in terms], *[right for _, right in terms])


def on_device(
    inputs,
    cotangent,
    seq_lengths,
    gains,
    gains_first,
    gains_second,
    conv_weight,
    conv_first,
    conv_second,
    in_weight,
    in_first,
    in_second,
    out_weight,
    out_first,
    out_second,
    gate_up,
    gate_up_first,
    gate_up_second,
    down_weight,
    down_first,
    down_second,
):
    tok_rows = inputs.shape[0]
    group_len = tok_rows * 8
    chan_len = conv_weight.shape[1] // 2
    rows_len = in_weight.shape[1]
    half = gate_up.shape[2] // 2
    wide = -(-half // 128) * 128
    mp_index = lax.axis_index(MP)
    zh = lax.axis_index("zh")

    resid = inputs.astype(f32)
    scale_one = lax.rsqrt(jnp.mean(resid * resid, axis=-1, keepdims=True) + norm_eps)
    unit_one = resid * scale_one
    normed_one = (unit_one * gains[0]).astype(bf16)

    def padded(block):
        return jnp.pad(block, ((0, 0), (0, wide - half)))

    own_in, away_in = halves(in_weight.astype(bf16), chan_len)
    own_out, away_out = halves(out_weight.astype(bf16).T, chan_len)
    own_down, away_down = halves(down_weight.astype(bf16).T, half)
    own, away = (
        jnp.concatenate([i[0], i[1], i[2], o, padded(d)], 1)
        for i, o, d in ((own_in, own_out, own_down), (away_in, away_out, away_down))
    )
    w_mix = lax.all_gather(joined(own, swapped(away, "zh"), 0), XY, axis=0, tiled=True)
    mix_cols = 4 * chan_len
    w_in, w_out = w_mix[:, : 3 * chan_len], w_mix[:, 3 * chan_len : mix_cols]
    w_down = w_mix[:, mix_cols:]
    own_gate, away_gate = halves(gate_up.astype(bf16), half)
    own, away = (jnp.concatenate([padded(g[0]), padded(g[1])], 1) for g in (own_gate, away_gate))
    gate_rows = joined(own, swapped(away, "zh"), 0)

    first_row = lax.axis_index(XY) * group_len
    place = positions(seq_lengths, first_row, group_len + 2)
    fwd_one = (place[:group_len] >= 1).astype(f32)[:, None]
    fwd_two = (place[:group_len] >= 2).astype(f32)[:, None]
    back_one = (place[1 : group_len + 1] >= 1).astype(f32)[:, None]
    back_two = (place[2:] >= 2).astype(f32)[:, None]

    own_rows = column_own(normed_one)
    group_in = by_place(own_rows, swapped(own_rows, "core"))
    lead = 16
    before = shifted(group_in[group_len - lead :], XY, 1)
    led_in = jnp.concatenate([before, group_in], 0)
    led_in, gate_rows, fwd_one, fwd_two, back_one, back_two, cotangent_sent = (
        lax.optimization_barrier(
            (led_in, gate_rows, fwd_one, fwd_two, back_one, back_two, cotangent)
        )
    )
    w_gate_up = lax.all_gather(gate_rows, XY, axis=0, tiled=True)
    own_cot = column_own(cotangent_sent)
    column_cot = jnp.concatenate([own_cot, swapped(own_cot, "core")], 0)
    column_cot, led_in = lax.optimization_barrier((column_cot, led_in))
    taps = halves(conv_weight, chan_len)[0]
    projected = dot(led_in, w_mix[:, :mix_cols], NN)
    proj_b = projected[lead:, :chan_len]
    proj_c = projected[lead:, chan_len : 2 * chan_len]
    proj_x = projected[lead:, 2 * chan_len : 3 * chan_len]
    extended = projected[:, :chan_len] * projected[:, 2 * chan_len : 3 * chan_len]
    gated = extended[lead:]
    one_back = extended[lead - 1 : lead - 1 + group_len] * fwd_one
    two_back = extended[lead - 2 : lead - 2 + group_len] * fwd_two
    convolved = taps[0] * gated + taps[1] * one_back + taps[2] * two_back
    mixed = (proj_c * convolved).astype(bf16)
    own_mixed, away_mixed = by_core(mixed)
    middle = resid + summed_over(core_summed((own_mixed, away_mixed), w_out, NT), RING, 4)
    grad_hidden = dot(column_cot, w_down, NN)
    middle, grad_hidden = lax.optimization_barrier((middle, grad_hidden))

    scale_two = lax.rsqrt(jnp.mean(middle * middle, axis=-1, keepdims=True) + norm_eps)
    unit_two = middle * scale_two
    normed_two = (unit_two * gains[1]).astype(bf16)
    own_mid = column_own(normed_two)
    column_mid = jnp.concatenate([own_mid, swapped(own_mid, "core")], 0)
    gate_vals = dot(column_mid, w_gate_up, NN)
    gate, up = gate_vals[:, :wide], gate_vals[:, wide:]
    sigma = jax.nn.sigmoid(gate)
    swish = gate * sigma
    hidden = (swish * up).astype(bf16)
    grad_gate = grad_hidden * up * sigma * (1.0 + gate * (1.0 - sigma))
    grad_up = grad_hidden * swish
    grad_pair = jnp.concatenate([grad_gate.astype(bf16), grad_up.astype(bf16)], 1)
    summed = core_summed(jnp.split(grad_pair, 2, 0), w_gate_up, NT)
    summed, grad_pair, hidden = lax.optimization_barrier((summed, grad_pair, hidden))
    grad_normed_two = summed_over(summed, RING, 4)
    grad_ff = weight_grads([[(column_mid, grad_pair)], [(column_cot, hidden)]])
    grad_normed_two, grad_ff = lax.optimization_barrier((grad_normed_two, grad_ff))
    grad_ff = lax.psum_scatter(grad_ff, XY, scatter_dimension=0, tiled=True)

    gain_two_part = jnp.sum(grad_normed_two * unit_two, axis=0)
    grad_unit_two = grad_normed_two * gains[1]
    grad_middle = cotangent.astype(f32) + scale_two * (
        grad_unit_two - unit_two * jnp.mean(grad_unit_two * unit_two, axis=-1, keepdims=True)
    )

    own_back = column_own(grad_middle.astype(bf16))
    ff_out = dot(hidden, w_down, NT).astype(bf16)
    own_back, ff_out = lax.optimization_barrier((own_back, ff_out))
    group_back = by_place(own_back, swapped(own_back, "core"))
    grad_mixed = dot(group_back, w_out, NN)
    grad_conv_out = grad_mixed * proj_c
    following = shifted(grad_conv_out[:2], XY, -1)
    grad_readout = (grad_mixed * convolved).astype(bf16)
    conv_part = jnp.stack(
        [
            jnp.sum(grad_conv_out * gated, axis=0),
            jnp.sum(grad_conv_out * one_back, axis=0),
            jnp.sum(grad_conv_out * two_back, axis=0),
        ]
    )
    ahead = jnp.concatenate([grad_conv_out, following], 0)
    grad_gated = (
        taps[0] * grad_conv_out
        + taps[1] * ahead[1 : group_len + 1] * back_one
        + taps[2] * ahead[2:] * back_two
    )
    grad_proj = jnp.concatenate(
        [
            (grad_gated * proj_x).astype(bf16),
            grad_readout,
            (grad_gated * proj_b).astype(bf16),
        ],
        1,
    )
    grad_mix = weight_grads([[(group_in, grad_proj)], [(group_back, mixed)]])
    grad_mix, grad_proj = lax.optimization_barrier((grad_mix, grad_proj))
    grad_mix = summed_over(grad_mix, XY, 16).astype(bf16)
    own, away = jnp.split(ff_out, 2, 0)
    ff_out = (own.astype(f32) + swapped(away, "core").astype(f32)).astype(bf16)
    grad_normed_one = dot(grad_proj, w_in, NT)
    gain_one_part = jnp.sum(grad_normed_one * group_in.astype(f32), axis=0) / gains[0]
    own, away = by_core(grad_normed_one.astype(bf16))
    own = (own.astype(f32) + swapped(away, "core").astype(f32)).astype(bf16)
    grad_normed_one = column_summed(own)
    block_out = (middle + column_summed(ff_out)).astype(bf16)

    def both(block):
        pair = block.reshape(2, rows_len, -1)
        return pick(pair, zh), swapped(pick(pair, 1 - zh), "zh")

    conv_full = lax.dynamic_update_slice(
        jnp.zeros((3, D), f32), conv_part, (jnp.int32(0), (2 * mp_index + zh) * chan_len)
    )
    small = jnp.concatenate([gain_one_part[None], gain_two_part[None], conv_full], 0)
    small = paired_sum(small, (("core", 1), ("zl", 1), ("zh", 1)))
    pair = grad_ff.reshape(2, rows_len, -1)
    own_ff, away_ff = pick(pair, zh), pick(pair, 1 - zh)
    away_ff, small, grad_mix = lax.optimization_barrier((away_ff, small, grad_mix))
    other_ff = swapped(away_ff, "zh")
    small = jnp.sum(spread(small, XY, 16), axis=0)
    gain_sum, conv_sum = small[:2], small[2:]

    grad_unit_one = grad_normed_one * gains[0]
    input_grad = grad_middle + scale_one * (
        grad_unit_one - unit_one * jnp.mean(grad_unit_one * unit_one, axis=-1, keepdims=True)
    )

    def spliced(pair, start, width):
        own, other = (block[:, start : start + width] for block in pair)
        return joined(own, other, 1).astype(f32)

    pair = both(grad_mix)
    grad_in = jnp.stack([spliced(pair, i * chan_len, chan_len) for i in range(3)])
    grad_out = spliced(pair, 3 * chan_len, chan_len).T
    pair = (own_ff, other_ff)
    grad_gate_up = jnp.stack([spliced(pair, i * wide, half) for i in range(2)])
    grad_down = spliced(pair, 2 * wide, half).T

    grad_taps = lax.dynamic_slice_in_dim(conv_sum, mp_index * 2 * chan_len, 2 * chan_len, 1)
    gains_set = adam(gains, gains_first, gains_second, gain_sum, 1.0, 0.0)
    conv_set = adam(conv_weight, conv_first, conv_second, grad_taps, 1.0, 0.0)
    in_set = adam(in_weight, in_first, in_second, grad_in, 2.0 * D ** (-0.5), weight_decay)
    out_set = adam(out_weight, out_first, out_second, grad_out, 2.0 * D ** (-0.5), weight_decay)
    gate_set = adam(
        gate_up, gate_up_first, gate_up_second, grad_gate_up, 2.0 * D ** (-0.5), weight_decay
    )
    down_set = adam(
        down_weight, down_first, down_second, grad_down, 2.0 * FF ** (-0.5), weight_decay
    )
    return (block_out, input_grad, *gains_set, *conv_set, *in_set, *out_set, *gate_set, *down_set)


def solution(mesh):
    parts = Mesh(mesh.devices.reshape(4, 4, 2, 2, 2), ("x", "y", "zh", "zl", "core"))
    tokens = P(DP + MP, None)
    taps = P(None, MP)
    wide_in = P(None, DP, MP)
    wide_out = P(MP, DP)
    in_specs = (
        (tokens,) * 2 + (P(),) * 4 + (taps,) * 3 + (wide_in,) * 3 + (wide_out,) * 3
        + (wide_in,) * 3 + (wide_out,) * 3
    )
    out_specs = (
        (tokens,) * 2 + (P(),) * 3 + (taps,) * 3 + (wide_in,) * 3 + (wide_out,) * 3
        + (wide_in,) * 3 + (wide_out,) * 3
    )
    return jax.shard_map(
        on_device, mesh=parts, in_specs=in_specs, out_specs=out_specs, check_vma=False
    )
```

```python
import jax
import jax.numpy as jnp
from jax import lax
from jax.experimental import pallas as pl
from jax.experimental.pallas import tpu as pltpu
from jax.sharding import Mesh
from jax.sharding import PartitionSpec as P

D = 1536
FF = 6912
STEP = 5

norm_eps = 1e-05
beta_one = 0.9
beta_two = 0.95
adam_eps = 1e-08
weight_decay = 0.1

bf16 = jnp.bfloat16
f32 = jnp.float32

XY = ("x", "y")
DP = ("x", "y", "zh")
MP = ("zl", "core")
RING = ("zh", "zl")
COL = ("zh", "zl", "core")


def positions(seq_lengths, first_row, count):
    ends = jnp.cumsum(seq_lengths)
    starts = ends - seq_lengths
    rows = first_row + jnp.arange(count, dtype=jnp.int32)
    covered = starts[None, :] <= rows[:, None]
    return rows - jnp.max(jnp.where(covered, starts[None, :], 0), axis=1)


def adam(weight, first, second, grad, rate, decay):
    first_new = beta_one * first + (1 - beta_one) * grad
    second_new = beta_two * second + (1 - beta_two) * grad * grad
    first_hat = first_new / (1 - beta_one**STEP)
    second_hat = second_new / (1 - beta_two**STEP)
    return (
        first_new,
        second_new,
        weight - rate * (first_hat / (jnp.sqrt(second_hat) + adam_eps) + decay * weight),
    )


def shifted(block, axes, distance):
    size = 1
    for axis in axes:
        size *= lax.axis_size(axis)
    route = [(i - distance, i) for i in range(size) if 0 <= i - distance < size]
    return lax.ppermute(block, axes, route)


def swapped(block, axis):
    return lax.ppermute(block, axis, [(0, 1), (1, 0)])


def exchanged(blocks, axes):
    return lax.all_to_all(blocks, axes, 0, 0, tiled=True)


def spread(block, axes, count):
    return exchanged(jnp.broadcast_to(block, (count, *block.shape)), axes)


def summed_over(block, axes, count):
    blocks = exchanged(block, axes).reshape(count, -1, *block.shape[1:])
    return jnp.sum(blocks.astype(f32), axis=0)


def from_others(blocks, axis):
    return [
        lax.ppermute(blocks[r], axis, [(i, (i + r) % 4) for i in range(4)]) for r in (1, 3, 2)
    ]


def ring_spread(block, axis):
    behind1, behind3, behind2 = from_others([block] * 4, axis)
    return jnp.stack([block, behind3, behind2, behind1])


def ring_summed(blocks, axis):
    total = blocks[0].astype(f32)
    for other in from_others(blocks, axis):
        total = total + other.astype(f32)
    return total


def rolled(blocks, shift):
    return jnp.stack([pick(blocks, (r - shift) % 4) for r in range(4)])


def column_own(block):
    return rolled(ring_spread(block, RING), lax.axis_index(RING)).reshape(-1, block.shape[1])


def column_summed(rows):
    return ring_summed(rolled(rows.reshape(4, -1, rows.shape[1]), -lax.axis_index(RING)), RING)


def by_place(own, other):
    own, other = (rows.reshape(4, -1, rows.shape[1]) for rows in (own, other))
    first = lax.axis_index("core") == 0
    rows = jnp.stack([jnp.where(first, own, other), jnp.where(first, other, own)], 1)
    return rows.reshape(-1, own.shape[2])


def by_core(rows):
    core = lax.axis_index("core")
    blocks = rows.reshape(4, 2, -1, rows.shape[1])
    return tuple(pick(blocks, c, 1).reshape(-1, rows.shape[1]) for c in (core, 1 - core))


def core_summed(left, right, dims):
    away = dot(left[1], right, dims).astype(bf16)
    away, own = lax.optimization_barrier((away, left[0]))
    own, away = lax.optimization_barrier((dot(own, right, dims), swapped(away, "core")))
    return (own + away.astype(f32)).astype(bf16)


def paired_sum(block, steps):
    for axis, bit in steps:
        route = [(i, i ^ bit) for i in range(lax.axis_size(axis))]
        block = block + lax.ppermute(block, axis, route)
    return block


def pick(blocks, index, axis=0):
    return lax.dynamic_index_in_dim(blocks, index, axis, keepdims=False)


def halves(block, width):
    low = lax.axis_index("zh") == 0
    first, last = block[..., :width], block[..., width:]
    return jnp.where(low, first, last), jnp.where(low, last, first)


def joined(own, other, axis):
    low = lax.axis_index("zh") == 0
    return jnp.where(
        low, jnp.concatenate([own, other], axis), jnp.concatenate([other, own], axis)
    )


def dot(left, right, dims):
    return lax.dot_general(left, right, ((dims[0], dims[1]), ((), ())), preferred_element_type=f32)


NN = ((1,), (0,))
NT = ((1,), (1,))
TN = ((0,), (0,))


def weight_grads(groups):
    rows, wide = groups[0][0][0].shape
    step = 512
    terms = [term for group in groups for term in group]
    count = len(terms)
    columns = sum(group[0][1].shape[1] for group in groups)

    def body(*refs):
        at, products = 0, []
        for group in groups:
            total = None
            for _ in group:
                product = dot(refs[at][...], refs[count + at][...], TN)
                total = product if total is None else total + product
                at += 1
            products.append(total.astype(bf16))
        refs[-1][...] = jnp.concatenate(products, 1)

    lefts = [pl.BlockSpec((left.shape[0], step), lambda i: (0, i)) for left, _ in terms]
    rights = [pl.BlockSpec(right.shape, lambda i: (0, 0)) for _, right in terms]
    return pl.pallas_call(
        body,
        grid=(wide // step,),
        in_specs=lefts + rights,
        out_specs=pl.BlockSpec((step, columns), lambda i: (i, 0)),
        out_shape=jax.ShapeDtypeStruct((wide, columns), bf16),
        compiler_params=pltpu.CompilerParams(vmem_limit_bytes=48 * 1024 * 1024),
        cost_estimate=pl.CostEstimate(
            flops=2 * sum(left.shape[0] * right.shape[1] for left, right in terms) * wide,
            bytes_accessed=2 * (len(terms) * rows * wide + (rows + wide) * columns),
            transcendentals=0,
        ),
    )(*[left for left, _ in terms], *[right for _, right in terms])


def on_device(
    inputs,
    cotangent,
    seq_lengths,
    gains,
    gains_first,
    gains_second,
    conv_weight,
    conv_first,
    conv_second,
    in_weight,
    in_first,
    in_second,
    out_weight,
    out_first,
    out_second,
    gate_up,
    gate_up_first,
    gate_up_second,
    down_weight,
    down_first,
    down_second,
):
    tok_rows = inputs.shape[0]
    group_len = tok_rows * 8
    chan_len = conv_weight.shape[1] // 2
    rows_len = in_weight.shape[1]
    half = gate_up.shape[2] // 2
    wide = -(-half // 128) * 128
    mp_index = lax.axis_index(MP)
    zh = lax.axis_index("zh")

    resid = inputs.astype(f32)
    scale_one = lax.rsqrt(jnp.mean(resid * resid, axis=-1, keepdims=True) + norm_eps)
    unit_one = resid * scale_one
    normed_one = (unit_one * gains[0]).astype(bf16)

    def padded(block):
        return jnp.pad(block, ((0, 0), (0, wide - half)))

    own_in, away_in = halves(in_weight.astype(bf16), chan_len)
    own_out, away_out = halves(out_weight.astype(bf16).T, chan_len)
    own_down, away_down = halves(down_weight.astype(bf16).T, half)
    own, away = (
        jnp.concatenate([i[0], i[1], i[2], o, padded(d)], 1)
        for i, o, d in ((own_in, own_out, own_down), (away_in, away_out, away_down))
    )
    w_mix = lax.all_gather(joined(own, swapped(away, "zh"), 0), XY, axis=0, tiled=True)
    mix_cols = 4 * chan_len
    w_in, w_out = w_mix[:, : 3 * chan_len], w_mix[:, 3 * chan_len : mix_cols]
    w_down = w_mix[:, mix_cols:]
    own_gate, away_gate = halves(gate_up.astype(bf16), half)
    own, away = (jnp.concatenate([padded(g[0]), padded(g[1])], 1) for g in (own_gate, away_gate))
    gate_rows = joined(own, swapped(away, "zh"), 0)

    first_row = lax.axis_index(XY) * group_len
    place = positions(seq_lengths, first_row, group_len + 2)
    fwd_one = (place[:group_len] >= 1).astype(f32)[:, None]
    fwd_two = (place[:group_len] >= 2).astype(f32)[:, None]
    back_one = (place[1 : group_len + 1] >= 1).astype(f32)[:, None]
    back_two = (place[2:] >= 2).astype(f32)[:, None]

    own_rows = column_own(normed_one)
    own_rows, gate_rows, cotangent_sent = lax.optimization_barrier(
        (own_rows, gate_rows, cotangent)
    )
    w_gate_up = lax.all_gather(gate_rows, XY, axis=0, tiled=True)
    own_cot = column_own(cotangent_sent)
    group_in = by_place(own_rows, swapped(own_rows, "core"))
    lead = 16
    before = shifted(group_in[group_len - lead :], XY, 1)
    led_in = jnp.concatenate([before, group_in], 0)
    led_in, own_cot, fwd_one, fwd_two, back_one, back_two = lax.optimization_barrier(
        (led_in, own_cot, fwd_one, fwd_two, back_one, back_two)
    )
    column_cot = jnp.concatenate([own_cot, swapped(own_cot, "core")], 0)
    taps = halves(conv_weight, chan_len)[0]
    projected = dot(led_in, w_mix[:, :mix_cols], NN)
    proj_b = projected[lead:, :chan_len]
    proj_c = projected[lead:, chan_len : 2 * chan_len]
    proj_x = projected[lead:, 2 * chan_len : 3 * chan_len]
    extended = projected[:, :chan_len] * projected[:, 2 * chan_len : 3 * chan_len]
    gated = extended[lead:]
    one_back = extended[lead - 1 : lead - 1 + group_len] * fwd_one
    two_back = extended[lead - 2 : lead - 2 + group_len] * fwd_two
    convolved = taps[0] * gated + taps[1] * one_back + taps[2] * two_back
    mixed = (proj_c * convolved).astype(bf16)
    own_mixed, away_mixed = by_core(mixed)
    middle = resid + summed_over(core_summed((own_mixed, away_mixed), w_out, NT), RING, 4)
    grad_hidden = dot(column_cot, w_down, NN)
    middle, grad_hidden = lax.optimization_barrier((middle, grad_hidden))

    scale_two = lax.rsqrt(jnp.mean(middle * middle, axis=-1, keepdims=True) + norm_eps)
    unit_two = middle * scale_two
    normed_two = (unit_two * gains[1]).astype(bf16)
    own_mid = column_own(normed_two)
    column_mid = jnp.concatenate([own_mid, swapped(own_mid, "core")], 0)
    gate_vals = dot(column_mid, w_gate_up, NN)
    gate, up = gate_vals[:, :wide], gate_vals[:, wide:]
    sigma = jax.nn.sigmoid(gate)
    swish = gate * sigma
    hidden = (swish * up).astype(bf16)
    grad_gate = grad_hidden * up * sigma * (1.0 + gate * (1.0 - sigma))
    grad_up = grad_hidden * swish
    grad_pair = jnp.concatenate([grad_gate.astype(bf16), grad_up.astype(bf16)], 1)
    summed = core_summed(jnp.split(grad_pair, 2, 0), w_gate_up, NT)
    summed, grad_pair, hidden = lax.optimization_barrier((summed, grad_pair, hidden))
    grad_normed_two = summed_over(summed, RING, 4)
    grad_ff = weight_grads([[(column_mid, grad_pair)], [(column_cot, hidden)]])
    grad_normed_two, grad_ff = lax.optimization_barrier((grad_normed_two, grad_ff))
    grad_ff = lax.psum_scatter(grad_ff, XY, scatter_dimension=0, tiled=True)

    gain_two_part = jnp.sum(grad_normed_two * unit_two, axis=0)
    grad_unit_two = grad_normed_two * gains[1]
    grad_middle = cotangent.astype(f32) + scale_two * (
        grad_unit_two - unit_two * jnp.mean(grad_unit_two * unit_two, axis=-1, keepdims=True)
    )

    own_back = column_own(grad_middle.astype(bf16))
    ff_out = dot(hidden, w_down, NT).astype(bf16)
    own_back, ff_out = lax.optimization_barrier((own_back, ff_out))
    group_back = by_place(own_back, swapped(own_back, "core"))
    grad_mixed = dot(group_back, w_out, NN)
    grad_conv_out = grad_mixed * proj_c
    following = shifted(grad_conv_out[:2], XY, -1)
    grad_readout = (grad_mixed * convolved).astype(bf16)
    conv_part = jnp.stack(
        [
            jnp.sum(grad_conv_out * gated, axis=0),
            jnp.sum(grad_conv_out * one_back, axis=0),
            jnp.sum(grad_conv_out * two_back, axis=0),
        ]
    )
    ahead = jnp.concatenate([grad_conv_out, following], 0)
    grad_gated = (
        taps[0] * grad_conv_out
        + taps[1] * ahead[1 : group_len + 1] * back_one
        + taps[2] * ahead[2:] * back_two
    )
    grad_proj = jnp.concatenate(
        [
            (grad_gated * proj_x).astype(bf16),
            grad_readout,
            (grad_gated * proj_b).astype(bf16),
        ],
        1,
    )
    grad_mix = weight_grads([[(group_in, grad_proj)], [(group_back, mixed)]])
    grad_mix, grad_proj = lax.optimization_barrier((grad_mix, grad_proj))
    grad_mix = summed_over(grad_mix, XY, 16).astype(bf16)
    own, away = jnp.split(ff_out, 2, 0)
    ff_out = (own.astype(f32) + swapped(away, "core").astype(f32)).astype(bf16)
    grad_normed_one = dot(grad_proj, w_in, NT)
    gain_one_part = jnp.sum(grad_normed_one * group_in.astype(f32), axis=0) / gains[0]
    own, away = by_core(grad_normed_one.astype(bf16))
    own = (own.astype(f32) + swapped(away, "core").astype(f32)).astype(bf16)
    grad_normed_one = column_summed(own)
    block_out = (middle + column_summed(ff_out)).astype(bf16)

    def both(block):
        pair = block.reshape(2, rows_len, -1)
        return pick(pair, zh), swapped(pick(pair, 1 - zh), "zh")

    conv_full = lax.dynamic_update_slice(
        jnp.zeros((3, D), f32), conv_part, (jnp.int32(0), (2 * mp_index + zh) * chan_len)
    )
    small = jnp.concatenate([gain_one_part[None], gain_two_part[None], conv_full], 0)
    small = paired_sum(small, (("core", 1), ("zl", 1), ("zh", 1)))
    pair = grad_ff.reshape(2, rows_len, -1)
    own_ff, away_ff = pick(pair, zh), pick(pair, 1 - zh)
    away_ff, small, grad_mix = lax.optimization_barrier((away_ff, small, grad_mix))
    other_ff = swapped(away_ff, "zh")
    small = jnp.sum(spread(small, XY, 16), axis=0)
    gain_sum, conv_sum = small[:2], small[2:]

    grad_unit_one = grad_normed_one * gains[0]
    input_grad = grad_middle + scale_one * (
        grad_unit_one - unit_one * jnp.mean(grad_unit_one * unit_one, axis=-1, keepdims=True)
    )

    def spliced(pair, start, width):
        own, other = (block[:, start : start + width] for block in pair)
        return joined(own, other, 1).astype(f32)

    pair = both(grad_mix)
    grad_in = jnp.stack([spliced(pair, i * chan_len, chan_len) for i in range(3)])
    grad_out = spliced(pair, 3 * chan_len, chan_len).T
    pair = (own_ff, other_ff)
    grad_gate_up = jnp.stack([spliced(pair, i * wide, half) for i in range(2)])
    grad_down = spliced(pair, 2 * wide, half).T

    grad_taps = lax.dynamic_slice_in_dim(conv_sum, mp_index * 2 * chan_len, 2 * chan_len, 1)
    gains_set = adam(gains, gains_first, gains_second, gain_sum, 1.0, 0.0)
    conv_set = adam(conv_weight, conv_first, conv_second, grad_taps, 1.0, 0.0)
    in_set = adam(in_weight, in_first, in_second, grad_in, 2.0 * D ** (-0.5), weight_decay)
    out_set = adam(out_weight, out_first, out_second, grad_out, 2.0 * D ** (-0.5), weight_decay)
    gate_set = adam(
        gate_up, gate_up_first, gate_up_second, grad_gate_up, 2.0 * D ** (-0.5), weight_decay
    )
    down_set = adam(
        down_weight, down_first, down_second, grad_down, 2.0 * FF ** (-0.5), weight_decay
    )
    return (block_out, input_grad, *gains_set, *conv_set, *in_set, *out_set, *gate_set, *down_set)


def solution(mesh):
    parts = Mesh(mesh.devices.reshape(4, 4, 2, 2, 2), ("x", "y", "zh", "zl", "core"))
    tokens = P(DP + MP, None)
    taps = P(None, MP)
    wide_in = P(None, DP, MP)
    wide_out = P(MP, DP)
    in_specs = (
        (tokens,) * 2 + (P(),) * 4 + (taps,) * 3 + (wide_in,) * 3 + (wide_out,) * 3
        + (wide_in,) * 3 + (wide_out,) * 3
    )
    out_specs = (
        (tokens,) * 2 + (P(),) * 3 + (taps,) * 3 + (wide_in,) * 3 + (wide_out,) * 3
        + (wide_in,) * 3 + (wide_out,) * 3
    )
    return jax.shard_map(
        on_device, mesh=parts, in_specs=in_specs, out_specs=out_specs, check_vma=False
    )
```

```python
import jax
import jax.numpy as jnp
from jax import lax
from jax.experimental import pallas as pl
from jax.experimental.pallas import tpu as pltpu
from jax.sharding import Mesh
from jax.sharding import PartitionSpec as P

D = 1536
FF = 6912
STEP = 5

norm_eps = 1e-05
beta_one = 0.9
beta_two = 0.95
adam_eps = 1e-08
weight_decay = 0.1

bf16 = jnp.bfloat16
f32 = jnp.float32

XY = ("x", "y")
DP = ("x", "y", "zh")
MP = ("zl", "core")
RING = ("zh", "zl")
COL = ("zh", "zl", "core")


def positions(seq_lengths, first_row, count):
    ends = jnp.cumsum(seq_lengths)
    starts = ends - seq_lengths
    rows = first_row + jnp.arange(count, dtype=jnp.int32)
    covered = starts[None, :] <= rows[:, None]
    return rows - jnp.max(jnp.where(covered, starts[None, :], 0), axis=1)


def adam(weight, first, second, grad, rate, decay):
    first_new = beta_one * first + (1 - beta_one) * grad
    second_new = beta_two * second + (1 - beta_two) * grad * grad
    first_hat = first_new / (1 - beta_one**STEP)
    second_hat = second_new / (1 - beta_two**STEP)
    return (
        first_new,
        second_new,
        weight - rate * (first_hat / (jnp.sqrt(second_hat) + adam_eps) + decay * weight),
    )


def shifted(block, axes, distance):
    size = 1
    for axis in axes:
        size *= lax.axis_size(axis)
    route = [(i - distance, i) for i in range(size) if 0 <= i - distance < size]
    return lax.ppermute(block, axes, route)


def swapped(block, axis):
    return lax.ppermute(block, axis, [(0, 1), (1, 0)])


def exchanged(blocks, axes):
    return lax.all_to_all(blocks, axes, 0, 0, tiled=True)


def spread(block, axes, count):
    return exchanged(jnp.broadcast_to(block, (count, *block.shape)), axes)


def summed_over(block, axes, count):
    blocks = exchanged(block, axes).reshape(count, -1, *block.shape[1:])
    return jnp.sum(blocks.astype(f32), axis=0)


def from_others(blocks, axis):
    return [
        lax.ppermute(blocks[r], axis, [(i, (i + r) % 4) for i in range(4)]) for r in (1, 3, 2)
    ]


def ring_spread(block, axis):
    behind1, behind3, behind2 = from_others([block] * 4, axis)
    return jnp.stack([block, behind3, behind2, behind1])


def ring_summed(blocks, axis):
    total = blocks[0].astype(f32)
    for other in from_others(blocks, axis):
        total = total + other.astype(f32)
    return total


def rolled(blocks, shift):
    return jnp.stack([pick(blocks, (r - shift) % 4) for r in range(4)])


def column_own(block):
    return rolled(ring_spread(block, RING), lax.axis_index(RING)).reshape(-1, block.shape[1])


def column_summed(rows):
    return ring_summed(rolled(rows.reshape(4, -1, rows.shape[1]), -lax.axis_index(RING)), RING)


def by_place(own, other):
    own, other = (rows.reshape(4, -1, rows.shape[1]) for rows in (own, other))
    first = lax.axis_index("core") == 0
    rows = jnp.stack([jnp.where(first, own, other), jnp.where(first, other, own)], 1)
    return rows.reshape(-1, own.shape[2])


def by_core(rows):
    core = lax.axis_index("core")
    blocks = rows.reshape(4, 2, -1, rows.shape[1])
    return tuple(pick(blocks, c, 1).reshape(-1, rows.shape[1]) for c in (core, 1 - core))


def core_summed(left, right, dims):
    away = dot(left[1], right, dims).astype(bf16)
    away, own = lax.optimization_barrier((away, left[0]))
    own, away = lax.optimization_barrier((dot(own, right, dims), swapped(away, "core")))
    return (own + away.astype(f32)).astype(bf16)


def paired_sum(block, steps):
    for axis, bit in steps:
        route = [(i, i ^ bit) for i in range(lax.axis_size(axis))]
        block = block + lax.ppermute(block, axis, route)
    return block


def pick(blocks, index, axis=0):
    return lax.dynamic_index_in_dim(blocks, index, axis, keepdims=False)


def halves(block, width):
    low = lax.axis_index("zh") == 0
    first, last = block[..., :width], block[..., width:]
    return jnp.where(low, first, last), jnp.where(low, last, first)


def joined(own, other, axis):
    low = lax.axis_index("zh") == 0
    return jnp.where(
        low, jnp.concatenate([own, other], axis), jnp.concatenate([other, own], axis)
    )


def dot(left, right, dims):
    return lax.dot_general(left, right, ((dims[0], dims[1]), ((), ())), preferred_element_type=f32)


NN = ((1,), (0,))
NT = ((1,), (1,))
TN = ((0,), (0,))


def weight_grads(groups):
    rows, wide = groups[0][0][0].shape
    step = 512
    terms = [term for group in groups for term in group]
    count = len(terms)
    columns = sum(group[0][1].shape[1] for group in groups)

    def body(*refs):
        at, products = 0, []
        for group in groups:
            total = None
            for _ in group:
                product = dot(refs[at][...], refs[count + at][...], TN)
                total = product if total is None else total + product
                at += 1
            products.append(total.astype(bf16))
        refs[-1][...] = jnp.concatenate(products, 1)

    lefts = [pl.BlockSpec((left.shape[0], step), lambda i: (0, i)) for left, _ in terms]
    rights = [pl.BlockSpec(right.shape, lambda i: (0, 0)) for _, right in terms]
    return pl.pallas_call(
        body,
        grid=(wide // step,),
        in_specs=lefts + rights,
        out_specs=pl.BlockSpec((step, columns), lambda i: (i, 0)),
        out_shape=jax.ShapeDtypeStruct((wide, columns), bf16),
        compiler_params=pltpu.CompilerParams(vmem_limit_bytes=48 * 1024 * 1024),
        cost_estimate=pl.CostEstimate(
            flops=2 * sum(left.shape[0] * right.shape[1] for left, right in terms) * wide,
            bytes_accessed=2 * (len(terms) * rows * wide + (rows + wide) * columns),
            transcendentals=0,
        ),
    )(*[left for left, _ in terms], *[right for _, right in terms])


def on_device(
    inputs,
    cotangent,
    seq_lengths,
    gains,
    gains_first,
    gains_second,
    conv_weight,
    conv_first,
    conv_second,
    in_weight,
    in_first,
    in_second,
    out_weight,
    out_first,
    out_second,
    gate_up,
    gate_up_first,
    gate_up_second,
    down_weight,
    down_first,
    down_second,
):
    tok_rows = inputs.shape[0]
    group_len = tok_rows * 8
    chan_len = conv_weight.shape[1] // 2
    rows_len = in_weight.shape[1]
    half = gate_up.shape[2] // 2
    wide = -(-half // 128) * 128
    mp_index = lax.axis_index(MP)
    zh = lax.axis_index("zh")

    resid = inputs.astype(f32)
    scale_one = lax.rsqrt(jnp.mean(resid * resid, axis=-1, keepdims=True) + norm_eps)
    unit_one = resid * scale_one
    normed_one = (unit_one * gains[0]).astype(bf16)

    def padded(block):
        return jnp.pad(block, ((0, 0), (0, wide - half)))

    own_in, away_in = halves(in_weight.astype(bf16), chan_len)
    own_out, away_out = halves(out_weight.astype(bf16).T, chan_len)
    own_down, away_down = halves(down_weight.astype(bf16).T, half)
    own, away = (
        jnp.concatenate([i[0], i[1], i[2], o, padded(d)], 1)
        for i, o, d in ((own_in, own_out, own_down), (away_in, away_out, away_down))
    )
    w_mix = lax.all_gather(joined(own, swapped(away, "zh"), 0), XY, axis=0, tiled=True)
    mix_cols = 4 * chan_len
    w_in, w_out = w_mix[:, : 3 * chan_len], w_mix[:, 3 * chan_len : mix_cols]
    w_down = w_mix[:, mix_cols:]
    own_gate, away_gate = halves(gate_up.astype(bf16), half)
    own, away = (jnp.concatenate([padded(g[0]), padded(g[1])], 1) for g in (own_gate, away_gate))
    gate_rows = joined(own, swapped(away, "zh"), 0)

    first_row = lax.axis_index(XY) * group_len
    place = positions(seq_lengths, first_row, group_len + 2)
    fwd_one = (place[:group_len] >= 1).astype(f32)[:, None]
    fwd_two = (place[:group_len] >= 2).astype(f32)[:, None]
    back_one = (place[1 : group_len + 1] >= 1).astype(f32)[:, None]
    back_two = (place[2:] >= 2).astype(f32)[:, None]

    own_rows = column_own(normed_one)
    own_rows, gate_rows, cotangent_sent = lax.optimization_barrier(
        (own_rows, gate_rows, cotangent)
    )
    w_gate_up = lax.all_gather(gate_rows, XY, axis=0, tiled=True)
    own_cot = column_own(cotangent_sent)
    group_in = by_place(own_rows, swapped(own_rows, "core"))
    lead = 16
    before = shifted(group_in[group_len - lead :], XY, 1)
    led_in = jnp.concatenate([before, group_in], 0)
    led_in, own_cot, fwd_one, fwd_two, back_one, back_two = lax.optimization_barrier(
        (led_in, own_cot, fwd_one, fwd_two, back_one, back_two)
    )
    column_cot = jnp.concatenate([own_cot, swapped(own_cot, "core")], 0)
    taps = halves(conv_weight, chan_len)[0]
    projected = dot(led_in, w_mix[:, :mix_cols], NN)
    proj_b = projected[lead:, :chan_len]
    proj_c = projected[lead:, chan_len : 2 * chan_len]
    proj_x = projected[lead:, 2 * chan_len : 3 * chan_len]
    extended = projected[:, :chan_len] * projected[:, 2 * chan_len : 3 * chan_len]
    gated = extended[lead:]
    one_back = extended[lead - 1 : lead - 1 + group_len] * fwd_one
    two_back = extended[lead - 2 : lead - 2 + group_len] * fwd_two
    convolved = taps[0] * gated + taps[1] * one_back + taps[2] * two_back
    mixed = (proj_c * convolved).astype(bf16)
    own_mixed, away_mixed = by_core(mixed)
    middle = resid + summed_over(core_summed((own_mixed, away_mixed), w_out, NT), RING, 4)
    grad_hidden = dot(column_cot, w_down, NN)
    middle, grad_hidden = lax.optimization_barrier((middle, grad_hidden))

    scale_two = lax.rsqrt(jnp.mean(middle * middle, axis=-1, keepdims=True) + norm_eps)
    unit_two = middle * scale_two
    normed_two = (unit_two * gains[1]).astype(bf16)
    own_mid = column_own(normed_two)
    column_mid = jnp.concatenate([own_mid, swapped(own_mid, "core")], 0)
    gate_vals = dot(column_mid, w_gate_up, NN)
    gate, up = gate_vals[:, :wide], gate_vals[:, wide:]
    sigma = jax.nn.sigmoid(gate)
    swish = gate * sigma
    hidden = (swish * up).astype(bf16)
    grad_gate = grad_hidden * up * sigma * (1.0 + gate * (1.0 - sigma))
    grad_up = grad_hidden * swish
    grad_pair = jnp.concatenate([grad_gate.astype(bf16), grad_up.astype(bf16)], 1)
    summed = core_summed(jnp.split(grad_pair, 2, 0), w_gate_up, NT)
    summed, grad_pair, hidden = lax.optimization_barrier((summed, grad_pair, hidden))
    grad_normed_two = summed_over(summed, RING, 4)
    grad_ff = weight_grads([[(column_mid, grad_pair)], [(column_cot, hidden)]])
    grad_normed_two, grad_ff = lax.optimization_barrier((grad_normed_two, grad_ff))
    grad_ff = lax.psum_scatter(grad_ff, XY, scatter_dimension=0, tiled=True)

    gain_two_part = jnp.sum(grad_normed_two * unit_two, axis=0)
    grad_unit_two = grad_normed_two * gains[1]
    grad_middle = cotangent.astype(f32) + scale_two * (
        grad_unit_two - unit_two * jnp.mean(grad_unit_two * unit_two, axis=-1, keepdims=True)
    )

    own_back = column_own(grad_middle.astype(bf16))
    ff_out = dot(hidden, w_down, NT).astype(bf16)
    own_back, ff_out = lax.optimization_barrier((own_back, ff_out))
    group_back = by_place(own_back, swapped(own_back, "core"))
    grad_mixed = dot(group_back, w_out, NN)
    grad_conv_out = grad_mixed * proj_c
    following = shifted(grad_conv_out[:2], XY, -1)
    grad_readout = (grad_mixed * convolved).astype(bf16)
    conv_part = jnp.stack(
        [
            jnp.sum(grad_conv_out * gated, axis=0),
            jnp.sum(grad_conv_out * one_back, axis=0),
            jnp.sum(grad_conv_out * two_back, axis=0),
        ]
    )
    ahead = jnp.concatenate([grad_conv_out, following], 0)
    grad_gated = (
        taps[0] * grad_conv_out
        + taps[1] * ahead[1 : group_len + 1] * back_one
        + taps[2] * ahead[2:] * back_two
    )
    grad_proj = jnp.concatenate(
        [
            (grad_gated * proj_x).astype(bf16),
            grad_readout,
            (grad_gated * proj_b).astype(bf16),
        ],
        1,
    )
    grad_mix = weight_grads([[(group_in, grad_proj)], [(group_back, mixed)]])
    grad_mix, grad_proj = lax.optimization_barrier((grad_mix, grad_proj))
    grad_mix = summed_over(grad_mix, XY, 16).astype(bf16)
    own, away = jnp.split(ff_out, 2, 0)
    ff_out = (own.astype(f32) + swapped(away, "core").astype(f32)).astype(bf16)
    grad_normed_one = dot(grad_proj, w_in, NT)
    gain_one_part = jnp.sum(grad_normed_one * group_in.astype(f32), axis=0) / gains[0]
    own, away = by_core(grad_normed_one.astype(bf16))
    own = (own.astype(f32) + swapped(away, "core").astype(f32)).astype(bf16)
    grad_normed_one = column_summed(own)
    block_out = (middle + column_summed(ff_out)).astype(bf16)

    def both(block):
        pair = block.reshape(2, rows_len, -1)
        return pick(pair, zh), swapped(pick(pair, 1 - zh), "zh")

    conv_full = lax.dynamic_update_slice(
        jnp.zeros((3, D), f32), conv_part, (jnp.int32(0), (2 * mp_index + zh) * chan_len)
    )
    small = jnp.concatenate([gain_one_part[None], gain_two_part[None], conv_full], 0)
    small = paired_sum(small, (("core", 1), ("zl", 1), ("zh", 1)))
    pair = grad_ff.reshape(2, rows_len, -1)
    own_ff, away_ff = pick(pair, zh), pick(pair, 1 - zh)
    small, grad_mix = lax.optimization_barrier((small, grad_mix))
    small = jnp.sum(spread(small, XY, 16), axis=0)
    away_ff, grad_mix = lax.optimization_barrier((away_ff, grad_mix))
    other_ff = swapped(away_ff, "zh")
    gain_sum, conv_sum = small[:2], small[2:]

    grad_unit_one = grad_normed_one * gains[0]
    input_grad = grad_middle + scale_one * (
        grad_unit_one - unit_one * jnp.mean(grad_unit_one * unit_one, axis=-1, keepdims=True)
    )

    def spliced(pair, start, width):
        own, other = (block[:, start : start + width] for block in pair)
        return joined(own, other, 1).astype(f32)

    pair = both(grad_mix)
    grad_in = jnp.stack([spliced(pair, i * chan_len, chan_len) for i in range(3)])
    grad_out = spliced(pair, 3 * chan_len, chan_len).T
    pair = (own_ff, other_ff)
    grad_gate_up = jnp.stack([spliced(pair, i * wide, half) for i in range(2)])
    grad_down = spliced(pair, 2 * wide, half).T

    grad_taps = lax.dynamic_slice_in_dim(conv_sum, mp_index * 2 * chan_len, 2 * chan_len, 1)
    gains_set = adam(gains, gains_first, gains_second, gain_sum, 1.0, 0.0)
    conv_set = adam(conv_weight, conv_first, conv_second, grad_taps, 1.0, 0.0)
    in_set = adam(in_weight, in_first, in_second, grad_in, 2.0 * D ** (-0.5), weight_decay)
    out_set = adam(out_weight, out_first, out_second, grad_out, 2.0 * D ** (-0.5), weight_decay)
    gate_set = adam(
        gate_up, gate_up_first, gate_up_second, grad_gate_up, 2.0 * D ** (-0.5), weight_decay
    )
    down_set = adam(
        down_weight, down_first, down_second, grad_down, 2.0 * FF ** (-0.5), weight_decay
    )
    return (block_out, input_grad, *gains_set, *conv_set, *in_set, *out_set, *gate_set, *down_set)


def solution(mesh):
    parts = Mesh(mesh.devices.reshape(4, 4, 2, 2, 2), ("x", "y", "zh", "zl", "core"))
    tokens = P(DP + MP, None)
    taps = P(None, MP)
    wide_in = P(None, DP, MP)
    wide_out = P(MP, DP)
    in_specs = (
        (tokens,) * 2 + (P(),) * 4 + (taps,) * 3 + (wide_in,) * 3 + (wide_out,) * 3
        + (wide_in,) * 3 + (wide_out,) * 3
    )
    out_specs = (
        (tokens,) * 2 + (P(),) * 3 + (taps,) * 3 + (wide_in,) * 3 + (wide_out,) * 3
        + (wide_in,) * 3 + (wide_out,) * 3
    )
    return jax.shard_map(
        on_device, mesh=parts, in_specs=in_specs, out_specs=out_specs, check_vma=False
    )
```

```python
import jax
import jax.numpy as jnp
from jax import lax
from jax.experimental import pallas as pl
from jax.experimental.pallas import tpu as pltpu
from jax.sharding import Mesh
from jax.sharding import PartitionSpec as P

D = 1536
FF = 6912
STEP = 5

norm_eps = 1e-05
beta_one = 0.9
beta_two = 0.95
adam_eps = 1e-08
weight_decay = 0.1

bf16 = jnp.bfloat16
f32 = jnp.float32

XY = ("x", "y")
DP = ("x", "y", "zh")
MP = ("zl", "core")
RING = ("zh", "zl")
COL = ("zh", "zl", "core")


def positions(seq_lengths, first_row, count):
    ends = jnp.cumsum(seq_lengths)
    starts = ends - seq_lengths
    rows = first_row + jnp.arange(count, dtype=jnp.int32)
    covered = starts[None, :] <= rows[:, None]
    return rows - jnp.max(jnp.where(covered, starts[None, :], 0), axis=1)


def adam(weight, first, second, grad, rate, decay):
    first_new = beta_one * first + (1 - beta_one) * grad
    second_new = beta_two * second + (1 - beta_two) * grad * grad
    first_hat = first_new / (1 - beta_one**STEP)
    second_hat = second_new / (1 - beta_two**STEP)
    return (
        first_new,
        second_new,
        weight - rate * (first_hat / (jnp.sqrt(second_hat) + adam_eps) + decay * weight),
    )


def shifted(block, axes, distance):
    size = 1
    for axis in axes:
        size *= lax.axis_size(axis)
    route = [(i - distance, i) for i in range(size) if 0 <= i - distance < size]
    return lax.ppermute(block, axes, route)


def swapped(block, axis):
    return lax.ppermute(block, axis, [(0, 1), (1, 0)])


def exchanged(blocks, axes):
    return lax.all_to_all(blocks, axes, 0, 0, tiled=True)


def spread(block, axes, count):
    return exchanged(jnp.broadcast_to(block, (count, *block.shape)), axes)


def summed_over(block, axes, count):
    blocks = exchanged(block, axes).reshape(count, -1, *block.shape[1:])
    return jnp.sum(blocks.astype(f32), axis=0)


def from_others(blocks, axis):
    return [
        lax.ppermute(blocks[r], axis, [(i, (i + r) % 4) for i in range(4)]) for r in (1, 3, 2)
    ]


def ring_spread(block, axis):
    behind1, behind3, behind2 = from_others([block] * 4, axis)
    return jnp.stack([block, behind3, behind2, behind1])


def ring_summed(blocks, axis):
    total = blocks[0].astype(f32)
    for other in from_others(blocks, axis):
        total = total + other.astype(f32)
    return total


def rolled(blocks, shift):
    return jnp.stack([pick(blocks, (r - shift) % 4) for r in range(4)])


def column_own(block):
    return rolled(ring_spread(block, RING), lax.axis_index(RING)).reshape(-1, block.shape[1])


def column_summed(rows):
    return ring_summed(rolled(rows.reshape(4, -1, rows.shape[1]), -lax.axis_index(RING)), RING)


def by_place(own, other):
    own, other = (rows.reshape(4, -1, rows.shape[1]) for rows in (own, other))
    first = lax.axis_index("core") == 0
    rows = jnp.stack([jnp.where(first, own, other), jnp.where(first, other, own)], 1)
    return rows.reshape(-1, own.shape[2])


def by_core(rows):
    core = lax.axis_index("core")
    blocks = rows.reshape(4, 2, -1, rows.shape[1])
    return tuple(pick(blocks, c, 1).reshape(-1, rows.shape[1]) for c in (core, 1 - core))


def core_summed(left, right, dims):
    away = dot(left[1], right, dims).astype(bf16)
    away, own = lax.optimization_barrier((away, left[0]))
    own, away = lax.optimization_barrier((dot(own, right, dims), swapped(away, "core")))
    return (own + away.astype(f32)).astype(bf16)


def paired_sum(block, steps):
    for axis, bit in steps:
        route = [(i, i ^ bit) for i in range(lax.axis_size(axis))]
        block = block + lax.ppermute(block, axis, route)
    return block


def pick(blocks, index, axis=0):
    return lax.dynamic_index_in_dim(blocks, index, axis, keepdims=False)


def halves(block, width):
    low = lax.axis_index("zh") == 0
    first, last = block[..., :width], block[..., width:]
    return jnp.where(low, first, last), jnp.where(low, last, first)


def joined(own, other, axis):
    low = lax.axis_index("zh") == 0
    return jnp.where(
        low, jnp.concatenate([own, other], axis), jnp.concatenate([other, own], axis)
    )


def dot(left, right, dims):
    return lax.dot_general(left, right, ((dims[0], dims[1]), ((), ())), preferred_element_type=f32)


NN = ((1,), (0,))
NT = ((1,), (1,))
TN = ((0,), (0,))


def weight_grads(groups):
    rows, wide = groups[0][0][0].shape
    step = 512
    terms = [term for group in groups for term in group]
    count = len(terms)
    columns = sum(group[0][1].shape[1] for group in groups)

    def body(*refs):
        at, products = 0, []
        for group in groups:
            total = None
            for _ in group:
                product = dot(refs[at][...], refs[count + at][...], TN)
                total = product if total is None else total + product
                at += 1
            products.append(total.astype(bf16))
        refs[-1][...] = jnp.concatenate(products, 1)

    lefts = [pl.BlockSpec((left.shape[0], step), lambda i: (0, i)) for left, _ in terms]
    rights = [pl.BlockSpec(right.shape, lambda i: (0, 0)) for _, right in terms]
    return pl.pallas_call(
        body,
        grid=(wide // step,),
        in_specs=lefts + rights,
        out_specs=pl.BlockSpec((step, columns), lambda i: (i, 0)),
        out_shape=jax.ShapeDtypeStruct((wide, columns), bf16),
        compiler_params=pltpu.CompilerParams(vmem_limit_bytes=48 * 1024 * 1024),
        cost_estimate=pl.CostEstimate(
            flops=2 * sum(left.shape[0] * right.shape[1] for left, right in terms) * wide,
            bytes_accessed=2 * (len(terms) * rows * wide + (rows + wide) * columns),
            transcendentals=0,
        ),
    )(*[left for left, _ in terms], *[right for _, right in terms])


def on_device(
    inputs,
    cotangent,
    seq_lengths,
    gains,
    gains_first,
    gains_second,
    conv_weight,
    conv_first,
    conv_second,
    in_weight,
    in_first,
    in_second,
    out_weight,
    out_first,
    out_second,
    gate_up,
    gate_up_first,
    gate_up_second,
    down_weight,
    down_first,
    down_second,
):
    tok_rows = inputs.shape[0]
    group_len = tok_rows * 8
    chan_len = conv_weight.shape[1] // 2
    rows_len = in_weight.shape[1]
    half = gate_up.shape[2] // 2
    wide = -(-half // 128) * 128
    mp_index = lax.axis_index(MP)
    zh = lax.axis_index("zh")

    resid = inputs.astype(f32)
    scale_one = lax.rsqrt(jnp.mean(resid * resid, axis=-1, keepdims=True) + norm_eps)
    unit_one = resid * scale_one
    normed_one = (unit_one * gains[0]).astype(bf16)

    def padded(block):
        return jnp.pad(block, ((0, 0), (0, wide - half)))

    own_in, away_in = halves(in_weight.astype(bf16), chan_len)
    own_out, away_out = halves(out_weight.astype(bf16).T, chan_len)
    own_down, away_down = halves(down_weight.astype(bf16).T, half)
    own, away = (
        jnp.concatenate([i[0], i[1], i[2], o, padded(d)], 1)
        for i, o, d in ((own_in, own_out, own_down), (away_in, away_out, away_down))
    )
    w_mix = lax.all_gather(joined(own, swapped(away, "zh"), 0), XY, axis=0, tiled=True)
    mix_cols = 4 * chan_len
    w_in, w_out = w_mix[:, : 3 * chan_len], w_mix[:, 3 * chan_len : mix_cols]
    w_down = w_mix[:, mix_cols:]
    own_gate, away_gate = halves(gate_up.astype(bf16), half)
    own, away = (jnp.concatenate([padded(g[0]), padded(g[1])], 1) for g in (own_gate, away_gate))
    gate_rows = joined(own, swapped(away, "zh"), 0)

    first_row = lax.axis_index(XY) * group_len
    place = positions(seq_lengths, first_row, group_len + 2)
    fwd_one = (place[:group_len] >= 1).astype(f32)[:, None]
    fwd_two = (place[:group_len] >= 2).astype(f32)[:, None]
    back_one = (place[1 : group_len + 1] >= 1).astype(f32)[:, None]
    back_two = (place[2:] >= 2).astype(f32)[:, None]

    own_rows = column_own(normed_one)
    own_rows, gate_rows, cotangent_sent = lax.optimization_barrier(
        (own_rows, gate_rows, cotangent)
    )
    w_gate_up = lax.all_gather(gate_rows, XY, axis=0, tiled=True)
    own_cot = column_own(cotangent_sent)
    group_in = by_place(own_rows, swapped(own_rows, "core"))
    lead = 16
    before = shifted(group_in[group_len - lead :], XY, 1)
    led_in = jnp.concatenate([before, group_in], 0)
    led_in, own_cot, fwd_one, fwd_two, back_one, back_two = lax.optimization_barrier(
        (led_in, own_cot, fwd_one, fwd_two, back_one, back_two)
    )
    column_cot = jnp.concatenate([own_cot, swapped(own_cot, "core")], 0)
    taps = halves(conv_weight, chan_len)[0]
    projected = dot(led_in, w_mix[:, :mix_cols], NN)
    proj_b = projected[lead:, :chan_len]
    proj_c = projected[lead:, chan_len : 2 * chan_len]
    proj_x = projected[lead:, 2 * chan_len : 3 * chan_len]
    extended = projected[:, :chan_len] * projected[:, 2 * chan_len : 3 * chan_len]
    gated = extended[lead:]
    one_back = extended[lead - 1 : lead - 1 + group_len] * fwd_one
    two_back = extended[lead - 2 : lead - 2 + group_len] * fwd_two
    convolved = taps[0] * gated + taps[1] * one_back + taps[2] * two_back
    mixed = (proj_c * convolved).astype(bf16)
    own_mixed, away_mixed = by_core(mixed)
    middle = resid + summed_over(core_summed((own_mixed, away_mixed), w_out, NT), RING, 4)
    grad_hidden = dot(column_cot, w_down, NN)
    middle, grad_hidden = lax.optimization_barrier((middle, grad_hidden))

    scale_two = lax.rsqrt(jnp.mean(middle * middle, axis=-1, keepdims=True) + norm_eps)
    unit_two = middle * scale_two
    normed_two = (unit_two * gains[1]).astype(bf16)
    own_mid = column_own(normed_two)
    column_mid = jnp.concatenate([own_mid, swapped(own_mid, "core")], 0)
    gate_vals = dot(column_mid, w_gate_up, NN)
    gate, up = gate_vals[:, :wide], gate_vals[:, wide:]
    sigma = jax.nn.sigmoid(gate)
    swish = gate * sigma
    hidden = (swish * up).astype(bf16)
    grad_gate = grad_hidden * up * sigma * (1.0 + gate * (1.0 - sigma))
    grad_up = grad_hidden * swish
    grad_pair = jnp.concatenate([grad_gate.astype(bf16), grad_up.astype(bf16)], 1)
    summed = core_summed(jnp.split(grad_pair, 2, 0), w_gate_up, NT)
    summed, grad_pair, hidden = lax.optimization_barrier((summed, grad_pair, hidden))
    grad_normed_two = summed_over(summed, RING, 4)
    grad_ff = weight_grads([[(column_mid, grad_pair)], [(column_cot, hidden)]])
    grad_normed_two, grad_ff = lax.optimization_barrier((grad_normed_two, grad_ff))
    grad_ff = lax.psum_scatter(grad_ff, XY, scatter_dimension=0, tiled=True)

    gain_two_part = jnp.sum(grad_normed_two * unit_two, axis=0)
    grad_unit_two = grad_normed_two * gains[1]
    grad_middle = cotangent.astype(f32) + scale_two * (
        grad_unit_two - unit_two * jnp.mean(grad_unit_two * unit_two, axis=-1, keepdims=True)
    )

    own_back = column_own(grad_middle.astype(bf16))
    ff_out = dot(hidden, w_down, NT).astype(bf16)
    own_back, ff_out = lax.optimization_barrier((own_back, ff_out))
    group_back = by_place(own_back, swapped(own_back, "core"))
    grad_mixed = dot(group_back, w_out, NN)
    grad_conv_out = grad_mixed * proj_c
    following = shifted(grad_conv_out[:2], XY, -1)
    grad_readout = (grad_mixed * convolved).astype(bf16)
    conv_part = jnp.stack(
        [
            jnp.sum(grad_conv_out * gated, axis=0),
            jnp.sum(grad_conv_out * one_back, axis=0),
            jnp.sum(grad_conv_out * two_back, axis=0),
        ]
    )
    ahead = jnp.concatenate([grad_conv_out, following], 0)
    grad_gated = (
        taps[0] * grad_conv_out
        + taps[1] * ahead[1 : group_len + 1] * back_one
        + taps[2] * ahead[2:] * back_two
    )
    grad_proj = jnp.concatenate(
        [
            (grad_gated * proj_x).astype(bf16),
            grad_readout,
            (grad_gated * proj_b).astype(bf16),
        ],
        1,
    )
    grad_mix = weight_grads([[(group_in, grad_proj)], [(group_back, mixed)]])
    grad_mix, grad_proj = lax.optimization_barrier((grad_mix, grad_proj))
    grad_mix = summed_over(grad_mix, XY, 16).astype(bf16)
    own, away = jnp.split(ff_out, 2, 0)
    ff_out = (own.astype(f32) + swapped(away, "core").astype(f32)).astype(bf16)
    ff_blocks = rolled(ff_out.reshape(4, tok_rows, D), -lax.axis_index(RING))
    ff_others = from_others(ff_blocks, RING)
    grad_normed_one = dot(grad_proj, w_in, NT)
    gain_one_part = jnp.sum(grad_normed_one * group_in.astype(f32), axis=0) / gains[0]
    own, away = by_core(grad_normed_one.astype(bf16))
    own = (own.astype(f32) + swapped(away, "core").astype(f32)).astype(bf16)
    grad_normed_one = column_summed(own)

    def both(block):
        pair = block.reshape(2, rows_len, -1)
        return pick(pair, zh), swapped(pick(pair, 1 - zh), "zh")

    conv_full = lax.dynamic_update_slice(
        jnp.zeros((3, D), f32), conv_part, (jnp.int32(0), (2 * mp_index + zh) * chan_len)
    )
    small = jnp.concatenate([gain_one_part[None], gain_two_part[None], conv_full], 0)
    small = paired_sum(small, (("core", 1), ("zl", 1), ("zh", 1)))
    pair = grad_ff.reshape(2, rows_len, -1)
    own_ff, away_ff = pick(pair, zh), pick(pair, 1 - zh)
    away_ff, small, grad_mix = lax.optimization_barrier((away_ff, small, grad_mix))
    other_ff, *ff_others = lax.optimization_barrier((swapped(away_ff, "zh"), *ff_others))
    block_out = middle + ff_blocks[0].astype(f32)
    for other in ff_others:
        block_out = block_out + other.astype(f32)
    block_out = block_out.astype(bf16)
    small = jnp.sum(spread(small, XY, 16), axis=0)
    gain_sum, conv_sum = small[:2], small[2:]

    grad_unit_one = grad_normed_one * gains[0]
    input_grad = grad_middle + scale_one * (
        grad_unit_one - unit_one * jnp.mean(grad_unit_one * unit_one, axis=-1, keepdims=True)
    )

    def spliced(pair, start, width):
        own, other = (block[:, start : start + width] for block in pair)
        return joined(own, other, 1).astype(f32)

    pair = both(grad_mix)
    grad_in = jnp.stack([spliced(pair, i * chan_len, chan_len) for i in range(3)])
    grad_out = spliced(pair, 3 * chan_len, chan_len).T
    pair = (own_ff, other_ff)
    grad_gate_up = jnp.stack([spliced(pair, i * wide, half) for i in range(2)])
    grad_down = spliced(pair, 2 * wide, half).T

    grad_taps = lax.dynamic_slice_in_dim(conv_sum, mp_index * 2 * chan_len, 2 * chan_len, 1)
    gains_set = adam(gains, gains_first, gains_second, gain_sum, 1.0, 0.0)
    conv_set = adam(conv_weight, conv_first, conv_second, grad_taps, 1.0, 0.0)
    in_set = adam(in_weight, in_first, in_second, grad_in, 2.0 * D ** (-0.5), weight_decay)
    out_set = adam(out_weight, out_first, out_second, grad_out, 2.0 * D ** (-0.5), weight_decay)
    gate_set = adam(
        gate_up, gate_up_first, gate_up_second, grad_gate_up, 2.0 * D ** (-0.5), weight_decay
    )
    down_set = adam(
        down_weight, down_first, down_second, grad_down, 2.0 * FF ** (-0.5), weight_decay
    )
    return (block_out, input_grad, *gains_set, *conv_set, *in_set, *out_set, *gate_set, *down_set)


def solution(mesh):
    parts = Mesh(mesh.devices.reshape(4, 4, 2, 2, 2), ("x", "y", "zh", "zl", "core"))
    tokens = P(DP + MP, None)
    taps = P(None, MP)
    wide_in = P(None, DP, MP)
    wide_out = P(MP, DP)
    in_specs = (
        (tokens,) * 2 + (P(),) * 4 + (taps,) * 3 + (wide_in,) * 3 + (wide_out,) * 3
        + (wide_in,) * 3 + (wide_out,) * 3
    )
    out_specs = (
        (tokens,) * 2 + (P(),) * 3 + (taps,) * 3 + (wide_in,) * 3 + (wide_out,) * 3
        + (wide_in,) * 3 + (wide_out,) * 3
    )
    return jax.shard_map(
        on_device, mesh=parts, in_specs=in_specs, out_specs=out_specs, check_vma=False
    )
```

```python
import jax
import jax.numpy as jnp
from jax import lax
from jax.experimental import pallas as pl
from jax.experimental.pallas import tpu as pltpu
from jax.sharding import Mesh
from jax.sharding import PartitionSpec as P

D = 1536
FF = 6912
STEP = 5

norm_eps = 1e-05
beta_one = 0.9
beta_two = 0.95
adam_eps = 1e-08
weight_decay = 0.1

bf16 = jnp.bfloat16
f32 = jnp.float32

XY = ("x", "y")
DP = ("x", "y", "zh")
MP = ("zl", "core")
RING = ("zh", "zl")
COL = ("zh", "zl", "core")


def positions(seq_lengths, first_row, count):
    ends = jnp.cumsum(seq_lengths)
    starts = ends - seq_lengths
    rows = first_row + jnp.arange(count, dtype=jnp.int32)
    covered = starts[None, :] <= rows[:, None]
    return rows - jnp.max(jnp.where(covered, starts[None, :], 0), axis=1)


def adam(weight, first, second, grad, rate, decay):
    first_new = beta_one * first + (1 - beta_one) * grad
    second_new = beta_two * second + (1 - beta_two) * grad * grad
    first_hat = first_new / (1 - beta_one**STEP)
    second_hat = second_new / (1 - beta_two**STEP)
    return (
        first_new,
        second_new,
        weight - rate * (first_hat / (jnp.sqrt(second_hat) + adam_eps) + decay * weight),
    )


def shifted(block, axes, distance):
    size = 1
    for axis in axes:
        size *= lax.axis_size(axis)
    route = [(i - distance, i) for i in range(size) if 0 <= i - distance < size]
    return lax.ppermute(block, axes, route)


def swapped(block, axis):
    return lax.ppermute(block, axis, [(0, 1), (1, 0)])


def exchanged(blocks, axes):
    return lax.all_to_all(blocks, axes, 0, 0, tiled=True)


def spread(block, axes, count):
    return exchanged(jnp.broadcast_to(block, (count, *block.shape)), axes)


def summed_over(block, axes, count):
    blocks = exchanged(block, axes).reshape(count, -1, *block.shape[1:])
    return jnp.sum(blocks.astype(f32), axis=0)


def from_others(blocks, axis):
    return [
        lax.ppermute(blocks[r], axis, [(i, (i + r) % 4) for i in range(4)]) for r in (1, 3, 2)
    ]


def ring_spread(block, axis):
    behind1, behind3, behind2 = from_others([block] * 4, axis)
    return jnp.stack([block, behind3, behind2, behind1])


def ring_summed(blocks, axis):
    total = blocks[0].astype(f32)
    for other in from_others(blocks, axis):
        total = total + other.astype(f32)
    return total


def rolled(blocks, shift):
    return jnp.stack([pick(blocks, (r - shift) % 4) for r in range(4)])


def column_own(block):
    return rolled(ring_spread(block, RING), lax.axis_index(RING)).reshape(-1, block.shape[1])


def column_summed(rows):
    return ring_summed(rolled(rows.reshape(4, -1, rows.shape[1]), -lax.axis_index(RING)), RING)


def by_place(own, other):
    own, other = (rows.reshape(4, -1, rows.shape[1]) for rows in (own, other))
    first = lax.axis_index("core") == 0
    rows = jnp.stack([jnp.where(first, own, other), jnp.where(first, other, own)], 1)
    return rows.reshape(-1, own.shape[2])


def by_core(rows):
    core = lax.axis_index("core")
    blocks = rows.reshape(4, 2, -1, rows.shape[1])
    return tuple(pick(blocks, c, 1).reshape(-1, rows.shape[1]) for c in (core, 1 - core))


def core_summed(left, right, dims):
    away = dot(left[1], right, dims).astype(bf16)
    away, own = lax.optimization_barrier((away, left[0]))
    own, away = lax.optimization_barrier((dot(own, right, dims), swapped(away, "core")))
    return (own + away.astype(f32)).astype(bf16)


def paired_sum(block, steps):
    for axis, bit in steps:
        route = [(i, i ^ bit) for i in range(lax.axis_size(axis))]
        block = block + lax.ppermute(block, axis, route)
    return block


def pick(blocks, index, axis=0):
    return lax.dynamic_index_in_dim(blocks, index, axis, keepdims=False)


def halves(block, width):
    low = lax.axis_index("zh") == 0
    first, last = block[..., :width], block[..., width:]
    return jnp.where(low, first, last), jnp.where(low, last, first)


def joined(own, other, axis):
    low = lax.axis_index("zh") == 0
    return jnp.where(
        low, jnp.concatenate([own, other], axis), jnp.concatenate([other, own], axis)
    )


def dot(left, right, dims):
    return lax.dot_general(left, right, ((dims[0], dims[1]), ((), ())), preferred_element_type=f32)


NN = ((1,), (0,))
NT = ((1,), (1,))
TN = ((0,), (0,))


def weight_grads(groups):
    rows, wide = groups[0][0][0].shape
    step = 512
    terms = [term for group in groups for term in group]
    count = len(terms)
    columns = sum(group[0][1].shape[1] for group in groups)

    def body(*refs):
        at, products = 0, []
        for group in groups:
            total = None
            for _ in group:
                product = dot(refs[at][...], refs[count + at][...], TN)
                total = product if total is None else total + product
                at += 1
            products.append(total.astype(bf16))
        refs[-1][...] = jnp.concatenate(products, 1)

    lefts = [pl.BlockSpec((left.shape[0], step), lambda i: (0, i)) for left, _ in terms]
    rights = [pl.BlockSpec(right.shape, lambda i: (0, 0)) for _, right in terms]
    return pl.pallas_call(
        body,
        grid=(wide // step,),
        in_specs=lefts + rights,
        out_specs=pl.BlockSpec((step, columns), lambda i: (i, 0)),
        out_shape=jax.ShapeDtypeStruct((wide, columns), bf16),
        compiler_params=pltpu.CompilerParams(vmem_limit_bytes=48 * 1024 * 1024),
        cost_estimate=pl.CostEstimate(
            flops=2 * sum(left.shape[0] * right.shape[1] for left, right in terms) * wide,
            bytes_accessed=2 * (len(terms) * rows * wide + (rows + wide) * columns),
            transcendentals=0,
        ),
    )(*[left for left, _ in terms], *[right for _, right in terms])


def on_device(
    inputs,
    cotangent,
    seq_lengths,
    gains,
    gains_first,
    gains_second,
    conv_weight,
    conv_first,
    conv_second,
    in_weight,
    in_first,
    in_second,
    out_weight,
    out_first,
    out_second,
    gate_up,
    gate_up_first,
    gate_up_second,
    down_weight,
    down_first,
    down_second,
):
    tok_rows = inputs.shape[0]
    group_len = tok_rows * 8
    chan_len = conv_weight.shape[1] // 2
    rows_len = in_weight.shape[1]
    half = gate_up.shape[2] // 2
    wide = -(-half // 128) * 128
    mp_index = lax.axis_index(MP)
    zh = lax.axis_index("zh")

    resid = inputs.astype(f32)
    scale_one = lax.rsqrt(jnp.mean(resid * resid, axis=-1, keepdims=True) + norm_eps)
    unit_one = resid * scale_one
    normed_one = (unit_one * gains[0]).astype(bf16)

    def padded(block):
        return jnp.pad(block, ((0, 0), (0, wide - half)))

    own_in, away_in = halves(in_weight.astype(bf16), chan_len)
    own_out, away_out = halves(out_weight.astype(bf16).T, chan_len)
    own_down, away_down = halves(down_weight.astype(bf16).T, half)
    own, away = (
        jnp.concatenate([i[0], i[1], i[2], o, padded(d)], 1)
        for i, o, d in ((own_in, own_out, own_down), (away_in, away_out, away_down))
    )
    w_mix = lax.all_gather(joined(own, swapped(away, "zh"), 0), XY, axis=0, tiled=True)
    mix_cols = 4 * chan_len
    w_in, w_out = w_mix[:, : 3 * chan_len], w_mix[:, 3 * chan_len : mix_cols]
    w_down = w_mix[:, mix_cols:]
    own_gate, away_gate = halves(gate_up.astype(bf16), half)
    own, away = (jnp.concatenate([padded(g[0]), padded(g[1])], 1) for g in (own_gate, away_gate))
    gate_rows = joined(own, swapped(away, "zh"), 0)

    first_row = lax.axis_index(XY) * group_len
    place = positions(seq_lengths, first_row, group_len + 2)
    fwd_one = (place[:group_len] >= 1).astype(f32)[:, None]
    fwd_two = (place[:group_len] >= 2).astype(f32)[:, None]
    back_one = (place[1 : group_len + 1] >= 1).astype(f32)[:, None]
    back_two = (place[2:] >= 2).astype(f32)[:, None]

    own_rows = column_own(normed_one)
    own_rows, gate_rows, cotangent_sent = lax.optimization_barrier(
        (own_rows, gate_rows, cotangent)
    )
    w_gate_up = lax.all_gather(gate_rows, XY, axis=0, tiled=True)
    own_cot = column_own(cotangent_sent)
    group_in = by_place(own_rows, swapped(own_rows, "core"))
    lead = 16
    before = shifted(group_in[group_len - lead :], XY, 1)
    led_in = jnp.concatenate([before, group_in], 0)
    led_in, own_cot, fwd_one, fwd_two, back_one, back_two = lax.optimization_barrier(
        (led_in, own_cot, fwd_one, fwd_two, back_one, back_two)
    )
    column_cot = jnp.concatenate([own_cot, swapped(own_cot, "core")], 0)
    taps = halves(conv_weight, chan_len)[0]
    projected = dot(led_in, w_mix[:, :mix_cols], NN)
    proj_b = projected[lead:, :chan_len]
    proj_c = projected[lead:, chan_len : 2 * chan_len]
    proj_x = projected[lead:, 2 * chan_len : 3 * chan_len]
    extended = projected[:, :chan_len] * projected[:, 2 * chan_len : 3 * chan_len]
    gated = extended[lead:]
    one_back = extended[lead - 1 : lead - 1 + group_len] * fwd_one
    two_back = extended[lead - 2 : lead - 2 + group_len] * fwd_two
    convolved = taps[0] * gated + taps[1] * one_back + taps[2] * two_back
    mixed = (proj_c * convolved).astype(bf16)
    own_mixed, away_mixed = by_core(mixed)
    middle = resid + column_summed(core_summed((own_mixed, away_mixed), w_out, NT))
    grad_hidden = dot(column_cot, w_down, NN)
    middle, grad_hidden = lax.optimization_barrier((middle, grad_hidden))

    scale_two = lax.rsqrt(jnp.mean(middle * middle, axis=-1, keepdims=True) + norm_eps)
    unit_two = middle * scale_two
    normed_two = (unit_two * gains[1]).astype(bf16)
    own_mid = column_own(normed_two)
    column_mid = jnp.concatenate([own_mid, swapped(own_mid, "core")], 0)
    gate_vals = dot(column_mid, w_gate_up, NN)
    gate, up = gate_vals[:, :wide], gate_vals[:, wide:]
    sigma = jax.nn.sigmoid(gate)
    swish = gate * sigma
    hidden = (swish * up).astype(bf16)
    grad_gate = grad_hidden * up * sigma * (1.0 + gate * (1.0 - sigma))
    grad_up = grad_hidden * swish
    grad_pair = jnp.concatenate([grad_gate.astype(bf16), grad_up.astype(bf16)], 1)
    summed = core_summed(jnp.split(grad_pair, 2, 0), w_gate_up, NT)
    summed, grad_pair, hidden = lax.optimization_barrier((summed, grad_pair, hidden))
    grad_normed_two = summed_over(summed, RING, 4)
    grad_ff = weight_grads([[(column_mid, grad_pair)], [(column_cot, hidden)]])
    grad_normed_two, grad_ff = lax.optimization_barrier((grad_normed_two, grad_ff))
    grad_ff = lax.psum_scatter(grad_ff, XY, scatter_dimension=0, tiled=True)

    gain_two_part = jnp.sum(grad_normed_two * unit_two, axis=0)
    grad_unit_two = grad_normed_two * gains[1]
    grad_middle = cotangent.astype(f32) + scale_two * (
        grad_unit_two - unit_two * jnp.mean(grad_unit_two * unit_two, axis=-1, keepdims=True)
    )

    own_back = column_own(grad_middle.astype(bf16))
    ff_out = dot(hidden, w_down, NT).astype(bf16)
    own_back, ff_out = lax.optimization_barrier((own_back, ff_out))
    group_back = by_place(own_back, swapped(own_back, "core"))
    grad_mixed = dot(group_back, w_out, NN)
    grad_conv_out = grad_mixed * proj_c
    following = shifted(grad_conv_out[:2], XY, -1)
    grad_readout = (grad_mixed * convolved).astype(bf16)
    conv_part = jnp.stack(
        [
            jnp.sum(grad_conv_out * gated, axis=0),
            jnp.sum(grad_conv_out * one_back, axis=0),
            jnp.sum(grad_conv_out * two_back, axis=0),
        ]
    )
    ahead = jnp.concatenate([grad_conv_out, following], 0)
    grad_gated = (
        taps[0] * grad_conv_out
        + taps[1] * ahead[1 : group_len + 1] * back_one
        + taps[2] * ahead[2:] * back_two
    )
    grad_proj = jnp.concatenate(
        [
            (grad_gated * proj_x).astype(bf16),
            grad_readout,
            (grad_gated * proj_b).astype(bf16),
        ],
        1,
    )
    grad_mix = weight_grads([[(group_in, grad_proj)], [(group_back, mixed)]])
    grad_mix, grad_proj = lax.optimization_barrier((grad_mix, grad_proj))
    grad_mix = summed_over(grad_mix, XY, 16).astype(bf16)
    own, away = jnp.split(ff_out, 2, 0)
    ff_out = (own.astype(f32) + swapped(away, "core").astype(f32)).astype(bf16)
    ff_blocks = rolled(ff_out.reshape(4, tok_rows, D), -lax.axis_index(RING))
    ff_others = from_others(ff_blocks, RING)
    grad_normed_one = dot(grad_proj, w_in, NT)
    gain_one_part = jnp.sum(grad_normed_one * group_in.astype(f32), axis=0) / gains[0]
    own, away = by_core(grad_normed_one.astype(bf16))
    own = (own.astype(f32) + swapped(away, "core").astype(f32)).astype(bf16)
    grad_normed_one = column_summed(own)

    def both(block):
        pair = block.reshape(2, rows_len, -1)
        return pick(pair, zh), swapped(pick(pair, 1 - zh), "zh")

    conv_full = lax.dynamic_update_slice(
        jnp.zeros((3, D), f32), conv_part, (jnp.int32(0), (2 * mp_index + zh) * chan_len)
    )
    small = jnp.concatenate([gain_one_part[None], gain_two_part[None], conv_full], 0)
    small = paired_sum(small, (("core", 1), ("zl", 1), ("zh", 1)))
    pair = grad_ff.reshape(2, rows_len, -1)
    own_ff, away_ff = pick(pair, zh), pick(pair, 1 - zh)
    away_ff, small, grad_mix = lax.optimization_barrier((away_ff, small, grad_mix))
    other_ff, *ff_others = lax.optimization_barrier((swapped(away_ff, "zh"), *ff_others))
    block_out = middle + ff_blocks[0].astype(f32)
    for other in ff_others:
        block_out = block_out + other.astype(f32)
    block_out = block_out.astype(bf16)
    small = jnp.sum(spread(small, XY, 16), axis=0)
    gain_sum, conv_sum = small[:2], small[2:]

    grad_unit_one = grad_normed_one * gains[0]
    input_grad = grad_middle + scale_one * (
        grad_unit_one - unit_one * jnp.mean(grad_unit_one * unit_one, axis=-1, keepdims=True)
    )

    def spliced(pair, start, width):
        own, other = (block[:, start : start + width] for block in pair)
        return joined(own, other, 1).astype(f32)

    pair = both(grad_mix)
    grad_in = jnp.stack([spliced(pair, i * chan_len, chan_len) for i in range(3)])
    grad_out = spliced(pair, 3 * chan_len, chan_len).T
    pair = (own_ff, other_ff)
    grad_gate_up = jnp.stack([spliced(pair, i * wide, half) for i in range(2)])
    grad_down = spliced(pair, 2 * wide, half).T

    grad_taps = lax.dynamic_slice_in_dim(conv_sum, mp_index * 2 * chan_len, 2 * chan_len, 1)
    gains_set = adam(gains, gains_first, gains_second, gain_sum, 1.0, 0.0)
    conv_set = adam(conv_weight, conv_first, conv_second, grad_taps, 1.0, 0.0)
    in_set = adam(in_weight, in_first, in_second, grad_in, 2.0 * D ** (-0.5), weight_decay)
    out_set = adam(out_weight, out_first, out_second, grad_out, 2.0 * D ** (-0.5), weight_decay)
    gate_set = adam(
        gate_up, gate_up_first, gate_up_second, grad_gate_up, 2.0 * D ** (-0.5), weight_decay
    )
    down_set = adam(
        down_weight, down_first, down_second, grad_down, 2.0 * FF ** (-0.5), weight_decay
    )
    return (block_out, input_grad, *gains_set, *conv_set, *in_set, *out_set, *gate_set, *down_set)


def solution(mesh):
    parts = Mesh(mesh.devices.reshape(4, 4, 2, 2, 2), ("x", "y", "zh", "zl", "core"))
    tokens = P(DP + MP, None)
    taps = P(None, MP)
    wide_in = P(None, DP, MP)
    wide_out = P(MP, DP)
    in_specs = (
        (tokens,) * 2 + (P(),) * 4 + (taps,) * 3 + (wide_in,) * 3 + (wide_out,) * 3
        + (wide_in,) * 3 + (wide_out,) * 3
    )
    out_specs = (
        (tokens,) * 2 + (P(),) * 3 + (taps,) * 3 + (wide_in,) * 3 + (wide_out,) * 3
        + (wide_in,) * 3 + (wide_out,) * 3
    )
    return jax.shard_map(
        on_device, mesh=parts, in_specs=in_specs, out_specs=out_specs, check_vma=False
    )
```
